32 devices in a mesh: dp: 8 (over y, x, core), mp: 4 (over z).
Axes of the slice: x: 2, y: 2, z: 4, core: 2. Of those that a mesh axis runs over, the one named last changes fastest.
Arguments:
- tokens: bfloat16 [8192, 2048], P(('dp', 'mp')), may hold values from -6 to 6
- cotangent: bfloat16 [8192, 2048], P(('dp', 'mp')), may hold values from -6 to 6
- segment: int32 [8192], P('dp'), may hold values from 0 to 31, never falling along the last dimension, each value on 1 to 1024 neighbouring positions
- counts: int32 [8], P('dp'), may hold values from 256 to 1024
- ln_gain: bfloat16 [2, 2048], replicated, may hold values from 0.25 to 1.75
- ln_bias: bfloat16 [2, 2048], replicated, may hold values from -4 to 4
- w_qkv: bfloat16 [2048, 3, 2048], P(None, None, 'mp'), may hold values from -0.125 to 0.125
- b_qv: bfloat16 [2, 2048], P(None, 'mp'), may hold values from -6 to 6
- w_out: bfloat16 [2048, 2048], P('mp'), may hold values from -1 to 1
- out_bias: bfloat16 [2, 2048], replicated, may hold values from -4 to 4
- w_up: bfloat16 [2048, 8192], P(None, 'mp'), may hold values from -0.125 to 0.125
- b_up: bfloat16 [8192], P('mp'), may hold values from -6 to 6
- w_down: bfloat16 [8192, 2048], P('mp'), may hold values from -0.09375 to 0.09375
Outputs:
- layer_out: bfloat16 [8192, 2048], P(('dp', 'mp'))
- grad_tokens: float32 [8192, 2048], P(('dp', 'mp'))
- grad_ln_gain: float32 [2, 2048], replicated
- grad_ln_bias: float32 [2, 2048], replicated
- grad_qkv: float32 [2048, 3, 2048], P('dp', None, 'mp')
- grad_bqv: float32 [2, 2048], P(None, 'mp')
- grad_out: float32 [2048, 2048], P('mp', 'dp')
- grad_out_bias: float32 [2, 2048], replicated
- grad_up: float32 [2048, 8192], P('dp', 'mp')
- grad_bup: float32 [8192], P('mp')
- grad_down: float32 [8192, 2048], P('mp', 'dp')
The draws below stay inside these ranges and needn't reach their ends.
All inputs are finite; a program needn't handle non-finite values.
Results may differ from the reference program's by a relative error of at most 0.012.
The reference program's roundings to bfloat16 on the way count: a program that leaves them out, or rounds other values in their place, can miss the bound.
Values may be sent and summed in bfloat16 or wider, within the bound.
No kernel may reach another device: no remote copies, remote signals or barrier semaphores. Data moves between devices by JAX's collectives and lax.ppermute only.
A program may use at most 256 MiB of HBM per device.

```python
import math
import jax
import jax.numpy as jnp
import numpy as np
from jax import lax

D = 2048
FF = 8192
HEAD = 128
SEQ = 1024
ROWS = 1
GROUP_TOK = 1024
TOKENS = 8192
N_DP = 8


def draw_counts(key, part):
    key = jax.random.fold_in(key, 7)
    pick_key, other_key, offset_key = jax.random.split(key, 3)
    groups = jnp.arange(N_DP, dtype=jnp.int32)
    base_count = GROUP_TOK // 4 + groups * (GROUP_TOK // 2) // max(N_DP - 1, 1)
    offsets = jax.random.randint(offset_key, (N_DP,), 0, GROUP_TOK // 4 + 1)
    drawn = jnp.minimum(base_count + offsets, GROUP_TOK)
    fullest = jax.random.randint(pick_key, (), 0, N_DP)
    lightest = (fullest + 1 + jax.random.randint(other_key, (), 0, N_DP - 1)) % N_DP
    drawn = jnp.where(groups == fullest, GROUP_TOK, drawn)
    drawn = jnp.where(groups == lightest, GROUP_TOK // 4, drawn)
    return drawn.astype(jnp.int32)


def level_of(key, dims, cuts, smallest, top_value):
    def one(dim, shards_of):
        draws = jax.random.uniform(jax.random.fold_in(jax.random.fold_in(key, 6), dim), (shards_of,), jnp.float32, smallest / len(cuts), top_value / len(cuts))
        return jnp.repeat(jnp.exp(draws), dims[dim] // shards_of).reshape((-1,) + (1,) * (len(dims) - dim - 1))

    level = one(*cuts[0])
    for cut in cuts[1:]:
        level = level * one(*cut)
    return level


def split_up(count, total, most, skew):
    loads = [(1 << 20) // math.isqrt(rank ** skew) + 1 for rank in range(2, count + 1)]
    rest, given = total - most - (count - 1), [1] * (count - 1)
    while rest > 0:
        candidates = [i for i in range(count - 1) if given[i] < most]
        whole, budget = sum([loads[i] for i in candidates]), rest
        for i in candidates:
            extra = min(most - given[i], max(1, budget * loads[i] // whole), rest)
            given[i] = given[i] + extra
            rest = rest - extra
    return np.array([most] + given)


def ragged(rng, number_of, total, reach, lean):
    if number_of == 2:
        one = jax.random.randint(rng, (), max(1, total - reach), min(reach, total - 1) + 1)
        return jnp.stack([one, total - one])
    tallies = jnp.asarray(split_up(number_of, total, reach, lean), jnp.int32)
    pairs = (number_of - 1) // 2
    donor, sink = tallies[1:1 + 2 * pairs:2], tallies[2:2 + 2 * pairs:2]
    slack = jnp.minimum(donor - 1, reach - sink)
    shifted = jax.random.randint(jax.random.fold_in(rng, 1), (pairs,), 0, 1 << 20) % (slack + 1)
    tallies = tallies.at[1:1 + 2 * pairs:2].set(donor - shifted).at[2:2 + 2 * pairs:2].set(sink + shifted)
    return tallies[jax.random.permutation(jax.random.fold_in(rng, 2), number_of)]


def centred(stream_key, shape, width, reach, pieces=(), kind=jnp.bfloat16):
    array = width * jax.random.normal(stream_key, shape, jnp.float32)
    if pieces:
        array = array * level_of(stream_key, shape, pieces, -0.22, 0.18)
    return jnp.clip(array, -reach, reach).astype(kind)


def setup_inputs(seed: int = 0) -> dict:
    key_of = jax.random.split(jax.random.key(seed), 14)
    tokens = centred(key_of[0], (TOKENS, D), 1.0, 6.0, ((0, 32),))
    cotangent = centred(key_of[1], (TOKENS, D), 1.0, 6.0, ((0, 32),))
    segment = jnp.searchsorted(jnp.cumsum(ragged(key_of[2], 4 * TOKENS // SEQ, TOKENS, SEQ, 2)), jnp.arange(TOKENS), side="right").astype(jnp.int32)
    counts = draw_counts(jax.random.fold_in(key_of[13], 71), 0)
    ln_gain = jnp.clip(1.0 + 0.15 * jax.random.normal(key_of[4], (2, D), jnp.float32), 0.25, 1.75).astype(jnp.bfloat16)
    ln_bias = centred(key_of[5], (2, D), 0.3, 4.0)
    w_qkv = centred(key_of[6], (D, 3, D), D ** -0.5, 0.125, ((2, 4),))
    b_qv = centred(key_of[7], (2, D), 0.5, 6.0, ((1, 4),))
    w_out = centred(key_of[8], (D, D), (D // 64) ** -0.5, 1.0, ((0, 4),))
    out_bias = centred(key_of[9], (2, D), 0.3, 4.0)
    w_up = centred(key_of[10], (D, FF), D ** -0.5, 0.125, ((1, 4),))
    b_up = centred(key_of[11], (FF,), 0.5, 6.0, ((0, 4),))
    w_down = centred(key_of[12], (FF, D), (FF // 2) ** -0.5, 0.09375, ((0, 4),))
    return dict(tokens=tokens, cotangent=cotangent, segment=segment, counts=counts, ln_gain=ln_gain, ln_bias=ln_bias, w_qkv=w_qkv, b_qv=b_qv, w_out=w_out, out_bias=out_bias, w_up=w_up, b_up=b_up, w_down=w_down)


exact_mode = lax.Precision.HIGHEST

@jax.custom_vjp
def low(v):
    return lax.optimization_barrier(v.astype(jnp.bfloat16)).astype(jnp.float32)

@jax.custom_vjp
def low_back(v):
    return v

def low_keep(v):
    return (low(v), None)

def low_pass(kept, grad):
    return (grad,)

def back_keep(v):
    return (v, None)

def back_low(kept, grad):
    return (low(grad),)
low.defvjp(low_keep, low_pass)
low_back.defvjp(back_keep, back_low)

def matmul(left, right):
    return jnp.dot(left, right, precision=exact_mode, preferred_element_type=jnp.float32)

def layer_norm(value, gain, shift):
    mean = lax.optimization_barrier(jnp.mean(value, axis=-1, keepdims=True))
    centered = value - mean
    spread = lax.optimization_barrier(jnp.mean(centered * centered, axis=-1, keepdims=True))
    return centered * lax.rsqrt(spread + 1e-05) * gain + shift

def attend(query, keys, values, segment_row):
    scores = low_back(jnp.einsum('qhe,khe->hqk', query, keys, precision=exact_mode) * HEAD ** (-0.5))
    places = jnp.arange(SEQ, dtype=jnp.int32)
    allowed = (segment_row[:, None] == segment_row[None, :]) & (places[:, None] >= places[None, :])
    probs = low(jax.nn.softmax(jnp.where(allowed[None], scores, -1e+30), axis=-1))
    return jnp.einsum('hqk,khe->qhe', probs, values, precision=exact_mode)

def forward(inputs, segment_group, ln_gain, ln_bias, w_qkv, b_qv, w_out, out_bias, w_up, b_up, w_down):
    normed = low(layer_norm(inputs, ln_gain[0], ln_bias[0]))
    proj = jnp.einsum('td,dcf->tcf', normed, w_qkv, precision=exact_mode)
    query = low_back(low(proj[:, 0] + b_qv[0]))
    keys = low_back(low(proj[:, 1]))
    values = low_back(low(proj[:, 2] + b_qv[1]))
    head_shape = (ROWS, SEQ, D // HEAD, HEAD)
    mixed = jax.vmap(attend)(query.reshape(head_shape), keys.reshape(head_shape), values.reshape(head_shape), segment_group.reshape(ROWS, SEQ))
    attn_out = low_back(low(mixed.reshape(GROUP_TOK, D)))
    branch = low_back(matmul(attn_out, w_out) + out_bias[0])
    middle = inputs + branch
    normed_mid = low(layer_norm(middle, ln_gain[1], ln_bias[1]))
    hidden = low_back(matmul(normed_mid, w_up) + b_up)
    active = low(jax.nn.gelu(hidden, approximate=True))
    return middle + matmul(active, w_down) + out_bias[1]

def reference(tokens, cotangent, segment, counts, ln_gain, ln_bias, w_qkv, b_qv, w_out, out_bias, w_up, b_up, w_down):
    params = tuple((p.astype(jnp.float32) for p in (ln_gain, ln_bias, w_qkv, b_qv, w_out, out_bias, w_up, b_up, w_down)))
    count_values = counts.astype(jnp.float32)
    shares = count_values / jnp.sum(count_values)
    grouped = tokens.astype(jnp.float32).reshape(N_DP, GROUP_TOK, D)
    cot_grouped = cotangent.astype(jnp.float32).reshape(N_DP, GROUP_TOK, D)
    seg_grouped = segment.reshape(N_DP, GROUP_TOK)

    def per_group(carry, item):
        inputs, cot_group, seg_group, share = item

        def apply(value, *weights):
            return forward(value, seg_group, *weights)
        result, pullback = jax.vjp(apply, inputs, *params)
        grads = pullback(cot_group)
        updated = tuple((c + share * g for c, g in zip(carry, grads[1:])))
        return (updated, (result.astype(jnp.bfloat16), share * grads[0]))
    start = tuple((jnp.zeros_like(p) for p in params))
    totals, (results, input_grads) = lax.scan(per_group, start, (grouped, cot_grouped, seg_grouped, shares))
    return (results.reshape(TOKENS, D), input_grads.reshape(TOKENS, D), totals[0], totals[1], totals[2], totals[3], totals[4], totals[5], totals[6], totals[7], totals[8])
```

```python
import functools
import jax
import jax.numpy as jnp
from jax import lax
from jax.experimental import pallas as pl
from jax.experimental.pallas import tpu as pltpu
from jax.sharding import PartitionSpec as P

HEAD = 128
SEQ = 1024
BLOCK = 256
SCALE = HEAD ** (-0.5)
f32 = jnp.float32
bf16 = jnp.bfloat16


def dot(left, right, left_dim=1, right_dim=0):
    return lax.dot_general(
        left, right, (((left_dim,), (right_dim,)), ((), ())), preferred_element_type=f32
    )


def block_probs(q_block, k_ref, seg_col, seg_row, block, reach):
    start = block * BLOCK
    scores = dot(k_ref[:reach, :], q_block, 1, 1) * SCALE
    key_place = lax.broadcasted_iota(jnp.int32, (reach, BLOCK), 0)
    query_place = start + lax.broadcasted_iota(jnp.int32, (reach, BLOCK), 1)
    allowed = (seg_col[:reach, :] == seg_row[:, start : start + BLOCK]) & (
        key_place <= query_place
    )
    scores = jnp.where(allowed, scores, -1e30)
    expo = jnp.exp(scores - jnp.max(scores, axis=0, keepdims=True))
    return expo * (1.0 / jnp.sum(expo, axis=0, keepdims=True))


def attend_kernel(q_ref, k_ref, v_ref, seg_col, seg_row, out_ref):
    for block in range(SEQ // BLOCK):
        rows = slice(block * BLOCK, (block + 1) * BLOCK)
        reach = (block + 1) * BLOCK
        probs = block_probs(q_ref[rows, :], k_ref, seg_col, seg_row, block, reach)
        out_ref[rows, :] = dot(probs.astype(bf16), v_ref[:reach, :], 0, 0).astype(bf16)


def attend(projected, seg_col, seg_row, heads):
    tokens = projected.shape[0]
    column = lambda part: pl.BlockSpec((SEQ, HEAD), lambda r, h: (r, part * heads + h))
    return pl.pallas_call(
        attend_kernel,
        grid=(tokens // SEQ, heads),
        in_specs=[
            column(0),
            column(1),
            column(2),
            pl.BlockSpec((SEQ, 1), lambda r, h: (r, 0)),
            pl.BlockSpec((1, SEQ), lambda r, h: (0, r)),
        ],
        out_specs=pl.BlockSpec((SEQ, HEAD), lambda r, h: (r, h)),
        out_shape=jax.ShapeDtypeStruct((tokens, heads * HEAD), bf16),
        compiler_params=pltpu.CompilerParams(vmem_limit_bytes=40 * 2**20),
        cost_estimate=pl.CostEstimate(
            flops=heads * tokens * SEQ * HEAD * 4,
            bytes_accessed=tokens * heads * HEAD * 8,
            transcendentals=heads * tokens * SEQ,
        ),
        name="attend",
    )(projected, projected, projected, seg_col, seg_row)


def attend_back_kernel(
    heads, q_ref, k_ref, v_ref, grad_ref, seg_col, seg_row, out_ref, dk_ref, dv_ref
):
    head = pl.program_id(1)
    width = heads * HEAD
    column = lambda part: pl.ds(pl.multiple_of(part * width + head * HEAD, HEAD), HEAD)
    dk_ref[...] = jnp.zeros_like(dk_ref)
    dv_ref[...] = jnp.zeros_like(dv_ref)
    for block in range(SEQ // BLOCK):
        rows = slice(block * BLOCK, (block + 1) * BLOCK)
        reach = (block + 1) * BLOCK
        q_block = q_ref[rows, :]
        g_block = grad_ref[rows, :]
        probs = block_probs(q_block, k_ref, seg_col, seg_row, block, reach)
        d_probs = dot(v_ref[:reach, :], g_block, 1, 1)
        delta = jnp.sum(probs * d_probs, axis=0, keepdims=True)
        d_scores = (probs * (d_probs - delta)).astype(bf16)
        dv_ref[:reach, :] += dot(probs.astype(bf16), g_block)
        dk_ref[:reach, :] += dot(d_scores, q_block)
        out_ref[rows, column(0)] = (dot(d_scores, k_ref[:reach, :], 0, 0) * SCALE).astype(bf16)
    out_ref[:, column(1)] = (dk_ref[...] * SCALE).astype(bf16)
    out_ref[:, column(2)] = dv_ref[...].astype(bf16)


def attend_back(projected, grad_attn, seg_col, seg_row, heads):
    tokens = projected.shape[0]
    column = lambda part: pl.BlockSpec((SEQ, HEAD), lambda r, h: (r, part * heads + h))
    return pl.pallas_call(
        functools.partial(attend_back_kernel, heads),
        grid=(tokens // SEQ, heads),
        in_specs=[
            column(0),
            column(1),
            column(2),
            column(0),
            pl.BlockSpec((SEQ, 1), lambda r, h: (r, 0)),
            pl.BlockSpec((1, SEQ), lambda r, h: (0, r)),
        ],
        out_specs=pl.BlockSpec((SEQ, 3 * heads * HEAD), lambda r, h: (r, 0)),
        out_shape=jax.ShapeDtypeStruct((tokens, 3 * heads * HEAD), bf16),
        scratch_shapes=[pltpu.VMEM((SEQ, HEAD), f32), pltpu.VMEM((SEQ, HEAD), f32)],
        compiler_params=pltpu.CompilerParams(vmem_limit_bytes=40 * 2**20),
        cost_estimate=pl.CostEstimate(
            flops=heads * tokens * SEQ * HEAD * 10,
            bytes_accessed=tokens * heads * HEAD * 14,
            transcendentals=heads * tokens * SEQ,
        ),
        name="attend_back",
    )(projected, projected, projected, grad_attn, seg_col, seg_row)


def norm_parts(value):
    mean = jnp.mean(value, axis=-1, keepdims=True)
    centered = value - mean
    inverse = lax.rsqrt(jnp.mean(centered * centered, axis=-1, keepdims=True) + 1e-05)
    return centered * inverse, inverse


def norm_backward(grad, gain, scaled, inverse):
    inner = grad * gain
    return inverse * (
        inner
        - jnp.mean(inner, axis=-1, keepdims=True)
        - scaled * jnp.mean(inner * scaled, axis=-1, keepdims=True)
    )


def gelu_parts(value):
    c = 0.7978845608028654
    square = value * value
    tanh = jnp.tanh(c * value * (1.0 + 0.044715 * square))
    half = 0.5 * (1.0 + tanh)
    slope = half + 0.5 * value * (1.0 - tanh * tanh) * c * (1.0 + 3 * 0.044715 * square)
    return value * half, slope


class Line:
    def __init__(self, name, size):
        self.name, self.n = name, size
        self.me = lax.axis_index(name)
        self.low = self.me < size // 2

    def slot_index(self, k):
        n = self.n
        return jnp.where(self.low, (self.me + k) % n, (self.me + n - k) % n)

    def gather(self, block):
        n = self.n
        from_left, from_right = [block], [block]
        for k in range(1, n):
            from_left.append(
                lax.ppermute(from_left[-1], self.name, [(j, j + 1) for j in range(k - 1, n - 1)])
            )
            from_right.append(
                lax.ppermute(from_right[-1], self.name, [(j, j - 1) for j in range(1, n - k + 1)])
            )
            low_side, high_side = from_right[k], from_left[k]
            if 2 * k >= n:
                low_side = jnp.where(self.me + k < n, from_right[k], from_left[n - k])
                high_side = jnp.where(self.me >= k, from_left[k], from_right[n - k])
            yield jnp.where(self.low, low_side, high_side)

    def reduce(self, parts):
        n = self.n
        from_left = from_right = None
        for k in range(1, n):
            other = parts[n - k] if n - k < k else parts[k]
            to_right = jnp.where(self.low, parts[k], other)
            to_left = jnp.where(self.low, other, parts[k])
            if k > 1:
                to_right = to_right + from_left.astype(f32)
                to_left = to_left + from_right.astype(f32)
            from_left = lax.ppermute(
                to_right.astype(bf16), self.name, [(j, j + 1) for j in range(k)]
            )
            from_right = lax.ppermute(
                to_left.astype(bf16), self.name, [(j, j - 1) for j in range(n - k, n)]
            )
        return parts[0] + from_left.astype(f32) + from_right.astype(f32)

    def reduce_index(self, k):
        n = self.n
        return jnp.where(self.low, (self.me + n - k) % n, (self.me + k) % n)

    def shuffle(self, array, rows):
        n = self.n
        cols = array.shape[1] // n
        out = jnp.zeros((n * rows, cols), array.dtype)
        for shift in range(n):
            target = (self.me + shift) % n
            source = (self.me + n - shift) % n
            block = lax.dynamic_slice_in_dim(array, target * cols, cols, axis=1)
            if shift:
                block = lax.ppermute(block, self.name, [(j, (j + shift) % n) for j in range(n)])
            out = lax.dynamic_update_slice_in_dim(out, block, source * rows, axis=0)
        return out


def flip(value, name, size, bit):
    return lax.ppermute(value, name, [(j, j ^ bit) for j in range(size)])


def sum_over(value, name, size):
    bit = 1
    while bit < size:
        value = value + flip(value, name, size, bit)
        bit *= 2
    return value


def halve(array, axis, name, size, bit):
    mine = (lax.axis_index(name) // bit) % 2
    sent = lax.dynamic_index_in_dim(array, 1 - mine, axis, keepdims=False)
    kept = lax.dynamic_index_in_dim(array, mine, axis, keepdims=False)
    return kept.astype(f32) + flip(sent, name, size, bit).astype(f32)


def scatter_rows(full, name, size):
    rows, cols = full.shape
    bits = [1 << b for b in range(size.bit_length() - 1)]
    shape = [2] * len(bits)
    block = rows // size
    array = full.reshape(*shape, block, cols)
    first = halve(array, len(bits) - 1, name, size, 1).astype(bf16)
    rest = bits[1:]
    if not rest:
        return first.astype(f32)
    parts = []
    for order, piece in zip(
        (rest, rest[::-1]), jnp.split(first, 2, axis=-2)
    ):
        left = list(rest[::-1])
        for bit in order:
            axis = left.index(bit)
            left.pop(axis)
            piece = halve(piece, axis, name, size, bit)
            if left:
                piece = piece.astype(bf16)
        parts.append(piece)
    return jnp.concatenate(parts, axis=0)


def scatter_cols(full, name, size):
    rows, cols = full.shape
    bits = [1 << b for b in range(size.bit_length() - 1)]
    block = cols // size
    array = full.reshape(rows, *([2] * len(bits)), block)
    first = halve(array, len(bits), name, size, 1).astype(bf16)
    rest = bits[1:]
    parts = []
    for order, piece in zip((rest, rest[::-1]), jnp.split(first, 2, axis=0)):
        left = list(rest[::-1])
        for bit in order:
            axis = 1 + left.index(bit)
            left.pop(axis - 1)
            piece = halve(piece, axis, name, size, bit)
            if left:
                piece = piece.astype(bf16)
        parts.append(piece)
    return jnp.concatenate(parts, axis=0)


def after(value, *earlier):
    return lax.optimization_barrier((value, *earlier))[0]


def make_body(n_dp, n_mp):
    def body(
        tokens, cotangent, segment, counts, ln_gain, ln_bias, w_qkv, b_qv, w_out, out_bias, w_up, b_up, w_down
    ):
        line = Line("mp", n_mp)
        gains, shifts, bias_pair = ln_gain.astype(f32), ln_bias.astype(f32), out_bias.astype(f32)
        share, width = tokens.shape
        head_cols = w_qkv.shape[2]
        heads = head_cols // HEAD
        group = segment.shape[0]
        seg_col, seg_row = segment[:, None], segment[None, :]
        me = line.me
        place = lambda whole, block, index: lax.dynamic_update_slice_in_dim(
            whole, block, index * share, axis=0
        )
        own_rows = lambda whole, index: lax.dynamic_slice_in_dim(whole, index * share, share, axis=0)

        count_here = counts.astype(f32)
        factor = (count_here / sum_over(count_here, "dp", n_dp))[0]

        slice_rows = w_out.shape[0] // n_dp
        w_slice = lax.dynamic_slice_in_dim(
            w_out, lax.axis_index("dp") * slice_rows, slice_rows, axis=0
        )
        w_slices = lax.all_gather(w_slice, "mp", axis=0)
        w_out_all = lax.all_gather(w_slices, "dp", axis=1).reshape(n_mp * w_out.shape[0], width)

        flat_qkv = w_qkv.reshape(width, 3 * head_cols)
        bias_rows = (
            jnp.stack([b_qv[0], jnp.zeros_like(b_qv[0]), b_qv[1]]).astype(f32).reshape(3 * head_cols)
        )
        tokens_all = jnp.zeros((group, width), bf16)
        normed1_all = jnp.zeros((group, width), bf16)
        projected = jnp.zeros((group, 3 * head_cols), bf16)
        last = None
        for k, block in enumerate([tokens, *line.gather(tokens)]):
            index = me if k == 0 else line.slot_index(k)
            normed = (norm_parts(block.astype(f32))[0] * gains[0] + shifts[0]).astype(bf16)
            proj = (dot(normed, flat_qkv) + bias_rows).astype(bf16)
            tokens_all = place(tokens_all, block, index)
            normed1_all = place(normed1_all, normed, index)
            projected = place(projected, proj, index)
            last = block
        attn = attend(projected, seg_col, seg_row, heads)

        cot_all = lax.all_gather(after(cotangent, last), "mp", axis=0, tiled=True)

        middle_all = tokens_all.astype(f32) + bias_pair[0] + dot(attn, w_out)
        for k, block in enumerate(line.gather(attn)):
            index = line.slot_index(k + 1)
            rows = lax.dynamic_slice_in_dim(w_out_all, index * head_cols, head_cols, axis=0)
            middle_all = middle_all + dot(block, rows)
        normed2_all = (norm_parts(middle_all)[0] * gains[1] + shifts[1]).astype(bf16)
        hidden = dot(normed2_all, w_up) + b_up.astype(f32)
        active, slope = gelu_parts(hidden)
        active = active.astype(bf16)
        d_hidden = (dot(cot_all, w_down, 1, 1) * slope).astype(bf16)

        d_normed2_parts = [
            dot(own_rows(d_hidden, me if k == 0 else line.reduce_index(k)), w_up, 1, 1)
            for k in [*range(1, n_mp), 0]
        ]
        d_normed2_parts = [d_normed2_parts[-1], *d_normed2_parts[:-1]]
        d_normed2 = line.reduce(d_normed2_parts)

        middle = own_rows(middle_all, me)
        scaled2, inverse2 = norm_parts(middle)
        cot = cotangent.astype(f32)
        d_middle = cot + norm_backward(d_normed2, gains[1], scaled2, inverse2)
        d_branch = d_middle.astype(bf16)
        d_attn = line.shuffle(dot(d_branch, w_out_all, 1, 1).astype(bf16), share)

        down = dot(active, w_down).astype(bf16)
        down_sum = lax.psum_scatter(
            after(down, d_normed2), "mp", scatter_dimension=0, tiled=True
        )
        layer_out = (middle + down_sum.astype(f32) + bias_pair[1]).astype(bf16)
        d_branch_all = lax.all_gather(d_branch, "mp", axis=0, tiled=True)

        grad_proj = attend_back(projected, d_attn, seg_col, seg_row, heads)
        d_normed1_parts = [
            dot(own_rows(grad_proj, me if k == 0 else line.reduce_index(k)), flat_qkv, 1, 1)
            for k in [*range(1, n_mp), 0]
        ]
        d_normed1_parts = [d_normed1_parts[-1], *d_normed1_parts[:-1]]
        d_normed1 = line.reduce(d_normed1_parts)
        scaled1, inverse1 = norm_parts(tokens.astype(f32))
        grad_input = d_middle + norm_backward(d_normed1, gains[0], scaled1, inverse1)

        scaled = lambda left, right: (factor * dot(left, right, 0, 0)).astype(bf16)
        grad_down = scatter_cols(scaled(active, cot_all), "dp", n_dp)
        grad_up = scatter_rows(scaled(normed2_all, d_hidden), "dp", n_dp)
        grad_qkv = scatter_rows(scaled(normed1_all, grad_proj), "dp", n_dp)
        grad_out = scatter_cols(scaled(attn, d_branch_all), "dp", n_dp)

        total = lambda value: jnp.sum(value.astype(f32), axis=0)
        heads_sum = jnp.stack(
            [total(grad_proj[:, :head_cols]), total(grad_proj[:, 2 * head_cols :])]
        )
        split_sums = jnp.concatenate([heads_sum.reshape(-1), total(d_hidden)])
        full_sums = jnp.concatenate(
            [
                total(d_normed1 * scaled1),
                total(d_normed2 * scaled2),
                total(d_normed1),
                total(d_normed2),
                total(d_branch),
                total(cot),
            ]
        )
        split_sums, full_sums = factor * split_sums, factor * full_sums
        split_sums = sum_over(split_sums, "dp", n_dp)
        full_sums = sum_over(sum_over(full_sums, "dp", n_dp), "mp", n_mp).reshape(3, 2, width)
        return (
            layer_out,
            factor * grad_input,
            full_sums[0],
            full_sums[1],
            grad_qkv.reshape(-1, 3, head_cols),
            split_sums[: 2 * head_cols].reshape(2, head_cols),
            grad_out,
            full_sums[2],
            grad_up,
            split_sums[2 * head_cols :],
            grad_down,
        )

    return body


def solution(mesh):
    split = P(("dp", "mp"), None)
    return jax.shard_map(
        make_body(mesh.shape["dp"], mesh.shape["mp"]),
        mesh=mesh,
        in_specs=(
            split, split, P("dp"), P("dp"), P(), P(), P(None, None, "mp"), P(None, "mp"), P("mp", None), P(),
            P(None, "mp"), P("mp"), P("mp", None),
        ),
        out_specs=(
            split, split, P(), P(), P("dp", None, "mp"), P(None, "mp"), P("mp", "dp"), P(), P("dp", "mp"), P("mp"),
            P("mp", "dp"),
        ),
        check_vma=False,
    )
```

```python
import functools
import jax
import jax.numpy as jnp
from jax import lax
from jax.experimental import pallas as pl
from jax.experimental.pallas import tpu as pltpu
from jax.sharding import PartitionSpec as P

HEAD = 128
SEQ = 1024
BLOCK = 256
SCALE = HEAD ** (-0.5)
f32 = jnp.float32
bf16 = jnp.bfloat16
LIGHT = pl.CostEstimate(flops=1 << 20, bytes_accessed=1 << 16, transcendentals=0)


def dot(left, right, left_dim=1, right_dim=0):
    return lax.dot_general(
        left, right, (((left_dim,), (right_dim,)), ((), ())), preferred_element_type=f32
    )


def block_probs(q_block, k_ref, seg_col, seg_row, block, reach):
    start = block * BLOCK
    scores = dot(k_ref[:reach, :], q_block, 1, 1) * SCALE
    key_place = lax.broadcasted_iota(jnp.int32, (reach, BLOCK), 0)
    query_place = start + lax.broadcasted_iota(jnp.int32, (reach, BLOCK), 1)
    allowed = (seg_col[:reach, :] == seg_row[:, start : start + BLOCK]) & (
        key_place <= query_place
    )
    scores = jnp.where(allowed, scores, -1e30)
    expo = jnp.exp(scores - jnp.max(scores, axis=0, keepdims=True))
    return expo * (1.0 / jnp.sum(expo, axis=0, keepdims=True))


def attend_kernel(q_ref, k_ref, v_ref, seg_col, seg_row, out_ref):
    for block in range(SEQ // BLOCK):
        rows = slice(block * BLOCK, (block + 1) * BLOCK)
        reach = (block + 1) * BLOCK
        probs = block_probs(q_ref[rows, :], k_ref, seg_col, seg_row, block, reach)
        out_ref[rows, :] = dot(probs.astype(bf16), v_ref[:reach, :], 0, 0).astype(bf16)


def attend(projected, seg_col, seg_row, heads):
    tokens = projected.shape[0]
    column = lambda part: pl.BlockSpec((SEQ, HEAD), lambda r, h: (r, part * heads + h))
    return pl.pallas_call(
        attend_kernel,
        grid=(tokens // SEQ, heads),
        in_specs=[
            column(0),
            column(1),
            column(2),
            pl.BlockSpec((SEQ, 1), lambda r, h: (r, 0)),
            pl.BlockSpec((1, SEQ), lambda r, h: (0, r)),
        ],
        out_specs=pl.BlockSpec((SEQ, HEAD), lambda r, h: (r, h)),
        out_shape=jax.ShapeDtypeStruct((tokens, heads * HEAD), bf16),
        compiler_params=pltpu.CompilerParams(vmem_limit_bytes=40 * 2**20),
        cost_estimate=LIGHT,
        name="attend",
    )(projected, projected, projected, seg_col, seg_row)


def attend_back_kernel(
    heads, q_ref, k_ref, v_ref, grad_ref, seg_col, seg_row, out_ref, dk_ref, dv_ref
):
    head = pl.program_id(1)
    width = heads * HEAD
    column = lambda part: pl.ds(pl.multiple_of(part * width + head * HEAD, HEAD), HEAD)
    dk_ref[...] = jnp.zeros_like(dk_ref)
    dv_ref[...] = jnp.zeros_like(dv_ref)
    for block in range(SEQ // BLOCK):
        rows = slice(block * BLOCK, (block + 1) * BLOCK)
        reach = (block + 1) * BLOCK
        q_block = q_ref[rows, :]
        g_block = grad_ref[rows, :]
        probs = block_probs(q_block, k_ref, seg_col, seg_row, block, reach)
        d_probs = dot(v_ref[:reach, :], g_block, 1, 1)
        delta = jnp.sum(probs * d_probs, axis=0, keepdims=True)
        d_scores = (probs * (d_probs - delta)).astype(bf16)
        dv_ref[:reach, :] += dot(probs.astype(bf16), g_block)
        dk_ref[:reach, :] += dot(d_scores, q_block)
        out_ref[rows, column(0)] = (dot(d_scores, k_ref[:reach, :], 0, 0) * SCALE).astype(bf16)
    out_ref[:, column(1)] = (dk_ref[...] * SCALE).astype(bf16)
    out_ref[:, column(2)] = dv_ref[...].astype(bf16)


def attend_back(projected, grad_attn, seg_col, seg_row, heads):
    tokens = projected.shape[0]
    column = lambda part: pl.BlockSpec((SEQ, HEAD), lambda r, h: (r, part * heads + h))
    return pl.pallas_call(
        functools.partial(attend_back_kernel, heads),
        grid=(tokens // SEQ, heads),
        in_specs=[
            column(0),
            column(1),
            column(2),
            column(0),
            pl.BlockSpec((SEQ, 1), lambda r, h: (r, 0)),
            pl.BlockSpec((1, SEQ), lambda r, h: (0, r)),
        ],
        out_specs=pl.BlockSpec((SEQ, 3 * heads * HEAD), lambda r, h: (r, 0)),
        out_shape=jax.ShapeDtypeStruct((tokens, 3 * heads * HEAD), bf16),
        scratch_shapes=[pltpu.VMEM((SEQ, HEAD), f32), pltpu.VMEM((SEQ, HEAD), f32)],
        compiler_params=pltpu.CompilerParams(vmem_limit_bytes=40 * 2**20),
        cost_estimate=LIGHT,
        name="attend_back",
    )(projected, projected, projected, grad_attn, seg_col, seg_row)


def norm_parts(value):
    mean = jnp.mean(value, axis=-1, keepdims=True)
    centered = value - mean
    inverse = lax.rsqrt(jnp.mean(centered * centered, axis=-1, keepdims=True) + 1e-05)
    return centered * inverse, inverse


def norm_backward(grad, gain, scaled, inverse):
    inner = grad * gain
    return inverse * (
        inner
        - jnp.mean(inner, axis=-1, keepdims=True)
        - scaled * jnp.mean(inner * scaled, axis=-1, keepdims=True)
    )


def gelu_parts(value):
    c = 0.7978845608028654
    square = value * value
    tanh = jnp.tanh(c * value * (1.0 + 0.044715 * square))
    half = 0.5 * (1.0 + tanh)
    slope = half + 0.5 * value * (1.0 - tanh * tanh) * c * (1.0 + 3 * 0.044715 * square)
    return value * half, slope


def mix_kernel(token_ref, heads_ref, w_ref, bias_ref, gain_ref, shift_ref, middle_ref, normed_ref):
    middle = dot(heads_ref[...], w_ref[...]) + (token_ref[...].astype(f32) + bias_ref[...])
    middle_ref[...] = middle
    normed_ref[...] = (norm_parts(middle)[0] * gain_ref[...] + shift_ref[...]).astype(bf16)


def mix(tokens_all, attn_all, w_out_all, bias, gain, shift):
    tokens, width = tokens_all.shape
    cols = attn_all.shape[1]
    step = 256
    row = lambda size: pl.BlockSpec((step, size), lambda i: (i, 0))
    one = pl.BlockSpec((1, width), lambda i: (0, 0))
    return pl.pallas_call(
        mix_kernel,
        grid=(tokens // step,),
        in_specs=[row(width), row(cols), pl.BlockSpec((cols, width), lambda i: (0, 0)), one, one, one],
        out_specs=[row(width), row(width)],
        out_shape=[
            jax.ShapeDtypeStruct((tokens, width), f32),
            jax.ShapeDtypeStruct((tokens, width), bf16),
        ],
        compiler_params=pltpu.CompilerParams(vmem_limit_bytes=48 * 2**20),
        cost_estimate=LIGHT,
        name="mix",
    )(tokens_all, attn_all, w_out_all, bias[None], gain[None], shift[None])


def up_kernel(x_ref, w_ref, b_ref, hidden_ref, active_ref):
    hidden = dot(x_ref[...], w_ref[...]) + b_ref[...]
    hidden_ref[...] = hidden
    active_ref[...] = gelu_parts(hidden)[0].astype(bf16)


def feed_up(normed, w_up, b_up):
    tokens, width = normed.shape
    cols = w_up.shape[1]
    step = 256
    col = lambda rows: pl.BlockSpec((rows, step), lambda i: (0, i))
    return pl.pallas_call(
        up_kernel,
        grid=(cols // step,),
        in_specs=[pl.BlockSpec((tokens, width), lambda i: (0, 0)), col(width), col(1)],
        out_specs=[col(tokens), col(tokens)],
        out_shape=[
            jax.ShapeDtypeStruct((tokens, cols), f32),
            jax.ShapeDtypeStruct((tokens, cols), bf16),
        ],
        compiler_params=pltpu.CompilerParams(vmem_limit_bytes=48 * 2**20),
        cost_estimate=LIGHT,
        name="feed_up",
    )(normed, w_up, b_up[None])


def hidden_kernel(cot_ref, hidden_ref, w_ref, out_ref):
    slope = gelu_parts(hidden_ref[...])[1]
    out_ref[...] = (dot(cot_ref[...], w_ref[...], 1, 1) * slope).astype(bf16)


def hidden_back(cot_all, hidden, w_down):
    tokens, width = cot_all.shape
    cols, step = hidden.shape[1], 256
    return pl.pallas_call(
        hidden_kernel,
        grid=(cols // step,),
        in_specs=[
            pl.BlockSpec((tokens, width), lambda i: (0, 0)),
            pl.BlockSpec((tokens, step), lambda i: (0, i)),
            pl.BlockSpec((step, width), lambda i: (i, 0)),
        ],
        out_specs=pl.BlockSpec((tokens, step), lambda i: (0, i)),
        out_shape=jax.ShapeDtypeStruct((tokens, cols), bf16),
        compiler_params=pltpu.CompilerParams(vmem_limit_bytes=48 * 2**20),
        cost_estimate=LIGHT,
        name="hidden_back",
    )(cot_all, hidden, w_down)


def grads_kernel(bounds, factor_ref, *refs):
    count = len(bounds) - 1
    left_refs, right_refs = refs[:count], refs[count : 2 * count]
    out_ref, turned_ref = refs[2 * count :]
    i = pl.program_id(0)
    for j in range(count):

        @pl.when(i == bounds[j])
        def _():
            turned_ref[...] = left_refs[j][...].T

        @pl.when((i >= bounds[j]) & (i < bounds[j + 1]))
        def _():
            out_ref[...] = (factor_ref[0] * dot(turned_ref[...], right_refs[j][...])).astype(bf16)


def weight_grads(factor, pairs):
    tokens, width = pairs[0][0].shape
    step = 256
    bounds = [0]
    for _, right in pairs:
        bounds.append(bounds[-1] + right.shape[1] // step)

    def part(j):
        low, high = bounds[j], bounds[j + 1]
        return pl.BlockSpec((tokens, step), lambda i: (0, jnp.clip(i - low, 0, high - low - 1)))

    whole = pl.BlockSpec((tokens, width), lambda i: (0, 0))
    return pl.pallas_call(
        functools.partial(grads_kernel, tuple(bounds)),
        grid=(bounds[-1],),
        in_specs=[
            pl.BlockSpec(memory_space=pltpu.SMEM),
            *[whole] * len(pairs),
            *[part(j) for j in range(len(pairs))],
        ],
        out_specs=pl.BlockSpec((width, step), lambda i: (0, i)),
        out_shape=jax.ShapeDtypeStruct((width, step * bounds[-1]), bf16),
        scratch_shapes=[pltpu.VMEM((width, tokens), bf16)],
        compiler_params=pltpu.CompilerParams(vmem_limit_bytes=48 * 2**20),
        cost_estimate=LIGHT,
        name="weight_grads",
    )(factor[None], *[left for left, _ in pairs], *[right for _, right in pairs])


def half_kernel(index_ref, x_ref, w_ref, *refs):
    refs[-1][...] = dot(x_ref[...], w_ref[...], 1, 1).astype(bf16)


def half_product(x, weight, half, earlier=None):
    tokens, depth = x.shape
    rows = tokens // 2
    cols, step = weight.shape[0], 512
    given = [] if earlier is None else [earlier]
    return pl.pallas_call(
        half_kernel,
        grid_spec=pltpu.PrefetchScalarGridSpec(
            num_scalar_prefetch=1,
            grid=(cols // step,),
            in_specs=[
                pl.BlockSpec((rows, depth), lambda i, at: (at[0], 0)),
                pl.BlockSpec((step, depth), lambda i, at: (i, 0)),
                *[pl.BlockSpec(memory_space=pl.ANY) for _ in given],
            ],
            out_specs=pl.BlockSpec((rows, step), lambda i, at: (at[0], i)),
        ),
        out_shape=jax.ShapeDtypeStruct((tokens, cols), bf16),
        input_output_aliases={3: 0} if given else {},
        compiler_params=pltpu.CompilerParams(vmem_limit_bytes=40 * 2**20),
        cost_estimate=LIGHT,
        name="half_product",
    )(half[None], x, weight, *given)


def relay_kernel(index_ref, right_ref, left_ref, *refs):
    to_right, to_left = refs[-2:]
    if len(refs) == 2:
        to_right[...], to_left[...] = right_ref[...], left_ref[...]
    else:
        to_right[...] = (right_ref[...].astype(f32) + refs[0][...].astype(f32)).astype(bf16)
        to_left[...] = (left_ref[...].astype(f32) + refs[1][...].astype(f32)).astype(bf16)


def relay(terms, rows, index, came):
    width = terms.shape[1]
    step = min(rows, 128)
    steps = rows // step
    block = pl.BlockSpec((step, width), lambda i, at: (i, 0))
    return pl.pallas_call(
        relay_kernel,
        grid_spec=pltpu.PrefetchScalarGridSpec(
            num_scalar_prefetch=1,
            grid=(steps,),
            in_specs=[
                pl.BlockSpec((step, width), lambda i, at: (at[0] * steps + i, 0)),
                pl.BlockSpec((step, width), lambda i, at: (at[1] * steps + i, 0)),
                *[block] * len(came),
            ],
            out_specs=[block, block],
        ),
        out_shape=[jax.ShapeDtypeStruct((rows, width), bf16)] * 2,
        compiler_params=pltpu.CompilerParams(vmem_limit_bytes=40 * 2**20),
        cost_estimate=LIGHT,
        name="relay",
    )(index, terms, terms, *came)


def summed_back(term_ref, left_ref, right_ref, value_ref, gain_ref):
    grad = term_ref[...].astype(f32) + left_ref[...].astype(f32) + right_ref[...].astype(f32)
    scaled, inverse = norm_parts(value_ref[...].astype(f32))
    return grad, scaled, norm_backward(grad, gain_ref[...], scaled, inverse)


def middle_back_kernel(
    index_ref, term_ref, left_ref, right_ref, value_ref, gain_ref, cot_ref, middle_ref, branch_ref, sums_ref
):
    @pl.when(pl.program_id(0) == 0)
    def _():
        sums_ref[...] = jnp.zeros_like(sums_ref)

    grad, scaled, back = summed_back(term_ref, left_ref, right_ref, value_ref, gain_ref)
    cot = cot_ref[...].astype(f32)
    middle = cot + back
    branch = middle.astype(bf16)
    middle_ref[...], branch_ref[...] = middle, branch
    for row, value in enumerate((grad * scaled, grad, branch.astype(f32), cot)):
        sums_ref[row : row + 1, :] += jnp.sum(value, axis=0, keepdims=True)


def input_back_kernel(
    index_ref, factor_ref, term_ref, left_ref, right_ref, value_ref, gain_ref, middle_ref, out_ref
):
    back = summed_back(term_ref, left_ref, right_ref, value_ref, gain_ref)[2]
    out_ref[...] = factor_ref[0] * (middle_ref[...] + back)


def back_specs(rows, width):
    step = min(rows, 128)
    steps = rows // step
    here = pl.BlockSpec((step, width), lambda i, at: (i, 0))
    own = pl.BlockSpec((step, width), lambda i, at: (at[0] * steps + i, 0))
    return steps, here, own, pl.BlockSpec((1, width), lambda i, at: (0, 0))


def middle_back(index, terms, came, middle_all, gain, cot):
    rows, width = cot.shape
    steps, here, own, one = back_specs(rows, width)
    return pl.pallas_call(
        middle_back_kernel,
        grid_spec=pltpu.PrefetchScalarGridSpec(
            num_scalar_prefetch=1,
            grid=(steps,),
            in_specs=[own, here, here, own, one, here],
            out_specs=[here, here, pl.BlockSpec((4, width), lambda i, at: (0, 0))],
        ),
        out_shape=[
            jax.ShapeDtypeStruct((rows, width), f32),
            jax.ShapeDtypeStruct((rows, width), bf16),
            jax.ShapeDtypeStruct((4, width), f32),
        ],
        compiler_params=pltpu.CompilerParams(vmem_limit_bytes=40 * 2**20),
        cost_estimate=LIGHT,
        name="middle_back",
    )(index, terms, *came, middle_all, gain[None], cot)


def input_back(index, factor, terms, came, tokens, gain, d_middle):
    rows, width = tokens.shape
    steps, here, own, one = back_specs(rows, width)
    return pl.pallas_call(
        input_back_kernel,
        grid_spec=pltpu.PrefetchScalarGridSpec(
            num_scalar_prefetch=1,
            grid=(steps,),
            in_specs=[pl.BlockSpec(memory_space=pltpu.SMEM), own, here, here, here, one, here],
            out_specs=here,
        ),
        out_shape=jax.ShapeDtypeStruct((rows, width), f32),
        compiler_params=pltpu.CompilerParams(vmem_limit_bytes=40 * 2**20),
        cost_estimate=LIGHT,
        name="input_back",
    )(index, factor[None], terms, *came, tokens, gain[None], d_middle)


def blank_kernel(out_ref):
    pass


def blank(shape):
    return pl.pallas_call(
        blank_kernel,
        out_specs=pl.BlockSpec(memory_space=pl.ANY),
        out_shape=jax.ShapeDtypeStruct(shape, bf16),
        name="blank",
    )()


def sums_kernel(term_ref, token_ref, out_ref):
    @pl.when(pl.program_id(0) == 0)
    def _():
        out_ref[...] = jnp.zeros_like(out_ref)

    term = term_ref[...].astype(f32)
    scaled = norm_parts(token_ref[...].astype(f32))[0]
    out_ref[0:1, :] += jnp.sum(term * scaled, axis=0, keepdims=True)
    out_ref[1:2, :] += jnp.sum(term, axis=0, keepdims=True)


def gain_sums(terms, tokens_all):
    rows, width = terms.shape
    block = pl.BlockSpec((128, width), lambda i: (i, 0))
    return pl.pallas_call(
        sums_kernel,
        grid=(rows // 128,),
        in_specs=[block, block],
        out_specs=pl.BlockSpec((2, width), lambda i: (0, 0)),
        out_shape=jax.ShapeDtypeStruct((2, width), f32),
        compiler_params=pltpu.CompilerParams(vmem_limit_bytes=40 * 2**20),
        cost_estimate=LIGHT,
        name="gain_sums",
    )(terms, tokens_all)


class Phases:
    def __init__(self):
        self.marks, self.kept, self.sends = (), [], []

    def __call__(self, *values):
        gate = (*self.marks, *self.sends)
        if gate:
            values = lax.optimization_barrier((*values, *gate))[: len(values)]
        return values if len(values) > 1 else values[0]

    def early(self, *values):
        if self.marks:
            values = lax.optimization_barrier((*values, *self.marks))[: len(values)]
        return values if len(values) > 1 else values[0]

    def send(self, *values):
        self.sends += values

    def keep(self, *values):
        self.kept += values
        return values if len(values) > 1 else values[0]

    def turn(self):
        self.marks, self.kept, self.sends = tuple(self.kept), [], []


class Line:
    def __init__(self, name, size):
        self.name, self.n = name, size
        self.me = lax.axis_index(name)
        self.low = self.me < size // 2

    def slot(self, k):
        n = self.n
        return jnp.where(self.low, (self.me + k) % n, (self.me + n - k) % n)

    def shuffle(self, phase, array):
        n = self.n
        cols = array.shape[1] // n
        out = []
        for shift in range(n):
            target = (self.me + shift) % n
            block = lax.dynamic_slice_in_dim(phase.early(array), target * cols, cols, axis=1)
            if shift:
                phase.send(block)
                block = lax.ppermute(block, self.name, [(j, (j + shift) % n) for j in range(n)])
            out.append(phase.keep(block))
        return out

    def shuffle_rows(self, phase, array, rows):
        n = self.n
        out = []
        for shift in range(1, n):
            target = (self.me + shift) % n
            block = lax.dynamic_slice_in_dim(phase.early(array), target * rows, rows, axis=0)
            out.append(lax.ppermute(block, self.name, [(j, (j + shift) % n) for j in range(n)]))
        return out

    def stack(self, blocks):
        n = self.n
        rows, cols = blocks[0].shape
        out = blank((n * rows, cols))
        for shift, block in enumerate(blocks):
            source = (self.me + n - shift) % n
            out = lax.dynamic_update_slice_in_dim(out, block, source * rows, axis=0)
        return out


class Gather:
    def __init__(self, line, block):
        self.line, self.left, self.right = line, [block], [block]

    def step(self, phase):
        line, n, k = self.line, self.line.n, len(self.left)
        left, right = phase.early(self.left[-1], self.right[-1])
        phase.send(left, right)
        self.left.append(lax.ppermute(left, line.name, [(j, j + 1) for j in range(k - 1, n - 1)]))
        self.right.append(lax.ppermute(right, line.name, [(j, j - 1) for j in range(1, n - k + 1)]))
        phase.keep(self.left[k], self.right[k])
        low_side, high_side = self.right[k], self.left[k]
        if 2 * k >= n:
            low_side = jnp.where(line.me + k < n, self.right[k], self.left[n - k])
            high_side = jnp.where(line.me >= k, self.left[k], self.right[n - k])
        return jnp.where(line.low, low_side, high_side)


class Reduce:
    def __init__(self, line, rows):
        self.line, self.rows, self.k, self.came, self.terms = line, rows, 1, (), None

    def step(self, phase):
        line, n, k = self.line, self.line.n, self.k
        blocks = [jnp.clip(line.me + n - k, 0, n - 1), jnp.clip(line.me - n + k, 0, n - 1)]
        self.terms = phase.early(self.terms)
        sent = relay(self.terms, self.rows, jnp.stack(blocks).astype(jnp.int32), self.came)
        phase.send(*sent)
        self.came = (
            lax.ppermute(sent[0], line.name, [(j, j + 1) for j in range(k)]),
            lax.ppermute(sent[1], line.name, [(j, j - 1) for j in range(n - k, n)]),
        )
        phase.keep(*self.came)
        self.k += 1


def flip(value, name, size, bit):
    return lax.ppermute(value, name, [(j, j ^ bit) for j in range(size)])


def sum_over(value, name, size):
    bit = 1
    while bit < size:
        value = value + flip(value, name, size, bit)
        bit *= 2
    return value


class Spread:
    def __init__(self, name, size, moved, still, moved_left, factor):
        self.name, self.size, self.factor, self.moved_left = name, size, factor, moved_left
        self.moved, self.still = moved, still
        self.bits = [1 << b for b in range(1, size.bit_length() - 1)]
        self.orders = [self.bits, self.bits[::-1]]
        self.block_cols = moved.shape[1] // size

    def blocks(self, moved, wanted):
        cols, index = self.block_cols, lax.axis_index(self.name)
        return jnp.concatenate(
            [lax.dynamic_slice_in_dim(moved, (index ^ r) * cols, cols, axis=1) for r in wanted], axis=1
        )

    def product(self, moved, still):
        left, right = (moved, still) if self.moved_left else (still, moved)
        return self.factor * dot(left, right, 0, 0)

    def listed(self, order, fixed):
        out = [sum(bit for bit, on in fixed.items() if on)]
        for bit in order[::-1]:
            if bit not in fixed:
                out = [*out, *[r + bit for r in out]]
        return out

    def cut(self, array, low, high):
        return array[low:high] if self.moved_left else array[:, low:high]

    def start(self, phase):
        moved = phase(self.moved)
        self.sent = self.product(self.blocks(moved, self.listed(self.bits, {1: True})), self.still).astype(bf16)
        return self.sent

    def cross(self, phase):
        sent = phase.early(self.sent)
        phase.send(sent)
        self.brought = flip(sent, self.name, self.size, 1)
        return self.brought

    def second(self, phase):
        moved, brought = phase(self.moved, self.brought)
        cols, along = self.block_cols, 0 if self.moved_left else 1
        half = self.still.shape[1] // 2
        first_list = self.listed(self.bits, {1: True})
        self.sent, self.kept = [], []
        for which, order in enumerate(self.orders):
            still = self.still[:, which * half : (which + 1) * half]
            part = lax.slice_in_dim(brought, which * half, (which + 1) * half, axis=1 - along)
            for on in (True, False):
                wanted = self.listed(order, {1: False, order[0]: on})
                places = [first_list.index(r + 1) for r in wanted]
                added = jnp.concatenate(
                    [self.cut(part, p * cols, (p + 1) * cols) for p in places], axis=along
                )
                value = (self.product(self.blocks(moved, wanted), still) + added.astype(f32)).astype(bf16)
                (self.sent if on else self.kept).append(value)
        self.done, self.air, self.result = 0, False, None
        return (*self.sent, *self.kept)

    def fly(self, phase):
        sent = phase.early(*self.sent)
        phase.send(*sent)
        self.flying = tuple(
            flip(value, self.name, self.size, order[self.done]) for value, order in zip(sent, self.orders)
        )
        self.done, self.air = self.done + 1, True
        return self.flying

    def land(self, phase):
        along, self.air = 0 if self.moved_left else 1, False
        flying = phase.early(*self.flying)
        totals = [k.astype(f32) + f.astype(f32) for k, f in zip(self.kept, flying)]
        if self.done == len(self.bits):
            self.result = jnp.concatenate(totals, axis=1 - along)
            return (self.result,)
        size = totals[0].shape[along]
        self.sent = [self.cut(t, size // 2, size).astype(bf16) for t in totals]
        self.kept = [self.cut(t, 0, size // 2).astype(bf16) for t in totals]
        return (*self.sent, *self.kept)

    def finish(self, phase):
        while self.result is None:
            (self.land if self.air else self.fly)(phase)
        return self.result


def after(value, *earlier):
    return lax.optimization_barrier((value, *earlier))[0]


def make_body(n_dp, n_mp):
    def body(
        tokens, cotangent, segment, counts, ln_gain, ln_bias, w_qkv, b_qv, w_out, out_bias, w_up, b_up, w_down
    ):
        line, phase = Line("mp", n_mp), Phases()
        keep, turn = phase.keep, phase.turn
        gains, shifts, bias_pair = ln_gain.astype(f32), ln_bias.astype(f32), out_bias.astype(f32)
        share, width = tokens.shape
        head_cols = w_qkv.shape[2]
        heads = head_cols // HEAD
        group = segment.shape[0]
        seg_col, seg_row = segment[:, None], segment[None, :]
        me = line.me
        place = lambda whole, block, index: lax.dynamic_update_slice_in_dim(
            whole, block, index * share, axis=0
        )
        rows_of = lambda whole, index: lax.dynamic_slice_in_dim(whole, index * share, share, axis=0)
        total = lambda value: jnp.sum(value.astype(f32), axis=0)
        slots, last = range(1, n_mp), n_mp - 1

        flat_qkv = jnp.concatenate([w_qkv[:, j] for j in range(3)], axis=1)
        bias_rows = (
            jnp.stack([b_qv[0], jnp.zeros_like(b_qv[0]), b_qv[1]]).astype(f32).reshape(3 * head_cols)
        )
        state = [blank((group, width)), blank((group, width)), blank((group, 3 * head_cols))]

        def project(k, block):
            block = phase(block)
            normed = (norm_parts(block.astype(f32))[0] * gains[0] + shifts[0]).astype(bf16)
            proj = (dot(normed, flat_qkv) + bias_rows).astype(bf16)
            for j, value in enumerate((block, normed, proj)):
                state[j] = keep(place(state[j], value, line.slot(k)))

        slice_rows = w_out.shape[0] // n_dp
        w_slice = lax.dynamic_slice_in_dim(
            w_out, lax.axis_index("dp") * slice_rows, slice_rows, axis=0
        )

        gather = Gather(line, tokens)
        token_slots = [tokens]
        for k in slots:
            token_slots.append(gather.step(phase))
            if k == 2:
                w_slices = lax.all_gather(phase(w_slice), "mp", axis=0)
            project(k - 1, token_slots[k - 1])
            turn()
        cot_gather = Gather(line, cotangent)
        cot_slots = [cotangent, cot_gather.step(phase)]
        w_out_all = lax.all_gather(phase(w_slices), "dp", axis=1).reshape(n_mp * w_out.shape[0], width)
        project(last, token_slots[last])
        tokens_all, normed1_all, projected = state
        attn = keep(attend(projected, seg_col, seg_row, heads))
        turn()

        set_heads = lambda whole, block, index: lax.dynamic_update_slice_in_dim(
            whole, block, index * head_cols, axis=1
        )
        attn_all = blank((group, n_mp * head_cols))
        attn_gather, attn_slots = Gather(line, attn), [attn]
        for k in slots:
            attn_slots.append(attn_gather.step(phase))
            attn_all = keep(set_heads(attn_all, phase(attn_slots[k - 1]), line.slot(k - 1)))
            if k == 2:
                cot_all = blank((group, width))
                for j in range(2):
                    cot_all = place(cot_all, phase(cot_slots[j]), line.slot(j))
                keep(cot_all)
            if k == 1:
                count_here = phase(counts.astype(f32))
                factor = keep((count_here / sum_over(count_here, "dp", n_dp))[0])
            turn()
        reduce_down, reduce2, reduce1 = (Reduce(line, share) for _ in range(3))
        for k in slots[1:]:
            cot_slots.append(cot_gather.step(phase))
            if k == 2:
                attn_all = set_heads(attn_all, phase(attn_slots[last]), line.slot(last))
                middle_all, normed2_all = mix(
                    tokens_all, attn_all, w_out_all, bias_pair[0], gains[1], shifts[1]
                )
                hidden, active = keep(*feed_up(normed2_all, w_up, b_up.astype(f32)))
                keep(middle_all, normed2_all)
            if k == 3:
                reduce_down.terms = keep(dot(phase(active), w_down).astype(bf16))
            if k > 2:
                cot_all = keep(place(cot_all, phase(cot_slots[k - 1]), line.slot(k - 1)))
            turn()

        reduce_down.step(phase)
        cot_all = place(cot_all, phase(cot_slots[last]), line.slot(last))
        d_hidden_all = keep(hidden_back(cot_all, hidden, w_down))
        reduce2.terms = keep(dot(d_hidden_all, w_up, 1, 1).astype(bf16))
        turn()
        for k in slots:
            reduce2.step(phase)
            if k == 1:
                feed_full = keep(
                    weight_grads(factor, [(phase(normed2_all), d_hidden_all), (cot_all, active)])
                )
            if k == 2:
                grad_feed = lax.psum_scatter(phase(feed_full), "dp", scatter_dimension=0, tiled=True)
                split_sums = keep(factor * total(phase(d_hidden_all)))
            turn()
        own = me[None].astype(jnp.int32)
        reduce_down.step(phase)
        d_middle, d_branch, own_sums = keep(
            *middle_back(own, phase(reduce2.terms), reduce2.came, middle_all, gains[1], cotangent)
        )
        d_attn_own = keep(dot(d_branch, w_out_all, 1, 1).astype(bf16))
        spread_out = Spread("dp", n_dp, after(d_branch, d_attn_own), rows_of(attn_all, me), False, factor)
        keep(spread_out.start(phase))
        turn()
        d_attn_blocks = line.shuffle(phase, d_attn_own)
        spread_out.cross(phase)
        keep(*spread_out.second(phase))
        turn()
        reduce_down.step(phase)
        keep(*spread_out.fly(phase))
        d_attn = line.stack(phase(*d_attn_blocks))
        grad_proj = keep(attend_back(projected, d_attn, seg_col, seg_row, heads))
        half = line.low.astype(jnp.int32)
        reduce1.terms = keep(half_product(grad_proj, flat_qkv, half))
        turn()
        for k in slots:
            reduce1.step(phase)
            if k == 1:
                keep(*spread_out.land(phase))
                keep(*spread_out.fly(phase))
                reduce1.terms = keep(half_product(phase(grad_proj), flat_qkv, 1 - half, reduce1.terms))
                qkv_full = weight_grads(factor, [(after(normed1_all, reduce1.terms), grad_proj)])
                grad_qkv = lax.psum_scatter(qkv_full, "dp", scatter_dimension=0, tiled=True)
                keep(qkv_full, grad_feed)
            if k == 2:
                out_rows = keep(spread_out.finish(phase))
                heads_sum = [total(phase(grad_proj)[:, :head_cols]), total(grad_proj[:, 2 * head_cols :])]
                gain1 = gain_sums(phase(reduce1.terms), tokens_all)
                full_sums = jnp.concatenate([gain1, own_sums], axis=0).reshape(-1)
                sums = keep(
                    jnp.concatenate(
                        [
                            sum_over(factor * full_sums, "mp", n_mp),
                            *[factor * s for s in heads_sum],
                            split_sums,
                        ]
                    )
                )
            if k == 3:
                sums = jnp.sum(lax.all_gather(phase(sums).reshape(1, 8, -1), "dp", axis=0, tiled=True), axis=0).reshape(-1)
                grad_feed = phase(grad_feed).astype(f32)
                feed_cols = grad_feed.shape[1] // 2
                grad_up, grad_down = keep(grad_feed[:, :feed_cols], grad_feed[:, feed_cols:].T)
                keep(grad_qkv)
                for _ in slots[3:]:
                    reduce_down.step(phase)
                down_sum = sum(
                    value.astype(f32)
                    for value in (rows_of(phase(reduce_down.terms), me), *reduce_down.came)
                )
                layer_out = keep((rows_of(middle_all, me) + down_sum + bias_pair[1]).astype(bf16))
            turn()
        out_blocks = line.shuffle_rows(phase, out_rows.astype(bf16), head_cols)
        grad_input = input_back(
            own, factor, phase(reduce1.terms), reduce1.came, tokens, gains[0], d_middle
        )
        full_sums = sums[: 6 * width].reshape(6, width)
        split_sums = sums[6 * width :]
        own_block = lax.dynamic_slice_in_dim(out_rows, me * head_cols, head_cols, axis=0)
        for block in out_blocks:
            own_block = own_block + block.astype(f32)
        grad_out = own_block
        grad_qkv = phase(grad_qkv).astype(f32)
        return (
            layer_out,
            grad_input,
            jnp.stack([full_sums[0], full_sums[2]]),
            jnp.stack([full_sums[1], full_sums[3]]),
            jnp.stack([grad_qkv[:, j * head_cols : (j + 1) * head_cols] for j in range(3)], axis=1),
            split_sums[: 2 * head_cols].reshape(2, head_cols),
            grad_out,
            full_sums[4:],
            grad_up,
            split_sums[2 * head_cols :],
            grad_down,
        )

    return body


def solution(mesh):
    split = P(("dp", "mp"), None)
    return jax.shard_map(
        make_body(mesh.shape["dp"], mesh.shape["mp"]),
        mesh=mesh,
        in_specs=(
            split, split, P("dp"), P("dp"), P(), P(), P(None, None, "mp"), P(None, "mp"), P("mp", None), P(),
            P(None, "mp"), P("mp"), P("mp", None),
        ),
        out_specs=(
            split, split, P(), P(), P("dp", None, "mp"), P(None, "mp"), P("mp", "dp"), P(), P("dp", "mp"), P("mp"),
            P("mp", "dp"),
        ),
        check_vma=False,
    )
```

```python
import functools
import jax
import jax.numpy as jnp
from jax import lax
from jax.experimental import pallas as pl
from jax.experimental.pallas import tpu as pltpu
from jax.sharding import PartitionSpec as P

HEAD = 128
SEQ = 1024
BLOCK = 256
SCALE = HEAD ** (-0.5)
f32 = jnp.float32
bf16 = jnp.bfloat16
MIB = 2**20
COST = pl.CostEstimate(flops=1 << 20, bytes_accessed=1 << 16, transcendentals=0)


def dot(left, right, left_dim=1, right_dim=0):
    return lax.dot_general(
        left, right, (((left_dim,), (right_dim,)), ((), ())), preferred_element_type=f32
    )


def block_probs(q_block, k_ref, seg_col, seg_row, block, reach):
    start = block * BLOCK
    scores = dot(k_ref[:reach, :], q_block, 1, 1) * SCALE
    key_place = lax.broadcasted_iota(jnp.int32, (reach, BLOCK), 0)
    query_place = start + lax.broadcasted_iota(jnp.int32, (reach, BLOCK), 1)
    allowed = (seg_col[:reach, :] == seg_row[:, start : start + BLOCK]) & (
        key_place <= query_place
    )
    scores = jnp.where(allowed, scores, -1e30)
    expo = jnp.exp(scores - jnp.max(scores, axis=0, keepdims=True))
    return expo * (1.0 / jnp.sum(expo, axis=0, keepdims=True))


def attend_kernel(q_ref, k_ref, v_ref, seg_col, seg_row, out_ref):
    for block in range(SEQ // BLOCK):
        rows = slice(block * BLOCK, (block + 1) * BLOCK)
        reach = (block + 1) * BLOCK
        probs = block_probs(q_ref[rows, :], k_ref, seg_col, seg_row, block, reach)
        out_ref[rows, :] = dot(probs.astype(bf16), v_ref[:reach, :], 0, 0).astype(bf16)


def attend(projected, seg_col, seg_row, heads):
    tokens = projected.shape[0]
    column = lambda part: pl.BlockSpec((SEQ, HEAD), lambda r, h: (r, part * heads + h))
    return pl.pallas_call(
        attend_kernel,
        grid=(tokens // SEQ, heads),
        in_specs=[
            column(0),
            column(1),
            column(2),
            pl.BlockSpec((SEQ, 1), lambda r, h: (r, 0)),
            pl.BlockSpec((1, SEQ), lambda r, h: (0, r)),
        ],
        out_specs=pl.BlockSpec((SEQ, HEAD), lambda r, h: (r, h)),
        out_shape=jax.ShapeDtypeStruct((tokens, heads * HEAD), bf16),
        compiler_params=pltpu.CompilerParams(vmem_limit_bytes=24 * MIB),
        cost_estimate=COST,
        name="attend",
    )(projected, projected, projected, seg_col, seg_row)


def attend_back_kernel(
    heads, q_ref, k_ref, v_ref, grad_ref, seg_col, seg_row, out_ref, dk_ref, dv_ref
):
    head = pl.program_id(1)
    width = heads * HEAD
    column = lambda part: pl.ds(pl.multiple_of(part * width + head * HEAD, HEAD), HEAD)
    dk_ref[...] = jnp.zeros_like(dk_ref)
    dv_ref[...] = jnp.zeros_like(dv_ref)
    for block in range(SEQ // BLOCK):
        rows = slice(block * BLOCK, (block + 1) * BLOCK)
        reach = (block + 1) * BLOCK
        q_block = q_ref[rows, :]
        g_block = grad_ref[rows, :]
        probs = block_probs(q_block, k_ref, seg_col, seg_row, block, reach)
        d_probs = dot(v_ref[:reach, :], g_block, 1, 1)
        delta = jnp.sum(probs * d_probs, axis=0, keepdims=True)
        d_scores = (probs * (d_probs - delta)).astype(bf16)
        dv_ref[:reach, :] += dot(probs.astype(bf16), g_block)
        dk_ref[:reach, :] += dot(d_scores, q_block)
        out_ref[rows, column(0)] = (dot(d_scores, k_ref[:reach, :], 0, 0) * SCALE).astype(bf16)
    out_ref[:, column(1)] = (dk_ref[...] * SCALE).astype(bf16)
    out_ref[:, column(2)] = dv_ref[...].astype(bf16)


def attend_back(projected, grad_attn, seg_col, seg_row, heads):
    tokens = projected.shape[0]
    column = lambda part: pl.BlockSpec((SEQ, HEAD), lambda r, h: (r, part * heads + h))
    return pl.pallas_call(
        functools.partial(attend_back_kernel, heads),
        grid=(tokens // SEQ, heads),
        in_specs=[
            column(0),
            column(1),
            column(2),
            column(0),
            pl.BlockSpec((SEQ, 1), lambda r, h: (r, 0)),
            pl.BlockSpec((1, SEQ), lambda r, h: (0, r)),
        ],
        out_specs=pl.BlockSpec((SEQ, 3 * heads * HEAD), lambda r, h: (r, 0)),
        out_shape=jax.ShapeDtypeStruct((tokens, 3 * heads * HEAD), bf16),
        scratch_shapes=[pltpu.VMEM((SEQ, HEAD), f32), pltpu.VMEM((SEQ, HEAD), f32)],
        compiler_params=pltpu.CompilerParams(vmem_limit_bytes=32 * MIB),
        cost_estimate=COST,
        name="attend_back",
    )(projected, projected, projected, grad_attn, seg_col, seg_row)


def norm_parts(value):
    mean = jnp.mean(value, axis=-1, keepdims=True)
    centered = value - mean
    inverse = lax.rsqrt(jnp.mean(centered * centered, axis=-1, keepdims=True) + 1e-05)
    return centered * inverse, inverse


def norm_backward(grad, gain, scaled, inverse):
    inner = grad * gain
    return inverse * (
        inner
        - jnp.mean(inner, axis=-1, keepdims=True)
        - scaled * jnp.mean(inner * scaled, axis=-1, keepdims=True)
    )


def gelu_parts(value):
    c = 0.7978845608028654
    square = value * value
    tanh = jnp.tanh(c * value * (1.0 + 0.044715 * square))
    half = 0.5 * (1.0 + tanh)
    slope = half + 0.5 * value * (1.0 - tanh * tanh) * c * (1.0 + 3 * 0.044715 * square)
    return value * half, slope


def mix_kernel(index_ref, sum_ref, heads_ref, w_ref, gain_ref, shift_ref, middle_ref, normed_ref):
    middle = sum_ref[...] + dot(heads_ref[...], w_ref[...])
    middle_ref[...] = middle
    normed_ref[...] = (norm_parts(middle)[0] * gain_ref[...] + shift_ref[...]).astype(bf16)


def mix(summed, heads_block, w_out_all, index, gain, shift):
    tokens, width = summed.shape
    cols = heads_block.shape[1]
    step = 256
    row = lambda size: pl.BlockSpec((step, size), lambda i, at: (i, 0))
    one = pl.BlockSpec((1, width), lambda i, at: (0, 0))
    return pl.pallas_call(
        mix_kernel,
        grid_spec=pltpu.PrefetchScalarGridSpec(
            num_scalar_prefetch=1,
            grid=(tokens // step,),
            in_specs=[row(width), row(cols), pl.BlockSpec((cols, width), lambda i, at: (at[0], 0)), one, one],
            out_specs=[row(width), row(width)],
        ),
        out_shape=[
            jax.ShapeDtypeStruct((tokens, width), f32),
            jax.ShapeDtypeStruct((tokens, width), bf16),
        ],
        compiler_params=pltpu.CompilerParams(vmem_limit_bytes=48 * MIB),
        cost_estimate=COST,
        name="mix",
    )(index[None].astype(jnp.int32), summed, heads_block, w_out_all, gain[None], shift[None])


def up_kernel(x_ref, w_ref, b_ref, hidden_ref, active_ref):
    hidden = dot(x_ref[...], w_ref[...]) + b_ref[...]
    hidden_ref[...] = hidden
    active_ref[...] = gelu_parts(hidden)[0].astype(bf16)


def feed_up(normed, w_up, b_up):
    tokens, width = normed.shape
    cols = w_up.shape[1]
    step = 256
    col = lambda rows: pl.BlockSpec((rows, step), lambda i: (0, i))
    return pl.pallas_call(
        up_kernel,
        grid=(cols // step,),
        in_specs=[pl.BlockSpec((tokens, width), lambda i: (0, 0)), col(width), col(1)],
        out_specs=[col(tokens), col(tokens)],
        out_shape=[
            jax.ShapeDtypeStruct((tokens, cols), f32),
            jax.ShapeDtypeStruct((tokens, cols), bf16),
        ],
        compiler_params=pltpu.CompilerParams(vmem_limit_bytes=48 * MIB),
        cost_estimate=COST,
        name="feed_up",
    )(normed, w_up, b_up[None])


def hidden_kernel(index_ref, cot_ref, hidden_ref, w_ref, *refs):
    slope = gelu_parts(hidden_ref[...])[1]
    refs[-1][...] = (dot(cot_ref[...], w_ref[...], 1, 1) * slope).astype(bf16)


def hidden_back(cot_all, hidden, w_down, half, earlier=None):
    tokens, width = cot_all.shape
    rows = tokens // 2
    cols, step = hidden.shape[1], 512
    given = [] if earlier is None else [earlier]
    return pl.pallas_call(
        hidden_kernel,
        grid_spec=pltpu.PrefetchScalarGridSpec(
            num_scalar_prefetch=1,
            grid=(cols // step,),
            in_specs=[
                pl.BlockSpec((rows, width), lambda i, at: (at[0], 0)),
                pl.BlockSpec((rows, step), lambda i, at: (at[0], i)),
                pl.BlockSpec((step, width), lambda i, at: (i, 0)),
                *[pl.BlockSpec(memory_space=pl.ANY) for _ in given],
            ],
            out_specs=pl.BlockSpec((rows, step), lambda i, at: (at[0], i)),
        ),
        out_shape=jax.ShapeDtypeStruct((tokens, cols), bf16),
        input_output_aliases={4: 0} if given else {},
        compiler_params=pltpu.CompilerParams(vmem_limit_bytes=20 * MIB),
        cost_estimate=COST,
        name="hidden_back",
    )(half[None], cot_all, hidden, w_down, *given)


def slope_kernel(index_ref, grad_ref, hidden_ref, out_ref):
    out_ref[...] = (grad_ref[...] * gelu_parts(hidden_ref[...])[1]).astype(bf16)


def slope_back(d_active, hidden, half):
    tokens, cols = hidden.shape
    step = 64
    steps = tokens // 2 // step
    place = pl.BlockSpec((step, cols), lambda i, at: (at[0] * steps + i, 0))
    return pl.pallas_call(
        slope_kernel,
        grid_spec=pltpu.PrefetchScalarGridSpec(
            num_scalar_prefetch=1,
            grid=(steps,),
            in_specs=[pl.BlockSpec((step, cols), lambda i, at: (i, 0)), place],
            out_specs=place,
        ),
        out_shape=jax.ShapeDtypeStruct((tokens, cols), bf16),
        compiler_params=pltpu.CompilerParams(vmem_limit_bytes=12 * MIB),
        cost_estimate=COST,
        name="slope_back",
    )(half[None], d_active, hidden)


def grads_kernel(factor_ref, left_ref, right_ref, *refs):
    out_ref, turned_ref = refs[-2:]

    @pl.when(pl.program_id(0) == 0)
    def _():
        turned_ref[...] = left_ref[...].T

    out_ref[...] = (factor_ref[0] * dot(turned_ref[...], right_ref[...])).astype(bf16)


def weight_grads(factor, left, right, parts=1, part=0, earlier=None):
    tokens, width = left.shape
    cols, step = right.shape[1], 256
    steps = cols // step
    given = [] if earlier is None else [earlier]
    return pl.pallas_call(
        grads_kernel,
        grid=(steps,),
        in_specs=[
            pl.BlockSpec(memory_space=pltpu.SMEM),
            pl.BlockSpec((tokens, width), lambda i: (0, 0)),
            pl.BlockSpec((tokens, step), lambda i: (0, i)),
            *[pl.BlockSpec(memory_space=pl.ANY) for _ in given],
        ],
        out_specs=pl.BlockSpec((width, step), lambda i: (0, part * steps + i)),
        out_shape=jax.ShapeDtypeStruct((width, parts * cols), bf16),
        input_output_aliases={3: 0} if given else {},
        scratch_shapes=[pltpu.VMEM((width, tokens), bf16)],
        compiler_params=pltpu.CompilerParams(vmem_limit_bytes=48 * MIB),
        cost_estimate=COST,
        name="weight_grads",
    )(factor[None], left, right, *given)


def half_kernel(index_ref, x_ref, w_ref, *refs):
    refs[-1][...] = dot(x_ref[...], w_ref[...], 1, 1).astype(bf16)


def half_product(x, weight, half, earlier=None):
    tokens, depth = x.shape
    rows = tokens // 2
    cols, step = weight.shape[0], 512
    given = [] if earlier is None else [earlier]
    return pl.pallas_call(
        half_kernel,
        grid_spec=pltpu.PrefetchScalarGridSpec(
            num_scalar_prefetch=1,
            grid=(cols // step,),
            in_specs=[
                pl.BlockSpec((rows, depth), lambda i, at: (at[0], 0)),
                pl.BlockSpec((step, depth), lambda i, at: (i, 0)),
                *[pl.BlockSpec(memory_space=pl.ANY) for _ in given],
            ],
            out_specs=pl.BlockSpec((rows, step), lambda i, at: (at[0], i)),
        ),
        out_shape=jax.ShapeDtypeStruct((tokens, cols), bf16),
        input_output_aliases={3: 0} if given else {},
        compiler_params=pltpu.CompilerParams(vmem_limit_bytes=40 * MIB),
        cost_estimate=COST,
        name="half_product",
    )(half[None], x, weight, *given)


def relay_kernel(index_ref, right_ref, left_ref, *refs):
    to_right, to_left = refs[-2:]
    if len(refs) == 2:
        to_right[...], to_left[...] = right_ref[...], left_ref[...]
    else:
        to_right[...] = (right_ref[...].astype(f32) + refs[0][...].astype(f32)).astype(bf16)
        to_left[...] = (left_ref[...].astype(f32) + refs[1][...].astype(f32)).astype(bf16)


def relay(terms, rows, index, came):
    width = terms.shape[1]
    step = min(rows, 128)
    steps = rows // step
    block = pl.BlockSpec((step, width), lambda i, at: (i, 0))
    return pl.pallas_call(
        relay_kernel,
        grid_spec=pltpu.PrefetchScalarGridSpec(
            num_scalar_prefetch=1,
            grid=(steps,),
            in_specs=[
                pl.BlockSpec((step, width), lambda i, at: (at[0] * steps + i, 0)),
                pl.BlockSpec((step, width), lambda i, at: (at[1] * steps + i, 0)),
                *[block] * len(came),
            ],
            out_specs=[block, block],
        ),
        out_shape=[jax.ShapeDtypeStruct((rows, width), bf16)] * 2,
        compiler_params=pltpu.CompilerParams(vmem_limit_bytes=12 * MIB),
        cost_estimate=COST,
        name="relay",
    )(index, terms, terms, *came)


def summed_back(term_ref, left_ref, right_ref, value_ref, gain_ref):
    grad = term_ref[...].astype(f32) + left_ref[...].astype(f32) + right_ref[...].astype(f32)
    scaled, inverse = norm_parts(value_ref[...].astype(f32))
    return grad, scaled, norm_backward(grad, gain_ref[...], scaled, inverse)


def middle_back_kernel(
    index_ref, term_ref, left_ref, right_ref, value_ref, gain_ref, cot_ref, middle_ref, branch_ref, sums_ref
):
    @pl.when(pl.program_id(0) == 0)
    def _():
        sums_ref[...] = jnp.zeros_like(sums_ref)

    grad, scaled, back = summed_back(term_ref, left_ref, right_ref, value_ref, gain_ref)
    cot = cot_ref[...].astype(f32)
    middle = cot + back
    branch = middle.astype(bf16)
    middle_ref[...], branch_ref[...] = middle, branch
    for row, value in enumerate((grad * scaled, grad, branch.astype(f32), cot)):
        sums_ref[row : row + 1, :] += jnp.sum(value, axis=0, keepdims=True)


def input_back_kernel(
    index_ref, factor_ref, term_ref, left_ref, right_ref, value_ref, gain_ref, middle_ref, out_ref
):
    back = summed_back(term_ref, left_ref, right_ref, value_ref, gain_ref)[2]
    out_ref[...] = factor_ref[0] * (middle_ref[...] + back)


def back_specs(rows, width):
    step = min(rows, 128)
    steps = rows // step
    here = pl.BlockSpec((step, width), lambda i, at: (i, 0))
    own = pl.BlockSpec((step, width), lambda i, at: (at[0] * steps + i, 0))
    return steps, here, own, pl.BlockSpec((1, width), lambda i, at: (0, 0))


def middle_back(index, terms, came, middle_all, gain, cot):
    rows, width = cot.shape
    steps, here, own, one = back_specs(rows, width)
    return pl.pallas_call(
        middle_back_kernel,
        grid_spec=pltpu.PrefetchScalarGridSpec(
            num_scalar_prefetch=1,
            grid=(steps,),
            in_specs=[own, here, here, own, one, here],
            out_specs=[here, here, pl.BlockSpec((4, width), lambda i, at: (0, 0))],
        ),
        out_shape=[
            jax.ShapeDtypeStruct((rows, width), f32),
            jax.ShapeDtypeStruct((rows, width), bf16),
            jax.ShapeDtypeStruct((4, width), f32),
        ],
        compiler_params=pltpu.CompilerParams(vmem_limit_bytes=16 * MIB),
        cost_estimate=COST,
        name="middle_back",
    )(index, terms, *came, middle_all, gain[None], cot)


def input_back(index, factor, terms, came, tokens, gain, d_middle):
    rows, width = tokens.shape
    steps, here, own, one = back_specs(rows, width)
    return pl.pallas_call(
        input_back_kernel,
        grid_spec=pltpu.PrefetchScalarGridSpec(
            num_scalar_prefetch=1,
            grid=(steps,),
            in_specs=[pl.BlockSpec(memory_space=pltpu.SMEM), own, here, here, here, one, here],
            out_specs=here,
        ),
        out_shape=jax.ShapeDtypeStruct((rows, width), f32),
        compiler_params=pltpu.CompilerParams(vmem_limit_bytes=16 * MIB),
        cost_estimate=COST,
        name="input_back",
    )(index, factor[None], terms, *came, tokens, gain[None], d_middle)


def blank_kernel(out_ref):
    pass


def blank(shape):
    return pl.pallas_call(
        blank_kernel,
        out_specs=pl.BlockSpec(memory_space=pl.ANY),
        out_shape=jax.ShapeDtypeStruct(shape, bf16),
        name="blank",
    )()


def sums_kernel(term_ref, token_ref, out_ref):
    @pl.when(pl.program_id(0) == 0)
    def _():
        out_ref[...] = jnp.zeros_like(out_ref)

    term = term_ref[...].astype(f32)
    scaled = norm_parts(token_ref[...].astype(f32))[0]
    out_ref[0:1, :] += jnp.sum(term * scaled, axis=0, keepdims=True)
    out_ref[1:2, :] += jnp.sum(term, axis=0, keepdims=True)


def gain_sums(terms, tokens_all):
    rows, width = terms.shape
    block = pl.BlockSpec((128, width), lambda i: (i, 0))
    return pl.pallas_call(
        sums_kernel,
        grid=(rows // 128,),
        in_specs=[block, block],
        out_specs=pl.BlockSpec((2, width), lambda i: (0, 0)),
        out_shape=jax.ShapeDtypeStruct((2, width), f32),
        compiler_params=pltpu.CompilerParams(vmem_limit_bytes=12 * MIB),
        cost_estimate=COST,
        name="gain_sums",
    )(terms, tokens_all)


class Phases:
    def __init__(self):
        self.marks, self.kept, self.sends = (), [], []

    def __call__(self, *values):
        gate = (*self.marks, *self.sends)
        if gate:
            values = lax.optimization_barrier((*values, *gate))[: len(values)]
        return values if len(values) > 1 else values[0]

    def early(self, *values):
        if self.marks:
            values = lax.optimization_barrier((*values, *self.marks))[: len(values)]
        return values if len(values) > 1 else values[0]

    def send(self, *values):
        self.sends += values

    def keep(self, *values):
        self.kept += values
        return values if len(values) > 1 else values[0]

    def turn(self):
        self.marks, self.kept, self.sends = tuple(self.kept), [], []


class Line:
    def __init__(self, name, size):
        self.name, self.n = name, size
        self.me = lax.axis_index(name)
        self.low = self.me < size // 2

    def slot(self, k):
        n = self.n
        return jnp.where(self.low, (self.me + k) % n, (self.me + n - k) % n)

    def shuffle(self, phase, array):
        n = self.n
        cols = array.shape[1] // n
        out = []
        for shift in range(n):
            target = (self.me + shift) % n
            block = lax.dynamic_slice_in_dim(phase.early(array), target * cols, cols, axis=1)
            if shift:
                phase.send(block)
                block = lax.ppermute(block, self.name, [(j, (j + shift) % n) for j in range(n)])
            out.append(phase.keep(block))
        return out

    def shuffle_rows(self, phase, array, rows):
        n = self.n
        out = []
        for shift in range(1, n):
            target = (self.me + shift) % n
            block = lax.dynamic_slice_in_dim(phase.early(array), target * rows, rows, axis=0)
            out.append(lax.ppermute(block, self.name, [(j, (j + shift) % n) for j in range(n)]))
        return out

    def stack(self, blocks):
        n = self.n
        rows, cols = blocks[0].shape
        out = blank((n * rows, cols))
        for shift, block in enumerate(blocks):
            source = (self.me + n - shift) % n
            out = lax.dynamic_update_slice_in_dim(out, block, source * rows, axis=0)
        return out


class Gather:
    def __init__(self, line, block):
        self.line, self.left, self.right, self.slots = line, [block], [block], {0: block}

    def step(self, phase):
        line, n, k = self.line, self.line.n, len(self.left)
        left, right = phase.early(self.left[-1], self.right[-1])
        phase.send(left, right)
        self.left.append(lax.ppermute(left, line.name, [(j, j + 1) for j in range(k - 1, n - 1)]))
        self.right.append(lax.ppermute(right, line.name, [(j, j - 1) for j in range(1, n - k + 1)]))
        phase.keep(self.left[k], self.right[k])

    def slot(self, phase, k):
        if k not in self.slots:
            line, n = self.line, self.line.n
            if 2 * k < n:
                left, right = phase(self.left[k], self.right[k])
                value = jnp.where(line.low, right, left)
            else:
                left, right, left_far, right_far = phase(
                    self.left[n - k], self.right[n - k], self.left[k], self.right[k]
                )
                low_side = jnp.where(line.me + k < n, right_far, left)
                high_side = jnp.where(line.me >= k, left_far, right)
                value = jnp.where(line.low, low_side, high_side)
            self.slots[k] = value
        return self.slots[k]


class Reduce:
    def __init__(self, line, rows):
        self.line, self.rows, self.k, self.came, self.terms = line, rows, 1, (), None

    def step(self, phase):
        line, n, k = self.line, self.line.n, self.k
        blocks = [jnp.clip(line.me + n - k, 0, n - 1), jnp.clip(line.me - n + k, 0, n - 1)]
        self.terms = phase.early(self.terms)
        sent = relay(self.terms, self.rows, jnp.stack(blocks).astype(jnp.int32), self.came)
        phase.send(*sent)
        self.came = (
            lax.ppermute(sent[0], line.name, [(j, j + 1) for j in range(k)]),
            lax.ppermute(sent[1], line.name, [(j, j - 1) for j in range(n - k, n)]),
        )
        phase.keep(*self.came)
        self.k += 1


def flip(value, name, size, bit):
    return lax.ppermute(value, name, [(j, j ^ bit) for j in range(size)])


def sum_over(value, name, size):
    bit = 1
    while bit < size:
        value = value + flip(value, name, size, bit)
        bit *= 2
    return value


class Spread:
    def __init__(self, name, size, moved, still, moved_left, factor):
        self.name, self.size, self.factor, self.moved_left = name, size, factor, moved_left
        self.moved, self.still = moved, still
        self.bits = [1 << b for b in range(1, size.bit_length() - 1)]
        self.orders = [self.bits, self.bits[::-1]]
        self.block_cols = moved.shape[1] // size

    def blocks(self, moved, wanted):
        cols, index = self.block_cols, lax.axis_index(self.name)
        return jnp.concatenate(
            [lax.dynamic_slice_in_dim(moved, (index ^ r) * cols, cols, axis=1) for r in wanted], axis=1
        )

    def product(self, moved, still):
        left, right = (moved, still) if self.moved_left else (still, moved)
        return self.factor * dot(left, right, 0, 0)

    def listed(self, order, fixed):
        out = [sum(bit for bit, on in fixed.items() if on)]
        for bit in order[::-1]:
            if bit not in fixed:
                out = [*out, *[r + bit for r in out]]
        return out

    def cut(self, array, low, high):
        return array[low:high] if self.moved_left else array[:, low:high]

    def start(self, phase):
        moved = phase(self.moved)
        self.sent = self.product(self.blocks(moved, self.listed(self.bits, {1: True})), self.still).astype(bf16)
        return self.sent

    def cross(self, phase):
        sent = phase.early(self.sent)
        phase.send(sent)
        self.brought = flip(sent, self.name, self.size, 1)
        return self.brought

    def second(self, phase):
        moved, brought = phase(self.moved, self.brought)
        cols, along = self.block_cols, 0 if self.moved_left else 1
        half = self.still.shape[1] // 2
        first_list = self.listed(self.bits, {1: True})
        self.sent, self.kept = [], []
        for which, order in enumerate(self.orders):
            still = self.still[:, which * half : (which + 1) * half]
            part = lax.slice_in_dim(brought, which * half, (which + 1) * half, axis=1 - along)
            for on in (True, False):
                wanted = self.listed(order, {1: False, order[0]: on})
                places = [first_list.index(r + 1) for r in wanted]
                added = jnp.concatenate(
                    [self.cut(part, p * cols, (p + 1) * cols) for p in places], axis=along
                )
                value = (self.product(self.blocks(moved, wanted), still) + added.astype(f32)).astype(bf16)
                (self.sent if on else self.kept).append(value)
        self.done, self.air, self.result = 0, False, None
        return (*self.sent, *self.kept)

    def fly(self, phase):
        sent = phase.early(*self.sent)
        phase.send(*sent)
        self.flying = tuple(
            flip(value, self.name, self.size, order[self.done]) for value, order in zip(sent, self.orders)
        )
        self.done, self.air = self.done + 1, True
        return self.flying

    def land(self, phase):
        along, self.air = 0 if self.moved_left else 1, False
        flying = phase.early(*self.flying)
        totals = [k.astype(f32) + f.astype(f32) for k, f in zip(self.kept, flying)]
        if self.done == len(self.bits):
            self.result = jnp.concatenate(totals, axis=1 - along)
            return (self.result,)
        size = totals[0].shape[along]
        self.sent = [self.cut(t, size // 2, size).astype(bf16) for t in totals]
        self.kept = [self.cut(t, 0, size // 2).astype(bf16) for t in totals]
        return (*self.sent, *self.kept)

    def finish(self, phase):
        while self.result is None:
            (self.land if self.air else self.fly)(phase)
        return self.result


def after(value, *earlier):
    return lax.optimization_barrier((value, *earlier))[0]


def make_body(n_dp, n_mp):
    def body(
        tokens, cotangent, segment, counts, ln_gain, ln_bias, w_qkv, b_qv, w_out, out_bias, w_up, b_up, w_down
    ):
        line, phase = Line("mp", n_mp), Phases()
        keep, turn = phase.keep, phase.turn
        gains, shifts, bias_pair = ln_gain.astype(f32), ln_bias.astype(f32), out_bias.astype(f32)
        share, width = tokens.shape
        head_cols = w_qkv.shape[2]
        heads = head_cols // HEAD
        group = segment.shape[0]
        seg_col, seg_row = segment[:, None], segment[None, :]
        me = line.me
        place = lambda whole, block, index: lax.dynamic_update_slice_in_dim(
            whole, block, index * share, axis=0
        )
        rows_of = lambda whole, index: lax.dynamic_slice_in_dim(whole, index * share, share, axis=0)
        total = lambda value: jnp.sum(value.astype(f32), axis=0)
        slots, last = range(1, n_mp), n_mp - 1

        flat_qkv = jnp.concatenate([w_qkv[:, j] for j in range(3)], axis=1)
        bias_rows = (
            jnp.stack([b_qv[0], jnp.zeros_like(b_qv[0]), b_qv[1]]).astype(f32).reshape(3 * head_cols)
        )
        state = [blank((group, width)), blank((group, width)), blank((group, 3 * head_cols))]

        def project(k):
            block = phase(gather.slot(phase, k))
            normed = (norm_parts(block.astype(f32))[0] * gains[0] + shifts[0]).astype(bf16)
            proj = (dot(normed, flat_qkv) + bias_rows).astype(bf16)
            for j, value in enumerate((block, normed, proj)):
                state[j] = keep(place(state[j], value, line.slot(k)))

        slice_rows = w_out.shape[0] // n_dp
        w_slice = lax.dynamic_slice_in_dim(
            w_out, lax.axis_index("dp") * slice_rows, slice_rows, axis=0
        )

        gather = Gather(line, tokens)
        for k in slots:
            gather.step(phase)
            if k == 2:
                w_slices = lax.all_gather(phase(w_slice), "mp", axis=0)
            project(k - 1)
            turn()
        cot_gather = Gather(line, cotangent)
        cot_gather.step(phase)
        w_out_all = lax.all_gather(phase(w_slices), "dp", axis=1).reshape(n_mp * w_out.shape[0], width)
        project(last)
        tokens_all, normed1_all, projected = state
        attn = keep(attend(projected, seg_col, seg_row, heads))
        turn()

        set_heads = lambda whole, block, index: lax.dynamic_update_slice_in_dim(
            whole, block, index * head_cols, axis=1
        )
        w_rows = lambda k: lax.dynamic_slice_in_dim(w_out_all, line.slot(k) * head_cols, head_cols, axis=0)
        half = line.low.astype(jnp.int32)
        attn_all = blank((group, n_mp * head_cols))
        cot_all = place(blank((group, width)), phase(cotangent), me)

        def place_near():
            nonlocal cot_all
            for j in range(1, n_mp // 2):
                for came, index in ((cot_gather.left[j], me - j), (cot_gather.right[j], me + j)):
                    here = (index >= 0) & (index < n_mp) & ((index < n_mp // 2) == line.low)
                    came = phase(came)
                    cot_all = place(cot_all, jnp.where(here, came, cotangent), jnp.where(here, index, me))
            cot_all = keep(phase(cot_all))

        attn_gather = Gather(line, attn)
        for k in slots:
            attn_gather.step(phase)
            attn_all = keep(set_heads(attn_all, phase(attn_gather.slot(phase, k - 1)), line.slot(k - 1)))
            if k == 1:
                middle_sum = keep(tokens_all.astype(f32) + bias_pair[0] + dot(phase(attn), w_out))
                count_here = phase(counts.astype(f32))
                factor = keep((count_here / sum_over(count_here, "dp", n_dp))[0])
            if k == 2 and n_mp == 4:
                place_near()
                near_rows = lax.dynamic_slice_in_dim(cot_all, (1 - half) * (group // 2), group // 2, axis=0)
                near_active = keep(dot(near_rows, w_down, 1, 1))
            if k == last:
                for j in range(1, last):
                    middle_sum = keep(middle_sum + dot(phase(attn_gather.slot(phase, j)), w_rows(j)))
            turn()
        reduce_down, reduce2, reduce1 = (Reduce(line, share) for _ in range(3))
        for k in slots[1:]:
            cot_gather.step(phase)
            if k == 2:
                heads_last = attn_gather.slot(phase, last)
                middle_all, normed2_all = mix(
                    middle_sum, heads_last, w_out_all, line.slot(last), gains[1], shifts[1]
                )
                hidden, active = keep(*feed_up(normed2_all, w_up, b_up.astype(f32)))
                keep(middle_all, normed2_all)
            if k == 3:
                attn_all = keep(set_heads(attn_all, heads_last, line.slot(last)))
                reduce_down.terms = keep(dot(phase(active), w_down).astype(bf16))
            if k == max(3, n_mp // 2):
                if n_mp == 4:
                    cot_all = keep(place(cot_all, cot_gather.slot(phase, 2), line.slot(2)))
                    d_hidden_all = keep(slope_back(phase(near_active), hidden, 1 - half))
                else:
                    place_near()
                    d_hidden_all = keep(hidden_back(cot_all, hidden, w_down, 1 - half))
            turn()

        reduce_down.step(phase)
        if n_mp == 4:
            edge = (me == 0) | (me == last)
            came = [phase(side[1], side[3]) for side in (cot_gather.left, cot_gather.right)]
            block = jnp.where(line.low, jnp.where(edge, came[1][1], came[1][0]), jnp.where(edge, came[0][1], came[0][0]))
            cot_all = place(cot_all, block, jnp.where(edge, line.slot(3), line.slot(1)))
        else:
            for k in slots:
                cot_all = place(cot_all, cot_gather.slot(phase, k), line.slot(k))
        d_hidden_all = keep(hidden_back(cot_all, hidden, w_down, half, d_hidden_all))
        reduce2.terms = keep(dot(d_hidden_all, w_up, 1, 1).astype(bf16))
        turn()
        for k in slots:
            reduce2.step(phase)
            if k == 1:
                feed_up_grad = keep(weight_grads(factor, phase(normed2_all), d_hidden_all, 2, 0))
            if k == 2:
                feed_full = keep(weight_grads(factor, phase(cot_all), active, 2, 1, feed_up_grad))
            if k == 3:
                grad_feed = lax.psum_scatter(phase(feed_full), "dp", scatter_dimension=0, tiled=True)
                split_sums = keep(factor * total(phase(d_hidden_all)))
            turn()
        own = me[None].astype(jnp.int32)
        reduce_down.step(phase)
        d_middle, d_branch, own_sums = keep(
            *middle_back(own, phase(reduce2.terms), reduce2.came, middle_all, gains[1], cotangent)
        )
        d_attn_own = keep(dot(d_branch, w_out_all, 1, 1).astype(bf16))
        spread_out = Spread("dp", n_dp, after(d_branch, d_attn_own), rows_of(attn_all, me), False, factor)
        keep(spread_out.start(phase))
        turn()
        d_attn_blocks = line.shuffle(phase, d_attn_own)
        spread_out.cross(phase)
        keep(*spread_out.second(phase))
        turn()
        reduce_down.step(phase)
        keep(*spread_out.fly(phase))
        d_attn = line.stack(phase(*d_attn_blocks))
        grad_proj = keep(attend_back(projected, d_attn, seg_col, seg_row, heads))
        reduce1.terms = keep(half_product(grad_proj, flat_qkv, half))
        qkv_full = keep(weight_grads(factor, after(normed1_all, reduce1.terms), grad_proj))
        turn()
        for k in slots:
            reduce1.step(phase)
            if k == 1:
                keep(*spread_out.land(phase))
                keep(*spread_out.fly(phase))
                reduce1.terms = keep(half_product(phase(grad_proj), flat_qkv, 1 - half, reduce1.terms))
                gain1 = gain_sums(reduce1.terms, tokens_all)
                full_sums = keep(factor * jnp.concatenate([gain1, own_sums], axis=0).reshape(-1))
                grad_qkv = lax.psum_scatter(phase(qkv_full), "dp", scatter_dimension=0, tiled=True)
                keep(grad_feed)
            if k == 2:
                out_rows = keep(spread_out.finish(phase))
                heads_sum = [total(phase(grad_proj)[:, :head_cols]), total(grad_proj[:, 2 * head_cols :])]
                split_sums = keep(jnp.concatenate([*[factor * s for s in heads_sum], split_sums]))
                full_sums = phase.early(full_sums)
                phase.send(full_sums)
                full_sums = keep(sum_over(full_sums, "mp", n_mp))
            if k == 3:
                keep(grad_qkv)
                sums = phase(jnp.concatenate([full_sums, split_sums])).reshape(1, 8, -1)
                sums = keep(lax.all_gather(sums, "dp", axis=0, tiled=True))
                for _ in slots[3:]:
                    reduce_down.step(phase)
            turn()
        out_blocks = line.shuffle_rows(phase, out_rows.astype(bf16), head_cols)
        grad_input = input_back(
            own, factor, phase(reduce1.terms), reduce1.came, tokens, gains[0], d_middle
        )
        sums = jnp.sum(sums, axis=0).reshape(-1)
        grad_feed = phase(grad_feed).astype(f32)
        feed_cols = grad_feed.shape[1] // 2
        grad_up, grad_down = grad_feed[:, :feed_cols], grad_feed[:, feed_cols:].T
        down_sum = sum(
            value.astype(f32) for value in (rows_of(phase(reduce_down.terms), me), *reduce_down.came)
        )
        layer_out = (rows_of(middle_all, me) + down_sum + bias_pair[1]).astype(bf16)
        full_sums = sums[: 6 * width].reshape(6, width)
        split_sums = sums[6 * width :]
        own_block = lax.dynamic_slice_in_dim(out_rows, me * head_cols, head_cols, axis=0)
        out_blocks = lax.optimization_barrier((*out_blocks, grad_input, layer_out, grad_up, grad_down))[:-4]
        for block in out_blocks:
            own_block = own_block + block.astype(f32)
        grad_out = own_block
        grad_qkv = phase(grad_qkv).astype(f32)
        return (
            layer_out,
            grad_input,
            jnp.stack([full_sums[0], full_sums[2]]),
            jnp.stack([full_sums[1], full_sums[3]]),
            jnp.stack([grad_qkv[:, j * head_cols : (j + 1) * head_cols] for j in range(3)], axis=1),
            split_sums[: 2 * head_cols].reshape(2, head_cols),
            grad_out,
            full_sums[4:],
            grad_up,
            split_sums[2 * head_cols :],
            grad_down,
        )

    return body


def solution(mesh):
    split = P(("dp", "mp"), None)
    return jax.shard_map(
        make_body(mesh.shape["dp"], mesh.shape["mp"]),
        mesh=mesh,
        in_specs=(
            split, split, P("dp"), P("dp"), P(), P(), P(None, None, "mp"), P(None, "mp"), P("mp", None), P(),
            P(None, "mp"), P("mp"), P("mp", None),
        ),
        out_specs=(
            split, split, P(), P(), P("dp", None, "mp"), P(None, "mp"), P("mp", "dp"), P(), P("dp", "mp"), P("mp"),
            P("mp", "dp"),
        ),
        check_vma=False,
    )
```

```python
import functools
import jax
import jax.numpy as jnp
from jax import lax
from jax.experimental import pallas as pl
from jax.experimental.pallas import tpu as pltpu
from jax.sharding import PartitionSpec as P

HEAD = 128
SEQ = 1024
BLOCK = 256
SCALE = HEAD ** (-0.5)
f32 = jnp.float32
bf16 = jnp.bfloat16
MIB = 2**20
COST = pl.CostEstimate(flops=1 << 20, bytes_accessed=1 << 16, transcendentals=0)


def dot(left, right, left_dim=1, right_dim=0):
    return lax.dot_general(
        left, right, (((left_dim,), (right_dim,)), ((), ())), preferred_element_type=f32
    )


def block_probs(q_block, k_ref, seg_col, seg_row, block, reach):
    start = block * BLOCK
    scores = dot(k_ref[:reach, :], q_block, 1, 1) * SCALE
    key_place = lax.broadcasted_iota(jnp.int32, (reach, BLOCK), 0)
    query_place = start + lax.broadcasted_iota(jnp.int32, (reach, BLOCK), 1)
    allowed = (seg_col[:reach, :] == seg_row[:, start : start + BLOCK]) & (
        key_place <= query_place
    )
    scores = jnp.where(allowed, scores, -1e30)
    expo = jnp.exp(scores - jnp.max(scores, axis=0, keepdims=True))
    return expo * (1.0 / jnp.sum(expo, axis=0, keepdims=True))


def attend_kernel(q_ref, k_ref, v_ref, seg_col, seg_row, out_ref):
    for block in range(SEQ // BLOCK):
        rows = slice(block * BLOCK, (block + 1) * BLOCK)
        reach = (block + 1) * BLOCK
        probs = block_probs(q_ref[rows, :], k_ref, seg_col, seg_row, block, reach)
        out_ref[rows, :] = dot(probs.astype(bf16), v_ref[:reach, :], 0, 0).astype(bf16)


def attend(projected, seg_col, seg_row, heads):
    tokens = projected.shape[0]
    column = lambda part: pl.BlockSpec((SEQ, HEAD), lambda r, h: (r, part * heads + h))
    return pl.pallas_call(
        attend_kernel,
        grid=(tokens // SEQ, heads),
        in_specs=[
            column(0),
            column(1),
            column(2),
            pl.BlockSpec((SEQ, 1), lambda r, h: (r, 0)),
            pl.BlockSpec((1, SEQ), lambda r, h: (0, r)),
        ],
        out_specs=pl.BlockSpec((SEQ, HEAD), lambda r, h: (r, h)),
        out_shape=jax.ShapeDtypeStruct((tokens, heads * HEAD), bf16),
        compiler_params=pltpu.CompilerParams(vmem_limit_bytes=24 * MIB),
        cost_estimate=COST,
        name="attend",
    )(projected, projected, projected, seg_col, seg_row)


def attend_back_kernel(
    heads, q_ref, k_ref, v_ref, grad_ref, seg_col, seg_row, out_ref, dk_ref, dv_ref
):
    head = pl.program_id(1)
    width = heads * HEAD
    column = lambda part: pl.ds(pl.multiple_of(part * width + head * HEAD, HEAD), HEAD)
    dk_ref[...] = jnp.zeros_like(dk_ref)
    dv_ref[...] = jnp.zeros_like(dv_ref)
    for block in range(SEQ // BLOCK):
        rows = slice(block * BLOCK, (block + 1) * BLOCK)
        reach = (block + 1) * BLOCK
        q_block = q_ref[rows, :]
        g_block = grad_ref[rows, :]
        probs = block_probs(q_block, k_ref, seg_col, seg_row, block, reach)
        d_probs = dot(v_ref[:reach, :], g_block, 1, 1)
        delta = jnp.sum(probs * d_probs, axis=0, keepdims=True)
        d_scores = (probs * (d_probs - delta)).astype(bf16)
        dv_ref[:reach, :] += dot(probs.astype(bf16), g_block)
        dk_ref[:reach, :] += dot(d_scores, q_block)
        out_ref[rows, column(0)] = (dot(d_scores, k_ref[:reach, :], 0, 0) * SCALE).astype(bf16)
    out_ref[:, column(1)] = (dk_ref[...] * SCALE).astype(bf16)
    out_ref[:, column(2)] = dv_ref[...].astype(bf16)


def attend_back(projected, grad_attn, seg_col, seg_row, heads):
    tokens = projected.shape[0]
    column = lambda part: pl.BlockSpec((SEQ, HEAD), lambda r, h: (r, part * heads + h))
    return pl.pallas_call(
        functools.partial(attend_back_kernel, heads),
        grid=(tokens // SEQ, heads),
        in_specs=[
            column(0),
            column(1),
            column(2),
            column(0),
            pl.BlockSpec((SEQ, 1), lambda r, h: (r, 0)),
            pl.BlockSpec((1, SEQ), lambda r, h: (0, r)),
        ],
        out_specs=pl.BlockSpec((SEQ, 3 * heads * HEAD), lambda r, h: (r, 0)),
        out_shape=jax.ShapeDtypeStruct((tokens, 3 * heads * HEAD), bf16),
        scratch_shapes=[pltpu.VMEM((SEQ, HEAD), f32), pltpu.VMEM((SEQ, HEAD), f32)],
        compiler_params=pltpu.CompilerParams(vmem_limit_bytes=32 * MIB),
        cost_estimate=COST,
        name="attend_back",
    )(projected, projected, projected, grad_attn, seg_col, seg_row)


def norm_parts(value):
    mean = jnp.mean(value, axis=-1, keepdims=True)
    centered = value - mean
    inverse = lax.rsqrt(jnp.mean(centered * centered, axis=-1, keepdims=True) + 1e-05)
    return centered * inverse, inverse


def norm_backward(grad, gain, scaled, inverse):
    inner = grad * gain
    return inverse * (
        inner
        - jnp.mean(inner, axis=-1, keepdims=True)
        - scaled * jnp.mean(inner * scaled, axis=-1, keepdims=True)
    )


def gelu_parts(value):
    c = 0.7978845608028654
    square = value * value
    tanh = jnp.tanh(c * value * (1.0 + 0.044715 * square))
    half = 0.5 * (1.0 + tanh)
    slope = half + 0.5 * value * (1.0 - tanh * tanh) * c * (1.0 + 3 * 0.044715 * square)
    return value * half, slope


def mix_kernel(index_ref, sum_ref, heads_ref, w_ref, gain_ref, shift_ref, middle_ref, normed_ref):
    middle = sum_ref[...] + dot(heads_ref[...], w_ref[...])
    middle_ref[...] = middle
    normed_ref[...] = (norm_parts(middle)[0] * gain_ref[...] + shift_ref[...]).astype(bf16)


def mix(summed, heads_block, w_out_all, index, gain, shift):
    tokens, width = summed.shape
    cols = heads_block.shape[1]
    step = 256
    row = lambda size: pl.BlockSpec((step, size), lambda i, at: (i, 0))
    one = pl.BlockSpec((1, width), lambda i, at: (0, 0))
    return pl.pallas_call(
        mix_kernel,
        grid_spec=pltpu.PrefetchScalarGridSpec(
            num_scalar_prefetch=1,
            grid=(tokens // step,),
            in_specs=[row(width), row(cols), pl.BlockSpec((cols, width), lambda i, at: (at[0], 0)), one, one],
            out_specs=[row(width), row(width)],
        ),
        out_shape=[
            jax.ShapeDtypeStruct((tokens, width), f32),
            jax.ShapeDtypeStruct((tokens, width), bf16),
        ],
        compiler_params=pltpu.CompilerParams(vmem_limit_bytes=48 * MIB),
        cost_estimate=COST,
        name="mix",
    )(index[None].astype(jnp.int32), summed, heads_block, w_out_all, gain[None], shift[None])


def up_kernel(x_ref, w_ref, b_ref, hidden_ref, active_ref):
    hidden = dot(x_ref[...], w_ref[...]) + b_ref[...]
    hidden_ref[...] = hidden
    active_ref[...] = gelu_parts(hidden)[0].astype(bf16)


def feed_up(normed, w_up, b_up):
    tokens, width = normed.shape
    cols = w_up.shape[1]
    step = 256
    col = lambda rows: pl.BlockSpec((rows, step), lambda i: (0, i))
    return pl.pallas_call(
        up_kernel,
        grid=(cols // step,),
        in_specs=[pl.BlockSpec((tokens, width), lambda i: (0, 0)), col(width), col(1)],
        out_specs=[col(tokens), col(tokens)],
        out_shape=[
            jax.ShapeDtypeStruct((tokens, cols), f32),
            jax.ShapeDtypeStruct((tokens, cols), bf16),
        ],
        compiler_params=pltpu.CompilerParams(vmem_limit_bytes=48 * MIB),
        cost_estimate=COST,
        name="feed_up",
    )(normed, w_up, b_up[None])


def hidden_kernel(index_ref, cot_ref, hidden_ref, w_ref, *refs):
    slope = gelu_parts(hidden_ref[...])[1]
    refs[-1][...] = (dot(cot_ref[...], w_ref[...], 1, 1) * slope).astype(bf16)


def hidden_back(cot_all, hidden, w_down, half, earlier=None):
    tokens, width = cot_all.shape
    rows = tokens // 2
    cols, step = hidden.shape[1], 512
    given = [] if earlier is None else [earlier]
    return pl.pallas_call(
        hidden_kernel,
        grid_spec=pltpu.PrefetchScalarGridSpec(
            num_scalar_prefetch=1,
            grid=(cols // step,),
            in_specs=[
                pl.BlockSpec((rows, width), lambda i, at: (at[0], 0)),
                pl.BlockSpec((rows, step), lambda i, at: (at[0], i)),
                pl.BlockSpec((step, width), lambda i, at: (i, 0)),
                *[pl.BlockSpec(memory_space=pl.ANY) for _ in given],
            ],
            out_specs=pl.BlockSpec((rows, step), lambda i, at: (at[0], i)),
        ),
        out_shape=jax.ShapeDtypeStruct((tokens, cols), bf16),
        input_output_aliases={4: 0} if given else {},
        compiler_params=pltpu.CompilerParams(vmem_limit_bytes=20 * MIB),
        cost_estimate=COST,
        name="hidden_back",
    )(half[None], cot_all, hidden, w_down, *given)


def slope_kernel(index_ref, grad_ref, hidden_ref, out_ref):
    out_ref[...] = (grad_ref[...] * gelu_parts(hidden_ref[...])[1]).astype(bf16)


def slope_back(d_active, hidden, half):
    tokens, cols = hidden.shape
    step = 64
    steps = tokens // 2 // step
    place = pl.BlockSpec((step, cols), lambda i, at: (at[0] * steps + i, 0))
    return pl.pallas_call(
        slope_kernel,
        grid_spec=pltpu.PrefetchScalarGridSpec(
            num_scalar_prefetch=1,
            grid=(steps,),
            in_specs=[pl.BlockSpec((step, cols), lambda i, at: (i, 0)), place],
            out_specs=place,
        ),
        out_shape=jax.ShapeDtypeStruct((tokens, cols), bf16),
        compiler_params=pltpu.CompilerParams(vmem_limit_bytes=12 * MIB),
        cost_estimate=COST,
        name="slope_back",
    )(half[None], d_active, hidden)


def grads_kernel(factor_ref, left_ref, right_ref, *refs):
    out_ref, turned_ref = refs[-2:]

    @pl.when(pl.program_id(0) == 0)
    def _():
        turned_ref[...] = left_ref[...].T

    out_ref[...] = (factor_ref[0] * dot(turned_ref[...], right_ref[...])).astype(bf16)


def weight_grads(factor, left, right, parts=1, part=0, earlier=None):
    tokens, width = left.shape
    cols, step = right.shape[1], 256
    steps = cols // step
    given = [] if earlier is None else [earlier]
    return pl.pallas_call(
        grads_kernel,
        grid=(steps,),
        in_specs=[
            pl.BlockSpec(memory_space=pltpu.SMEM),
            pl.BlockSpec((tokens, width), lambda i: (0, 0)),
            pl.BlockSpec((tokens, step), lambda i: (0, i)),
            *[pl.BlockSpec(memory_space=pl.ANY) for _ in given],
        ],
        out_specs=pl.BlockSpec((width, step), lambda i: (0, part * steps + i)),
        out_shape=jax.ShapeDtypeStruct((width, parts * cols), bf16),
        input_output_aliases={3: 0} if given else {},
        scratch_shapes=[pltpu.VMEM((width, tokens), bf16)],
        compiler_params=pltpu.CompilerParams(vmem_limit_bytes=48 * MIB),
        cost_estimate=COST,
        name="weight_grads",
    )(factor[None], left, right, *given)


def half_kernel(index_ref, x_ref, w_ref, *refs):
    refs[-1][...] = dot(x_ref[...], w_ref[...], 1, 1).astype(bf16)


def half_product(x, weight, half, earlier=None):
    tokens, depth = x.shape
    rows = tokens // 2
    cols, step = weight.shape[0], 512
    given = [] if earlier is None else [earlier]
    return pl.pallas_call(
        half_kernel,
        grid_spec=pltpu.PrefetchScalarGridSpec(
            num_scalar_prefetch=1,
            grid=(cols // step,),
            in_specs=[
                pl.BlockSpec((rows, depth), lambda i, at: (at[0], 0)),
                pl.BlockSpec((step, depth), lambda i, at: (i, 0)),
                *[pl.BlockSpec(memory_space=pl.ANY) for _ in given],
            ],
            out_specs=pl.BlockSpec((rows, step), lambda i, at: (at[0], i)),
        ),
        out_shape=jax.ShapeDtypeStruct((tokens, cols), bf16),
        input_output_aliases={3: 0} if given else {},
        compiler_params=pltpu.CompilerParams(vmem_limit_bytes=40 * MIB),
        cost_estimate=COST,
        name="half_product",
    )(half[None], x, weight, *given)


def relay_kernel(index_ref, right_ref, left_ref, *refs):
    to_right, to_left = refs[-2:]
    if len(refs) == 2:
        to_right[...], to_left[...] = right_ref[...], left_ref[...]
    else:
        to_right[...] = (right_ref[...].astype(f32) + refs[0][...].astype(f32)).astype(bf16)
        to_left[...] = (left_ref[...].astype(f32) + refs[1][...].astype(f32)).astype(bf16)


def relay(terms, rows, index, came):
    width = terms.shape[1]
    step = min(rows, 128)
    steps = rows // step
    block = pl.BlockSpec((step, width), lambda i, at: (i, 0))
    return pl.pallas_call(
        relay_kernel,
        grid_spec=pltpu.PrefetchScalarGridSpec(
            num_scalar_prefetch=1,
            grid=(steps,),
            in_specs=[
                pl.BlockSpec((step, width), lambda i, at: (at[0] * steps + i, 0)),
                pl.BlockSpec((step, width), lambda i, at: (at[1] * steps + i, 0)),
                *[block] * len(came),
            ],
            out_specs=[block, block],
        ),
        out_shape=[jax.ShapeDtypeStruct((rows, width), bf16)] * 2,
        compiler_params=pltpu.CompilerParams(vmem_limit_bytes=12 * MIB),
        cost_estimate=COST,
        name="relay",
    )(index, terms, terms, *came)


def summed_back(term_ref, left_ref, right_ref, value_ref, gain_ref):
    grad = term_ref[...].astype(f32) + left_ref[...].astype(f32) + right_ref[...].astype(f32)
    scaled, inverse = norm_parts(value_ref[...].astype(f32))
    return grad, scaled, norm_backward(grad, gain_ref[...], scaled, inverse)


def middle_back_kernel(
    index_ref, term_ref, left_ref, right_ref, value_ref, gain_ref, cot_ref, middle_ref, branch_ref, sums_ref
):
    @pl.when(pl.program_id(0) == 0)
    def _():
        sums_ref[...] = jnp.zeros_like(sums_ref)

    grad, scaled, back = summed_back(term_ref, left_ref, right_ref, value_ref, gain_ref)
    cot = cot_ref[...].astype(f32)
    middle = cot + back
    branch = middle.astype(bf16)
    middle_ref[...], branch_ref[...] = middle, branch
    for row, value in enumerate((grad * scaled, grad, branch.astype(f32), cot)):
        sums_ref[row : row + 1, :] += jnp.sum(value, axis=0, keepdims=True)


def input_back_kernel(
    index_ref, factor_ref, term_ref, left_ref, right_ref, value_ref, gain_ref, middle_ref, out_ref
):
    back = summed_back(term_ref, left_ref, right_ref, value_ref, gain_ref)[2]
    out_ref[...] = factor_ref[0] * (middle_ref[...] + back)


def back_specs(rows, width):
    step = min(rows, 128)
    steps = rows // step
    here = pl.BlockSpec((step, width), lambda i, at: (i, 0))
    own = pl.BlockSpec((step, width), lambda i, at: (at[0] * steps + i, 0))
    return steps, here, own, pl.BlockSpec((1, width), lambda i, at: (0, 0))


def middle_back(index, terms, came, middle_all, gain, cot):
    rows, width = cot.shape
    steps, here, own, one = back_specs(rows, width)
    return pl.pallas_call(
        middle_back_kernel,
        grid_spec=pltpu.PrefetchScalarGridSpec(
            num_scalar_prefetch=1,
            grid=(steps,),
            in_specs=[own, here, here, own, one, here],
            out_specs=[here, here, pl.BlockSpec((4, width), lambda i, at: (0, 0))],
        ),
        out_shape=[
            jax.ShapeDtypeStruct((rows, width), f32),
            jax.ShapeDtypeStruct((rows, width), bf16),
            jax.ShapeDtypeStruct((4, width), f32),
        ],
        compiler_params=pltpu.CompilerParams(vmem_limit_bytes=48 * MIB),
        cost_estimate=COST,
        name="middle_back",
    )(index, terms, *came, middle_all, gain[None], cot)


def input_back(index, factor, terms, came, tokens, gain, d_middle):
    rows, width = tokens.shape
    steps, here, own, one = back_specs(rows, width)
    return pl.pallas_call(
        input_back_kernel,
        grid_spec=pltpu.PrefetchScalarGridSpec(
            num_scalar_prefetch=1,
            grid=(steps,),
            in_specs=[pl.BlockSpec(memory_space=pltpu.SMEM), own, here, here, here, one, here],
            out_specs=here,
        ),
        out_shape=jax.ShapeDtypeStruct((rows, width), f32),
        compiler_params=pltpu.CompilerParams(vmem_limit_bytes=48 * MIB),
        cost_estimate=COST,
        name="input_back",
    )(index, factor[None], terms, *came, tokens, gain[None], d_middle)


def present_kernel(qkv_ref, up_ref, down_ref, qkv_out, up_out, down_out):
    cols = qkv_out.shape[2]
    for j in range(3):
        qkv_out[j] = qkv_ref[:, j * cols : (j + 1) * cols].astype(f32)
    up_out[...] = up_ref[...].astype(f32)
    down_out[...] = down_ref[...].astype(f32).T


def present(qkv, up, down):
    rows, cols = up.shape
    head_cols = qkv.shape[1] // 3
    step = min(rows, 128)
    row = lambda size: pl.BlockSpec((step, size), lambda i: (i, 0))
    return pl.pallas_call(
        present_kernel,
        grid=(rows // step,),
        in_specs=[row(3 * head_cols), row(cols), row(cols)],
        out_specs=[
            pl.BlockSpec((3, step, head_cols), lambda i: (0, i, 0)),
            row(cols),
            pl.BlockSpec((cols, step), lambda i: (0, i)),
        ],
        out_shape=[
            jax.ShapeDtypeStruct((3, rows, head_cols), f32),
            jax.ShapeDtypeStruct((rows, cols), f32),
            jax.ShapeDtypeStruct((cols, rows), f32),
        ],
        compiler_params=pltpu.CompilerParams(vmem_limit_bytes=48 * MIB),
        cost_estimate=COST,
        name="present",
    )(qkv, up, down)


def blank_kernel(out_ref):
    pass


def blank(shape):
    return pl.pallas_call(
        blank_kernel,
        out_specs=pl.BlockSpec(memory_space=pl.ANY),
        out_shape=jax.ShapeDtypeStruct(shape, bf16),
        name="blank",
    )()


def sums_kernel(term_ref, token_ref, out_ref):
    @pl.when(pl.program_id(0) == 0)
    def _():
        out_ref[...] = jnp.zeros_like(out_ref)

    term = term_ref[...].astype(f32)
    scaled = norm_parts(token_ref[...].astype(f32))[0]
    out_ref[0:1, :] += jnp.sum(term * scaled, axis=0, keepdims=True)
    out_ref[1:2, :] += jnp.sum(term, axis=0, keepdims=True)


def gain_sums(terms, tokens_all):
    rows, width = terms.shape
    block = pl.BlockSpec((128, width), lambda i: (i, 0))
    return pl.pallas_call(
        sums_kernel,
        grid=(rows // 128,),
        in_specs=[block, block],
        out_specs=pl.BlockSpec((2, width), lambda i: (0, 0)),
        out_shape=jax.ShapeDtypeStruct((2, width), f32),
        compiler_params=pltpu.CompilerParams(vmem_limit_bytes=12 * MIB),
        cost_estimate=COST,
        name="gain_sums",
    )(terms, tokens_all)


class Phases:
    def __init__(self):
        self.marks, self.kept, self.sends = (), [], []

    def __call__(self, *values):
        gate = (*self.marks, *self.sends)
        if gate:
            values = lax.optimization_barrier((*values, *gate))[: len(values)]
        return values if len(values) > 1 else values[0]

    def early(self, *values):
        if self.marks:
            values = lax.optimization_barrier((*values, *self.marks))[: len(values)]
        return values if len(values) > 1 else values[0]

    def send(self, *values):
        self.sends += values

    def keep(self, *values):
        self.kept += values
        return values if len(values) > 1 else values[0]

    def turn(self):
        self.marks, self.kept, self.sends = tuple(self.kept), [], []


class Line:
    def __init__(self, name, size):
        self.name, self.n = name, size
        self.me = lax.axis_index(name)
        self.low = self.me < size // 2

    def slot(self, k):
        n = self.n
        return jnp.where(self.low, (self.me + k) % n, (self.me + n - k) % n)

    def shuffle(self, phase, array):
        n = self.n
        cols = array.shape[1] // n
        out = []
        for shift in range(n):
            target = (self.me + shift) % n
            block = lax.dynamic_slice_in_dim(phase.early(array), target * cols, cols, axis=1)
            if shift:
                phase.send(block)
                block = lax.ppermute(block, self.name, [(j, (j + shift) % n) for j in range(n)])
            out.append(phase.keep(block))
        return out

    def shuffle_rows(self, phase, array, rows):
        n = self.n
        out = []
        for shift in range(1, n):
            target = (self.me + shift) % n
            block = lax.dynamic_slice_in_dim(phase.early(array), target * rows, rows, axis=0)
            phase.send(block)
            out.append(lax.ppermute(block, self.name, [(j, (j + shift) % n) for j in range(n)]))
        return out

    def stack(self, blocks):
        n = self.n
        rows, cols = blocks[0].shape
        out = blank((n * rows, cols))
        for shift, block in enumerate(blocks):
            source = (self.me + n - shift) % n
            out = lax.dynamic_update_slice_in_dim(out, block, source * rows, axis=0)
        return out


class Gather:
    def __init__(self, line, block):
        self.line, self.left, self.right, self.slots = line, [block], [block], {0: block}

    def step(self, phase):
        line, n, k = self.line, self.line.n, len(self.left)
        left, right = phase.early(self.left[-1], self.right[-1])
        phase.send(left, right)
        self.left.append(lax.ppermute(left, line.name, [(j, j + 1) for j in range(k - 1, n - 1)]))
        self.right.append(lax.ppermute(right, line.name, [(j, j - 1) for j in range(1, n - k + 1)]))
        phase.keep(self.left[k], self.right[k])

    def slot(self, phase, k):
        if k not in self.slots:
            line, n = self.line, self.line.n
            if 2 * k < n:
                left, right = phase(self.left[k], self.right[k])
                value = jnp.where(line.low, right, left)
            else:
                left, right, left_far, right_far = phase(
                    self.left[n - k], self.right[n - k], self.left[k], self.right[k]
                )
                low_side = jnp.where(line.me + k < n, right_far, left)
                high_side = jnp.where(line.me >= k, left_far, right)
                value = jnp.where(line.low, low_side, high_side)
            self.slots[k] = value
        return self.slots[k]


class Reduce:
    def __init__(self, line, rows):
        self.line, self.rows, self.k, self.came, self.terms = line, rows, 1, (), None

    def step(self, phase):
        line, n, k = self.line, self.line.n, self.k
        blocks = [jnp.clip(line.me + n - k, 0, n - 1), jnp.clip(line.me - n + k, 0, n - 1)]
        self.terms = phase.early(self.terms)
        sent = relay(self.terms, self.rows, jnp.stack(blocks).astype(jnp.int32), self.came)
        phase.send(*sent)
        self.came = (
            lax.ppermute(sent[0], line.name, [(j, j + 1) for j in range(k)]),
            lax.ppermute(sent[1], line.name, [(j, j - 1) for j in range(n - k, n)]),
        )
        phase.keep(*self.came)
        self.k += 1


def flip(value, name, size, bit):
    return lax.ppermute(value, name, [(j, j ^ bit) for j in range(size)])


def sum_over(value, name, size, bit=1):
    while bit < size:
        value = value + flip(value, name, size, bit)
        bit *= 2
    return value


class Spread:
    def __init__(self, name, size, moved, still, moved_left, factor):
        self.name, self.size, self.factor, self.moved_left = name, size, factor, moved_left
        self.moved, self.still = moved, still
        self.bits = [1 << b for b in range(1, size.bit_length() - 1)]
        self.orders = [self.bits, self.bits[::-1]]
        self.block_cols = moved.shape[1] // size

    def blocks(self, moved, wanted):
        cols, index = self.block_cols, lax.axis_index(self.name)
        return jnp.concatenate(
            [lax.dynamic_slice_in_dim(moved, (index ^ r) * cols, cols, axis=1) for r in wanted], axis=1
        )

    def product(self, moved, still):
        left, right = (moved, still) if self.moved_left else (still, moved)
        return self.factor * dot(left, right, 0, 0)

    def listed(self, order, fixed):
        out = [sum(bit for bit, on in fixed.items() if on)]
        for bit in order[::-1]:
            if bit not in fixed:
                out = [*out, *[r + bit for r in out]]
        return out

    def cut(self, array, low, high):
        return array[low:high] if self.moved_left else array[:, low:high]

    def start(self, phase):
        moved = phase(self.moved)
        self.sent = self.product(self.blocks(moved, self.listed(self.bits, {1: True})), self.still).astype(bf16)
        return self.sent

    def cross(self, phase):
        sent = phase.early(self.sent)
        phase.send(sent)
        self.brought = flip(sent, self.name, self.size, 1)
        return self.brought

    def second(self, phase):
        moved, brought = phase(self.moved, self.brought)
        cols, along = self.block_cols, 0 if self.moved_left else 1
        half = self.still.shape[1] // 2
        first_list = self.listed(self.bits, {1: True})
        self.sent, self.kept = [], []
        for which, order in enumerate(self.orders):
            still = self.still[:, which * half : (which + 1) * half]
            part = lax.slice_in_dim(brought, which * half, (which + 1) * half, axis=1 - along)
            for on in (True, False):
                wanted = self.listed(order, {1: False, order[0]: on})
                places = [first_list.index(r + 1) for r in wanted]
                added = jnp.concatenate(
                    [self.cut(part, p * cols, (p + 1) * cols) for p in places], axis=along
                )
                value = (self.product(self.blocks(moved, wanted), still) + added.astype(f32)).astype(bf16)
                (self.sent if on else self.kept).append(value)
        self.done, self.air, self.result = 0, False, None
        return (*self.sent, *self.kept)

    def fly(self, phase):
        sent = phase.early(*self.sent)
        phase.send(*sent)
        self.flying = tuple(
            flip(value, self.name, self.size, order[self.done]) for value, order in zip(sent, self.orders)
        )
        self.done, self.air = self.done + 1, True
        return self.flying

    def land(self, phase):
        along, self.air = 0 if self.moved_left else 1, False
        flying = phase(*self.flying)
        totals = [k.astype(f32) + f.astype(f32) for k, f in zip(self.kept, flying)]
        if self.done == len(self.bits):
            self.result = jnp.concatenate(totals, axis=1 - along)
            return (self.result,)
        size = totals[0].shape[along]
        self.sent = [self.cut(t, size // 2, size).astype(bf16) for t in totals]
        self.kept = [self.cut(t, 0, size // 2).astype(bf16) for t in totals]
        return (*self.sent, *self.kept)

    def finish(self, phase):
        while self.result is None:
            (self.land if self.air else self.fly)(phase)
        return self.result


def after(value, *earlier):
    return lax.optimization_barrier((value, *earlier))[0]


def make_body(n_dp, n_mp):
    def body(
        tokens, cotangent, segment, counts, ln_gain, ln_bias, w_qkv, b_qv, w_out, out_bias, w_up, b_up, w_down
    ):
        line, phase = Line("mp", n_mp), Phases()
        keep, turn = phase.keep, phase.turn
        gains, shifts, bias_pair = ln_gain.astype(f32), ln_bias.astype(f32), out_bias.astype(f32)
        share, width = tokens.shape
        head_cols = w_qkv.shape[2]
        heads = head_cols // HEAD
        group = segment.shape[0]
        seg_col, seg_row = segment[:, None], segment[None, :]
        me = line.me
        place = lambda whole, block, index: lax.dynamic_update_slice_in_dim(
            whole, block, index * share, axis=0
        )
        rows_of = lambda whole, index: lax.dynamic_slice_in_dim(whole, index * share, share, axis=0)
        total = lambda value: jnp.sum(value.astype(f32), axis=0)
        slots, last = range(1, n_mp), n_mp - 1

        flat_qkv = jnp.concatenate([w_qkv[:, j] for j in range(3)], axis=1)
        bias_rows = (
            jnp.stack([b_qv[0], jnp.zeros_like(b_qv[0]), b_qv[1]]).astype(f32).reshape(3 * head_cols)
        )
        state = [blank((group, width)), blank((group, width)), blank((group, 3 * head_cols))]

        def project(k):
            block = phase(gather.slot(phase, k))
            normed = (norm_parts(block.astype(f32))[0] * gains[0] + shifts[0]).astype(bf16)
            proj = (dot(normed, flat_qkv) + bias_rows).astype(bf16)
            for j, value in enumerate((block, normed, proj)):
                state[j] = keep(place(state[j], value, line.slot(k)))

        slice_rows = w_out.shape[0] // n_dp
        w_slice = lax.dynamic_slice_in_dim(
            w_out, lax.axis_index("dp") * slice_rows, slice_rows, axis=0
        )

        gather = Gather(line, tokens)
        for k in slots:
            gather.step(phase)
            if k == 2:
                w_slices = lax.all_gather(phase(w_slice), "mp", axis=0)
            project(k - 1)
            turn()
        cot_gather = Gather(line, cotangent)
        cot_gather.step(phase)
        w_out_all = lax.all_gather(phase(w_slices), "dp", axis=1).reshape(n_mp * w_out.shape[0], width)
        project(last)
        tokens_all, normed1_all, projected = state
        attn = keep(attend(projected, seg_col, seg_row, heads))
        turn()

        set_heads = lambda whole, block, index: lax.dynamic_update_slice_in_dim(
            whole, block, index * head_cols, axis=1
        )
        w_rows = lambda k: lax.dynamic_slice_in_dim(w_out_all, line.slot(k) * head_cols, head_cols, axis=0)
        half = line.low.astype(jnp.int32)
        attn_all = blank((group, n_mp * head_cols))
        cot_all = place(blank((group, width)), phase(cotangent), me)

        def place_near():
            nonlocal cot_all
            for j in range(1, n_mp // 2):
                for came, index in ((cot_gather.left[j], me - j), (cot_gather.right[j], me + j)):
                    here = (index >= 0) & (index < n_mp) & ((index < n_mp // 2) == line.low)
                    came = phase(came)
                    cot_all = place(cot_all, jnp.where(here, came, cotangent), jnp.where(here, index, me))
            cot_all = keep(phase(cot_all))

        attn_gather = Gather(line, attn)
        for k in slots:
            attn_gather.step(phase)
            attn_all = keep(set_heads(attn_all, phase(attn_gather.slot(phase, k - 1)), line.slot(k - 1)))
            if k == 1:
                middle_sum = keep(tokens_all.astype(f32) + bias_pair[0] + dot(phase(attn), w_out))
                count_here = phase(counts.astype(f32))
                factor = keep((count_here / sum_over(count_here, "dp", n_dp))[0])
            if k == 2 and n_mp == 4:
                place_near()
                near_rows = lax.dynamic_slice_in_dim(cot_all, (1 - half) * (group // 2), group // 2, axis=0)
                near_active = keep(dot(near_rows, w_down, 1, 1))
            if k == last:
                for j in range(1, last):
                    middle_sum = keep(middle_sum + dot(phase(attn_gather.slot(phase, j)), w_rows(j)))
            turn()
        reduce_down, reduce2, reduce1 = (Reduce(line, share) for _ in range(3))
        for k in slots[1:]:
            cot_gather.step(phase)
            if k == 2:
                heads_last = attn_gather.slot(phase, last)
                middle_all, normed2_all = mix(
                    middle_sum, heads_last, w_out_all, line.slot(last), gains[1], shifts[1]
                )
                hidden, active = keep(*feed_up(normed2_all, w_up, b_up.astype(f32)))
                keep(middle_all, normed2_all)
            if k == 3:
                attn_all = keep(set_heads(attn_all, phase(heads_last), line.slot(last)))
                reduce_down.terms = keep(dot(phase(active), w_down).astype(bf16))
            if k == max(3, n_mp // 2):
                if n_mp == 4:
                    cot_all = keep(place(cot_all, cot_gather.slot(phase, 2), line.slot(2)))
                    d_hidden_all = keep(slope_back(phase(near_active), hidden, 1 - half))
                else:
                    place_near()
                    d_hidden_all = keep(hidden_back(cot_all, hidden, w_down, 1 - half))
            turn()

        scatter = lambda full: lax.psum_scatter(phase(full), "dp", scatter_dimension=0, tiled=True)

        reduce_down.step(phase)
        if n_mp == 4:
            edge = (me == 0) | (me == last)
            came = [phase(side[1], side[3]) for side in (cot_gather.left, cot_gather.right)]
            block = jnp.where(line.low, jnp.where(edge, came[1][1], came[1][0]), jnp.where(edge, came[0][1], came[0][0]))
            cot_all = place(cot_all, block, jnp.where(edge, line.slot(3), line.slot(1)))
        else:
            for k in slots:
                cot_all = place(cot_all, cot_gather.slot(phase, k), line.slot(k))
        d_hidden_all = keep(hidden_back(cot_all, hidden, w_down, half, d_hidden_all))
        reduce2.terms = keep(dot(d_hidden_all, w_up, 1, 1).astype(bf16))
        turn()
        for k in slots:
            reduce2.step(phase)
            if k == 1:
                up_full = keep(weight_grads(factor, phase(normed2_all), d_hidden_all))
            if k == 2:
                grad_up = scatter(up_full)
                down_full = keep(weight_grads(factor, phase(cot_all), active))
            if k == 3:
                grad_down = scatter(down_full)
                split_sums = keep(factor * total(phase(d_hidden_all)))
            turn()
        own = me[None].astype(jnp.int32)
        reduce_down.step(phase)
        d_middle, d_branch, own_sums = keep(
            *middle_back(own, phase(reduce2.terms), reduce2.came, middle_all, gains[1], cotangent)
        )
        d_attn_own = keep(dot(d_branch, w_out_all, 1, 1).astype(bf16))
        spread_out = Spread("dp", n_dp, after(d_branch, d_attn_own), rows_of(attn_all, me), False, factor)
        keep(spread_out.start(phase))
        turn()
        d_attn_blocks = line.shuffle(phase, d_attn_own)
        spread_out.cross(phase)
        keep(*spread_out.second(phase))
        keep(grad_up)
        turn()
        reduce_down.step(phase)
        d_attn = line.stack(phase(*d_attn_blocks))
        grad_proj = keep(attend_back(projected, d_attn, seg_col, seg_row, heads))
        reduce1.terms = keep(half_product(grad_proj, flat_qkv, half))
        turn()
        for k in slots:
            reduce1.step(phase)
            if k == 1:
                keep(*spread_out.fly(phase))
                reduce1.terms = keep(half_product(phase(grad_proj), flat_qkv, 1 - half, reduce1.terms))
                gain1 = gain_sums(reduce1.terms, tokens_all)
                full_sums = factor * jnp.concatenate([gain1, own_sums], axis=0).reshape(-1)
                full_sums = keep(full_sums + keep(flip(full_sums, "mp", n_mp, 1)))
                qkv_full = keep(weight_grads(factor, after(normed1_all, gain1), grad_proj))
                keep(grad_down)
            if k == 2:
                grad_qkv = scatter(qkv_full)
                keep(*spread_out.land(phase))
                heads_sum = [total(phase(grad_proj)[:, :head_cols]), total(grad_proj[:, 2 * head_cols :])]
                split_sums = keep(jnp.concatenate([*[factor * s for s in heads_sum], split_sums]))
            if k == 3:
                keep(*spread_out.fly(phase))
                for _ in slots[3:]:
                    reduce_down.step(phase)
                down_sum = sum(
                    value.astype(f32)
                    for value in (rows_of(phase(reduce_down.terms), me), *reduce_down.came)
                )
                layer_out = keep((rows_of(middle_all, me) + down_sum + bias_pair[1]).astype(bf16))
                full_sums = keep(sum_over(phase(full_sums), "mp", n_mp, 2))
            turn()
        out_rows = spread_out.finish(phase)
        out_blocks = line.shuffle_rows(phase, out_rows.astype(bf16), head_cols)
        grad_input = input_back(
            own, factor, phase(reduce1.terms), reduce1.came, tokens, gains[0], d_middle
        )
        grad_qkv, grad_up, grad_down = present(*phase(grad_qkv, grad_up, grad_down))
        sums = after(jnp.concatenate([full_sums, split_sums]), grad_input).reshape(1, 8, -1)
        sums = lax.all_gather(sums, "dp", axis=0, tiled=True)
        sums, grad_qkv, *out_blocks = lax.optimization_barrier((sums, grad_qkv, *out_blocks))
        grad_out = lax.dynamic_slice_in_dim(out_rows, me * head_cols, head_cols, axis=0)
        for block in out_blocks:
            grad_out = grad_out + block.astype(f32)
        sums = jnp.sum(sums, axis=0).reshape(-1)
        full_sums = sums[: 6 * width].reshape(6, width)
        split_sums = sums[6 * width :]
        return (
            layer_out,
            grad_input,
            jnp.stack([full_sums[0], full_sums[2]]),
            jnp.stack([full_sums[1], full_sums[3]]),
            grad_qkv.transpose(1, 0, 2),
            split_sums[: 2 * head_cols].reshape(2, head_cols),
            grad_out,
            full_sums[4:],
            grad_up,
            split_sums[2 * head_cols :],
            grad_down,
        )

    return body


def solution(mesh):
    split = P(("dp", "mp"), None)
    return jax.shard_map(
        make_body(mesh.shape["dp"], mesh.shape["mp"]),
        mesh=mesh,
        in_specs=(
            split, split, P("dp"), P("dp"), P(), P(), P(None, None, "mp"), P(None, "mp"), P("mp", None), P(),
            P(None, "mp"), P("mp"), P("mp", None),
        ),
        out_specs=(
            split, split, P(), P(), P("dp", None, "mp"), P(None, "mp"), P("mp", "dp"), P(), P("dp", "mp"), P("mp"),
            P("mp", "dp"),
        ),
        check_vma=False,
    )
```

```python
import functools
import jax
import jax.numpy as jnp
from jax import lax
from jax.experimental import pallas as pl
from jax.experimental.pallas import tpu as pltpu
from jax.sharding import PartitionSpec as P

HEAD = 128
SEQ = 1024
BLOCK = 256
SCALE = HEAD ** (-0.5)
f32 = jnp.float32
bf16 = jnp.bfloat16
MIB = 2**20
COST = pl.CostEstimate(flops=1 << 20, bytes_accessed=1 << 16, transcendentals=0)


def dot(left, right, left_dim=1, right_dim=0):
    return lax.dot_general(
        left, right, (((left_dim,), (right_dim,)), ((), ())), preferred_element_type=f32
    )


def block_probs(q_block, k_ref, seg_col, seg_row, block, reach):
    start = block * BLOCK
    scores = dot(k_ref[:reach, :], q_block, 1, 1) * SCALE
    key_place = lax.broadcasted_iota(jnp.int32, (reach, BLOCK), 0)
    query_place = start + lax.broadcasted_iota(jnp.int32, (reach, BLOCK), 1)
    allowed = (seg_col[:reach, :] == seg_row[:, start : start + BLOCK]) & (
        key_place <= query_place
    )
    scores = jnp.where(allowed, scores, -1e30)
    expo = jnp.exp(scores - jnp.max(scores, axis=0, keepdims=True))
    return expo * (1.0 / jnp.sum(expo, axis=0, keepdims=True))


def attend_kernel(q_ref, k_ref, v_ref, seg_col, seg_row, out_ref):
    for block in range(SEQ // BLOCK):
        rows = slice(block * BLOCK, (block + 1) * BLOCK)
        reach = (block + 1) * BLOCK
        probs = block_probs(q_ref[rows, :], k_ref, seg_col, seg_row, block, reach)
        out_ref[rows, :] = dot(probs.astype(bf16), v_ref[:reach, :], 0, 0).astype(bf16)


def attend(projected, seg_col, seg_row, heads):
    tokens = projected.shape[0]
    column = lambda part: pl.BlockSpec((SEQ, HEAD), lambda r, h: (r, part * heads + h))
    return pl.pallas_call(
        attend_kernel,
        grid=(tokens // SEQ, heads),
        in_specs=[
            column(0),
            column(1),
            column(2),
            pl.BlockSpec((SEQ, 1), lambda r, h: (r, 0)),
            pl.BlockSpec((1, SEQ), lambda r, h: (0, r)),
        ],
        out_specs=pl.BlockSpec((SEQ, HEAD), lambda r, h: (r, h)),
        out_shape=jax.ShapeDtypeStruct((tokens, heads * HEAD), bf16),
        compiler_params=pltpu.CompilerParams(vmem_limit_bytes=24 * MIB),
        cost_estimate=COST,
        name="attend",
    )(projected, projected, projected, seg_col, seg_row)


def attend_back_kernel(
    heads, q_ref, k_ref, v_ref, grad_ref, seg_col, seg_row, out_ref, dk_ref, dv_ref
):
    head = pl.program_id(1)
    width = heads * HEAD
    column = lambda part: pl.ds(pl.multiple_of(part * width + head * HEAD, HEAD), HEAD)
    dk_ref[...] = jnp.zeros_like(dk_ref)
    dv_ref[...] = jnp.zeros_like(dv_ref)
    for block in range(SEQ // BLOCK):
        rows = slice(block * BLOCK, (block + 1) * BLOCK)
        reach = (block + 1) * BLOCK
        q_block = q_ref[rows, :]
        g_block = grad_ref[rows, :]
        probs = block_probs(q_block, k_ref, seg_col, seg_row, block, reach)
        d_probs = dot(v_ref[:reach, :], g_block, 1, 1)
        delta = jnp.sum(probs * d_probs, axis=0, keepdims=True)
        d_scores = (probs * (d_probs - delta)).astype(bf16)
        dv_ref[:reach, :] += dot(probs.astype(bf16), g_block)
        dk_ref[:reach, :] += dot(d_scores, q_block)
        out_ref[rows, column(0)] = (dot(d_scores, k_ref[:reach, :], 0, 0) * SCALE).astype(bf16)
    out_ref[:, column(1)] = (dk_ref[...] * SCALE).astype(bf16)
    out_ref[:, column(2)] = dv_ref[...].astype(bf16)


def attend_back(projected, grad_attn, seg_col, seg_row, heads):
    tokens = projected.shape[0]
    column = lambda part: pl.BlockSpec((SEQ, HEAD), lambda r, h: (r, part * heads + h))
    return pl.pallas_call(
        functools.partial(attend_back_kernel, heads),
        grid=(tokens // SEQ, heads),
        in_specs=[
            column(0),
            column(1),
            column(2),
            column(0),
            pl.BlockSpec((SEQ, 1), lambda r, h: (r, 0)),
            pl.BlockSpec((1, SEQ), lambda r, h: (0, r)),
        ],
        out_specs=pl.BlockSpec((SEQ, 3 * heads * HEAD), lambda r, h: (r, 0)),
        out_shape=jax.ShapeDtypeStruct((tokens, 3 * heads * HEAD), bf16),
        scratch_shapes=[pltpu.VMEM((SEQ, HEAD), f32), pltpu.VMEM((SEQ, HEAD), f32)],
        compiler_params=pltpu.CompilerParams(vmem_limit_bytes=32 * MIB),
        cost_estimate=COST,
        name="attend_back",
    )(projected, projected, projected, grad_attn, seg_col, seg_row)


def norm_parts(value):
    mean = jnp.mean(value, axis=-1, keepdims=True)
    centered = value - mean
    inverse = lax.rsqrt(jnp.mean(centered * centered, axis=-1, keepdims=True) + 1e-05)
    return centered * inverse, inverse


def norm_backward(grad, gain, scaled, inverse):
    inner = grad * gain
    return inverse * (
        inner
        - jnp.mean(inner, axis=-1, keepdims=True)
        - scaled * jnp.mean(inner * scaled, axis=-1, keepdims=True)
    )


def gelu_parts(value):
    c = 0.7978845608028654
    square = value * value
    tanh = jnp.tanh(c * value * (1.0 + 0.044715 * square))
    half = 0.5 * (1.0 + tanh)
    slope = half + 0.5 * value * (1.0 - tanh * tanh) * c * (1.0 + 3 * 0.044715 * square)
    return value * half, slope


def mix_kernel(index_ref, sum_ref, heads_ref, w_ref, gain_ref, shift_ref, middle_ref, normed_ref):
    middle = sum_ref[...] + dot(heads_ref[...], w_ref[...])
    middle_ref[...] = middle
    normed_ref[...] = (norm_parts(middle)[0] * gain_ref[...] + shift_ref[...]).astype(bf16)


def mix(summed, heads_block, w_out_all, index, gain, shift):
    tokens, width = summed.shape
    cols = heads_block.shape[1]
    step = 256
    row = lambda size: pl.BlockSpec((step, size), lambda i, at: (i, 0))
    one = pl.BlockSpec((1, width), lambda i, at: (0, 0))
    return pl.pallas_call(
        mix_kernel,
        grid_spec=pltpu.PrefetchScalarGridSpec(
            num_scalar_prefetch=1,
            grid=(tokens // step,),
            in_specs=[row(width), row(cols), pl.BlockSpec((cols, width), lambda i, at: (at[0], 0)), one, one],
            out_specs=[row(width), row(width)],
        ),
        out_shape=[
            jax.ShapeDtypeStruct((tokens, width), f32),
            jax.ShapeDtypeStruct((tokens, width), bf16),
        ],
        compiler_params=pltpu.CompilerParams(vmem_limit_bytes=48 * MIB),
        cost_estimate=COST,
        name="mix",
    )(index[None].astype(jnp.int32), summed, heads_block, w_out_all, gain[None], shift[None])


def up_kernel(x_ref, w_ref, b_ref, hidden_ref, active_ref):
    hidden = dot(x_ref[...], w_ref[...]) + b_ref[...]
    hidden_ref[...] = hidden
    active_ref[...] = gelu_parts(hidden)[0].astype(bf16)


def feed_up(normed, w_up, b_up):
    tokens, width = normed.shape
    cols = w_up.shape[1]
    step = 256
    col = lambda rows: pl.BlockSpec((rows, step), lambda i: (0, i))
    return pl.pallas_call(
        up_kernel,
        grid=(cols // step,),
        in_specs=[pl.BlockSpec((tokens, width), lambda i: (0, 0)), col(width), col(1)],
        out_specs=[col(tokens), col(tokens)],
        out_shape=[
            jax.ShapeDtypeStruct((tokens, cols), f32),
            jax.ShapeDtypeStruct((tokens, cols), bf16),
        ],
        compiler_params=pltpu.CompilerParams(vmem_limit_bytes=48 * MIB),
        cost_estimate=COST,
        name="feed_up",
    )(normed, w_up, b_up[None])


def hidden_kernel(index_ref, cot_ref, hidden_ref, w_ref, *refs):
    slope = gelu_parts(hidden_ref[...])[1]
    refs[-1][...] = (dot(cot_ref[...], w_ref[...], 1, 1) * slope).astype(bf16)


def hidden_back(cot_all, hidden, w_down, half, earlier=None):
    tokens, width = cot_all.shape
    rows = tokens // 2
    cols, step = hidden.shape[1], 512
    given = [] if earlier is None else [earlier]
    return pl.pallas_call(
        hidden_kernel,
        grid_spec=pltpu.PrefetchScalarGridSpec(
            num_scalar_prefetch=1,
            grid=(cols // step,),
            in_specs=[
                pl.BlockSpec((rows, width), lambda i, at: (at[0], 0)),
                pl.BlockSpec((rows, step), lambda i, at: (at[0], i)),
                pl.BlockSpec((step, width), lambda i, at: (i, 0)),
                *[pl.BlockSpec(memory_space=pl.ANY) for _ in given],
            ],
            out_specs=pl.BlockSpec((rows, step), lambda i, at: (at[0], i)),
        ),
        out_shape=jax.ShapeDtypeStruct((tokens, cols), bf16),
        input_output_aliases={4: 0} if given else {},
        compiler_params=pltpu.CompilerParams(vmem_limit_bytes=20 * MIB),
        cost_estimate=COST,
        name="hidden_back",
    )(half[None], cot_all, hidden, w_down, *given)


def slope_kernel(index_ref, grad_ref, hidden_ref, out_ref):
    out_ref[...] = (grad_ref[...] * gelu_parts(hidden_ref[...])[1]).astype(bf16)


def slope_back(d_active, hidden, half):
    tokens, cols = hidden.shape
    step = 64
    steps = tokens // 2 // step
    place = pl.BlockSpec((step, cols), lambda i, at: (at[0] * steps + i, 0))
    return pl.pallas_call(
        slope_kernel,
        grid_spec=pltpu.PrefetchScalarGridSpec(
            num_scalar_prefetch=1,
            grid=(steps,),
            in_specs=[pl.BlockSpec((step, cols), lambda i, at: (i, 0)), place],
            out_specs=place,
        ),
        out_shape=jax.ShapeDtypeStruct((tokens, cols), bf16),
        compiler_params=pltpu.CompilerParams(vmem_limit_bytes=12 * MIB),
        cost_estimate=COST,
        name="slope_back",
    )(half[None], d_active, hidden)


def grads_kernel(factor_ref, left_ref, right_ref, *refs):
    out_ref, turned_ref = refs[-2:]

    @pl.when(pl.program_id(0) == 0)
    def _():
        turned_ref[...] = left_ref[...].T

    out_ref[...] = (factor_ref[0] * dot(turned_ref[...], right_ref[...])).astype(bf16)


def weight_grads(factor, left, right, parts=1, part=0, earlier=None):
    tokens, width = left.shape
    cols, step = right.shape[1], 256
    steps = cols // step
    given = [] if earlier is None else [earlier]
    return pl.pallas_call(
        grads_kernel,
        grid=(steps,),
        in_specs=[
            pl.BlockSpec(memory_space=pltpu.SMEM),
            pl.BlockSpec((tokens, width), lambda i: (0, 0)),
            pl.BlockSpec((tokens, step), lambda i: (0, i)),
            *[pl.BlockSpec(memory_space=pl.ANY) for _ in given],
        ],
        out_specs=pl.BlockSpec((width, step), lambda i: (0, part * steps + i)),
        out_shape=jax.ShapeDtypeStruct((width, parts * cols), bf16),
        input_output_aliases={3: 0} if given else {},
        scratch_shapes=[pltpu.VMEM((width, tokens), bf16)],
        compiler_params=pltpu.CompilerParams(vmem_limit_bytes=48 * MIB),
        cost_estimate=COST,
        name="weight_grads",
    )(factor[None], left, right, *given)


def half_kernel(index_ref, x_ref, w_ref, *refs):
    refs[-1][...] = dot(x_ref[...], w_ref[...], 1, 1).astype(bf16)


def half_product(x, weight, half, earlier=None):
    tokens, depth = x.shape
    rows = tokens // 2
    cols, step = weight.shape[0], 512
    given = [] if earlier is None else [earlier]
    return pl.pallas_call(
        half_kernel,
        grid_spec=pltpu.PrefetchScalarGridSpec(
            num_scalar_prefetch=1,
            grid=(cols // step,),
            in_specs=[
                pl.BlockSpec((rows, depth), lambda i, at: (at[0], 0)),
                pl.BlockSpec((step, depth), lambda i, at: (i, 0)),
                *[pl.BlockSpec(memory_space=pl.ANY) for _ in given],
            ],
            out_specs=pl.BlockSpec((rows, step), lambda i, at: (at[0], i)),
        ),
        out_shape=jax.ShapeDtypeStruct((tokens, cols), bf16),
        input_output_aliases={3: 0} if given else {},
        compiler_params=pltpu.CompilerParams(vmem_limit_bytes=40 * MIB),
        cost_estimate=COST,
        name="half_product",
    )(half[None], x, weight, *given)


def relay(terms, rows, index, came):
    sent = [lax.dynamic_slice_in_dim(terms, index[j] * rows, rows, axis=0) for j in range(2)]
    if came:
        sent = [(term.astype(f32) + value.astype(f32)).astype(bf16) for term, value in zip(sent, came)]
    return sent


def summed_back(term_ref, left_ref, right_ref, value_ref, gain_ref):
    grad = term_ref[...].astype(f32) + left_ref[...].astype(f32) + right_ref[...].astype(f32)
    scaled, inverse = norm_parts(value_ref[...].astype(f32))
    return grad, scaled, norm_backward(grad, gain_ref[...], scaled, inverse)


def middle_back_kernel(
    index_ref, term_ref, left_ref, right_ref, value_ref, gain_ref, cot_ref, middle_ref, branch_ref, sums_ref
):
    @pl.when(pl.program_id(0) == 0)
    def _():
        sums_ref[...] = jnp.zeros_like(sums_ref)

    grad, scaled, back = summed_back(term_ref, left_ref, right_ref, value_ref, gain_ref)
    cot = cot_ref[...].astype(f32)
    middle = cot + back
    branch = middle.astype(bf16)
    middle_ref[...], branch_ref[...] = middle, branch
    for row, value in enumerate((grad * scaled, grad, branch.astype(f32), cot)):
        sums_ref[row : row + 1, :] += jnp.sum(value, axis=0, keepdims=True)


def input_back_kernel(
    index_ref, factor_ref, term_ref, left_ref, right_ref, value_ref, gain_ref, middle_ref, out_ref
):
    back = summed_back(term_ref, left_ref, right_ref, value_ref, gain_ref)[2]
    out_ref[...] = factor_ref[0] * (middle_ref[...] + back)


def back_specs(rows, width):
    step = min(rows, 128)
    steps = rows // step
    here = pl.BlockSpec((step, width), lambda i, at: (i, 0))
    own = pl.BlockSpec((step, width), lambda i, at: (at[0] * steps + i, 0))
    return steps, here, own, pl.BlockSpec((1, width), lambda i, at: (0, 0))


def middle_back(index, terms, came, middle_all, gain, cot):
    rows, width = cot.shape
    steps, here, own, one = back_specs(rows, width)
    return pl.pallas_call(
        middle_back_kernel,
        grid_spec=pltpu.PrefetchScalarGridSpec(
            num_scalar_prefetch=1,
            grid=(steps,),
            in_specs=[own, here, here, own, one, here],
            out_specs=[here, here, pl.BlockSpec((4, width), lambda i, at: (0, 0))],
        ),
        out_shape=[
            jax.ShapeDtypeStruct((rows, width), f32),
            jax.ShapeDtypeStruct((rows, width), bf16),
            jax.ShapeDtypeStruct((4, width), f32),
        ],
        compiler_params=pltpu.CompilerParams(vmem_limit_bytes=48 * MIB),
        cost_estimate=COST,
        name="middle_back",
    )(index, terms, *came, middle_all, gain[None], cot)


def input_back(index, factor, terms, came, tokens, gain, d_middle):
    rows, width = tokens.shape
    steps, here, own, one = back_specs(rows, width)
    return pl.pallas_call(
        input_back_kernel,
        grid_spec=pltpu.PrefetchScalarGridSpec(
            num_scalar_prefetch=1,
            grid=(steps,),
            in_specs=[pl.BlockSpec(memory_space=pltpu.SMEM), own, here, here, here, one, here],
            out_specs=here,
        ),
        out_shape=jax.ShapeDtypeStruct((rows, width), f32),
        compiler_params=pltpu.CompilerParams(vmem_limit_bytes=48 * MIB),
        cost_estimate=COST,
        name="input_back",
    )(index, factor[None], terms, *came, tokens, gain[None], d_middle)


def present_kernel(qkv_ref, up_ref, down_ref, qkv_out, up_out, down_out):
    cols = qkv_out.shape[2]
    for j in range(3):
        qkv_out[j] = qkv_ref[:, j * cols : (j + 1) * cols].astype(f32)
    up_out[...] = up_ref[...].astype(f32)
    down_out[...] = down_ref[...].astype(f32).T


def present(qkv, up, down):
    rows, cols = up.shape
    head_cols = qkv.shape[1] // 3
    step = min(rows, 128)
    row = lambda size: pl.BlockSpec((step, size), lambda i: (i, 0))
    return pl.pallas_call(
        present_kernel,
        grid=(rows // step,),
        in_specs=[row(3 * head_cols), row(cols), row(cols)],
        out_specs=[
            pl.BlockSpec((3, step, head_cols), lambda i: (0, i, 0)),
            row(cols),
            pl.BlockSpec((cols, step), lambda i: (0, i)),
        ],
        out_shape=[
            jax.ShapeDtypeStruct((3, rows, head_cols), f32),
            jax.ShapeDtypeStruct((rows, cols), f32),
            jax.ShapeDtypeStruct((cols, rows), f32),
        ],
        compiler_params=pltpu.CompilerParams(vmem_limit_bytes=48 * MIB),
        cost_estimate=COST,
        name="present",
    )(qkv, up, down)


def blank_kernel(out_ref):
    pass


def blank(shape):
    return pl.pallas_call(
        blank_kernel,
        out_specs=pl.BlockSpec(memory_space=pl.ANY),
        out_shape=jax.ShapeDtypeStruct(shape, bf16),
        name="blank",
    )()


def sums_kernel(term_ref, token_ref, out_ref):
    @pl.when(pl.program_id(0) == 0)
    def _():
        out_ref[...] = jnp.zeros_like(out_ref)

    term = term_ref[...].astype(f32)
    scaled = norm_parts(token_ref[...].astype(f32))[0]
    out_ref[0:1, :] += jnp.sum(term * scaled, axis=0, keepdims=True)
    out_ref[1:2, :] += jnp.sum(term, axis=0, keepdims=True)


def gain_sums(terms, tokens_all):
    rows, width = terms.shape
    block = pl.BlockSpec((128, width), lambda i: (i, 0))
    return pl.pallas_call(
        sums_kernel,
        grid=(rows // 128,),
        in_specs=[block, block],
        out_specs=pl.BlockSpec((2, width), lambda i: (0, 0)),
        out_shape=jax.ShapeDtypeStruct((2, width), f32),
        compiler_params=pltpu.CompilerParams(vmem_limit_bytes=12 * MIB),
        cost_estimate=COST,
        name="gain_sums",
    )(terms, tokens_all)


class Phases:
    def __init__(self):
        self.marks, self.kept, self.sends = (), [], []

    def __call__(self, *values):
        gate = (*self.marks, *self.sends)
        if gate:
            values = lax.optimization_barrier((*values, *gate))[: len(values)]
        return values if len(values) > 1 else values[0]

    def early(self, *values):
        if self.marks:
            values = lax.optimization_barrier((*values, *self.marks))[: len(values)]
        return values if len(values) > 1 else values[0]

    def send(self, *values):
        self.sends += values

    def keep(self, *values):
        self.kept += values
        return values if len(values) > 1 else values[0]

    def turn(self):
        self.marks, self.kept, self.sends = tuple(self.kept), [], []


class Line:
    def __init__(self, name, size):
        self.name, self.n = name, size
        self.me = lax.axis_index(name)
        self.low = self.me < size // 2

    def slot(self, k):
        n = self.n
        return jnp.where(self.low, (self.me + k) % n, (self.me + n - k) % n)

    def shuffle(self, phase, array):
        n = self.n
        cols = array.shape[1] // n
        out = []
        for shift in range(n):
            target = (self.me + shift) % n
            block = lax.dynamic_slice_in_dim(phase.early(array), target * cols, cols, axis=1)
            if shift:
                phase.send(block)
                block = lax.ppermute(block, self.name, [(j, (j + shift) % n) for j in range(n)])
            out.append(phase.keep(block))
        return out

    def shuffle_rows(self, phase, array, rows):
        n = self.n
        out = []
        for shift in range(1, n):
            target = (self.me + shift) % n
            block = lax.dynamic_slice_in_dim(phase.early(array), target * rows, rows, axis=0)
            phase.send(block)
            out.append(lax.ppermute(block, self.name, [(j, (j + shift) % n) for j in range(n)]))
        return out

    def stack(self, blocks):
        n = self.n
        rows, cols = blocks[0].shape
        out = blank((n * rows, cols))
        for shift, block in enumerate(blocks):
            source = (self.me + n - shift) % n
            out = lax.dynamic_update_slice_in_dim(out, block, source * rows, axis=0)
        return out


class Gather:
    def __init__(self, line, block):
        self.line, self.left, self.right, self.slots = line, [block], [block], {0: block}

    def step(self, phase):
        line, n, k = self.line, self.line.n, len(self.left)
        left, right = phase.early(self.left[-1], self.right[-1])
        phase.send(left, right)
        self.left.append(lax.ppermute(left, line.name, [(j, j + 1) for j in range(k - 1, n - 1)]))
        self.right.append(lax.ppermute(right, line.name, [(j, j - 1) for j in range(1, n - k + 1)]))
        phase.keep(self.left[k], self.right[k])

    def slot(self, phase, k):
        if k not in self.slots:
            line, n = self.line, self.line.n
            if 2 * k < n:
                left, right = phase(self.left[k], self.right[k])
                value = jnp.where(line.low, right, left)
            else:
                left, right, left_far, right_far = phase(
                    self.left[n - k], self.right[n - k], self.left[k], self.right[k]
                )
                low_side = jnp.where(line.me + k < n, right_far, left)
                high_side = jnp.where(line.me >= k, left_far, right)
                value = jnp.where(line.low, low_side, high_side)
            self.slots[k] = value
        return self.slots[k]


class Reduce:
    def __init__(self, line, rows):
        self.line, self.rows, self.k, self.came, self.terms = line, rows, 1, (), None

    def step(self, phase):
        line, n, k = self.line, self.line.n, self.k
        blocks = [jnp.clip(line.me + n - k, 0, n - 1), jnp.clip(line.me - n + k, 0, n - 1)]
        self.terms = phase.early(self.terms)
        sent = relay(self.terms, self.rows, jnp.stack(blocks).astype(jnp.int32), self.came)
        phase.send(*sent)
        self.came = (
            lax.ppermute(sent[0], line.name, [(j, j + 1) for j in range(k)]),
            lax.ppermute(sent[1], line.name, [(j, j - 1) for j in range(n - k, n)]),
        )
        phase.keep(*self.came)
        self.k += 1


def flip(value, name, size, bit):
    return lax.ppermute(value, name, [(j, j ^ bit) for j in range(size)])


def sum_over(value, name, size, bit=1):
    while bit < size:
        value = value + flip(value, name, size, bit)
        bit *= 2
    return value


class Spread:
    def __init__(self, name, size, moved, still, moved_left, factor):
        self.name, self.size, self.factor, self.moved_left = name, size, factor, moved_left
        self.moved, self.still = moved, still
        self.bits = [1 << b for b in range(1, size.bit_length() - 1)]
        self.orders = [self.bits, self.bits[::-1]]
        self.block_cols = moved.shape[1] // size

    def blocks(self, moved, wanted):
        cols, index = self.block_cols, lax.axis_index(self.name)
        return jnp.concatenate(
            [lax.dynamic_slice_in_dim(moved, (index ^ r) * cols, cols, axis=1) for r in wanted], axis=1
        )

    def product(self, moved, still):
        left, right = (moved, still) if self.moved_left else (still, moved)
        return self.factor * dot(left, right, 0, 0)

    def listed(self, order, fixed):
        out = [sum(bit for bit, on in fixed.items() if on)]
        for bit in order[::-1]:
            if bit not in fixed:
                out = [*out, *[r + bit for r in out]]
        return out

    def cut(self, array, low, high):
        return array[low:high] if self.moved_left else array[:, low:high]

    def start(self, phase):
        moved = phase(self.moved)
        self.sent = self.product(self.blocks(moved, self.listed(self.bits, {1: True})), self.still).astype(bf16)
        return self.sent

    def cross(self, phase):
        sent = phase.early(self.sent)
        phase.send(sent)
        self.brought = flip(sent, self.name, self.size, 1)
        return self.brought

    def second(self, phase):
        moved, brought = phase(self.moved, self.brought)
        cols, along = self.block_cols, 0 if self.moved_left else 1
        half = self.still.shape[1] // 2
        first_list = self.listed(self.bits, {1: True})
        self.sent, self.kept = [], []
        for which, order in enumerate(self.orders):
            still = self.still[:, which * half : (which + 1) * half]
            part = lax.slice_in_dim(brought, which * half, (which + 1) * half, axis=1 - along)
            for on in (True, False):
                wanted = self.listed(order, {1: False, order[0]: on})
                places = [first_list.index(r + 1) for r in wanted]
                added = jnp.concatenate(
                    [self.cut(part, p * cols, (p + 1) * cols) for p in places], axis=along
                )
                value = (self.product(self.blocks(moved, wanted), still) + added.astype(f32)).astype(bf16)
                (self.sent if on else self.kept).append(value)
        self.done, self.air, self.result = 0, False, None
        return (*self.sent, *self.kept)

    def fly(self, phase):
        sent = phase.early(*self.sent)
        phase.send(*sent)
        self.flying = tuple(
            flip(value, self.name, self.size, order[self.done]) for value, order in zip(sent, self.orders)
        )
        self.done, self.air = self.done + 1, True
        return self.flying

    def land(self, phase):
        along, self.air = 0 if self.moved_left else 1, False
        flying = phase(*self.flying)
        totals = [k.astype(f32) + f.astype(f32) for k, f in zip(self.kept, flying)]
        if self.done == len(self.bits):
            self.result = jnp.concatenate(totals, axis=1 - along)
            return (self.result,)
        size = totals[0].shape[along]
        self.sent = [self.cut(t, size // 2, size).astype(bf16) for t in totals]
        self.kept = [self.cut(t, 0, size // 2).astype(bf16) for t in totals]
        return (*self.sent, *self.kept)

    def finish(self, phase):
        while self.result is None:
            (self.land if self.air else self.fly)(phase)
        return self.result


def after(value, *earlier):
    return lax.optimization_barrier((value, *earlier))[0]


def make_body(n_dp, n_mp):
    def body(
        tokens, cotangent, segment, counts, ln_gain, ln_bias, w_qkv, b_qv, w_out, out_bias, w_up, b_up, w_down
    ):
        line, phase = Line("mp", n_mp), Phases()
        keep, turn = phase.keep, phase.turn
        gains, shifts, bias_pair = ln_gain.astype(f32), ln_bias.astype(f32), out_bias.astype(f32)
        share, width = tokens.shape
        head_cols = w_qkv.shape[2]
        heads = head_cols // HEAD
        group = segment.shape[0]
        seg_col, seg_row = segment[:, None], segment[None, :]
        me = line.me
        place = lambda whole, block, index: lax.dynamic_update_slice_in_dim(
            whole, block, index * share, axis=0
        )
        rows_of = lambda whole, index: lax.dynamic_slice_in_dim(whole, index * share, share, axis=0)
        total = lambda value: jnp.sum(value.astype(f32), axis=0)
        slots, last = range(1, n_mp), n_mp - 1

        flat_qkv = jnp.concatenate([w_qkv[:, j] for j in range(3)], axis=1)
        bias_rows = (
            jnp.stack([b_qv[0], jnp.zeros_like(b_qv[0]), b_qv[1]]).astype(f32).reshape(3 * head_cols)
        )
        state = [blank((group, width)), blank((group, width)), blank((group, 3 * head_cols))]

        def project(k):
            block = phase(gather.slot(phase, k))
            normed = (norm_parts(block.astype(f32))[0] * gains[0] + shifts[0]).astype(bf16)
            proj = (dot(normed, flat_qkv) + bias_rows).astype(bf16)
            for j, value in enumerate((block, normed, proj)):
                state[j] = keep(place(state[j], value, line.slot(k)))

        slice_rows = w_out.shape[0] // n_dp
        w_slice = lax.dynamic_slice_in_dim(
            w_out, lax.axis_index("dp") * slice_rows, slice_rows, axis=0
        )

        gather = Gather(line, tokens)
        for k in slots:
            gather.step(phase)
            if k == 2:
                w_slices = lax.all_gather(phase(w_slice), "mp", axis=0)
            project(k - 1)
            turn()
        cot_gather = Gather(line, cotangent)
        cot_gather.step(phase)
        w_out_all = lax.all_gather(phase(w_slices), "dp", axis=1).reshape(n_mp * w_out.shape[0], width)
        project(last)
        tokens_all, normed1_all, projected = state
        attn = keep(attend(projected, seg_col, seg_row, heads))
        turn()

        set_heads = lambda whole, block, index: lax.dynamic_update_slice_in_dim(
            whole, block, index * head_cols, axis=1
        )
        w_rows = lambda k: lax.dynamic_slice_in_dim(w_out_all, line.slot(k) * head_cols, head_cols, axis=0)
        half = line.low.astype(jnp.int32)
        attn_all = blank((group, n_mp * head_cols))
        cot_all = place(blank((group, width)), phase(cotangent), me)

        def place_near():
            nonlocal cot_all
            for j in range(1, n_mp // 2):
                for came, index in ((cot_gather.left[j], me - j), (cot_gather.right[j], me + j)):
                    here = (index >= 0) & (index < n_mp) & ((index < n_mp // 2) == line.low)
                    came = phase(came)
                    cot_all = place(cot_all, jnp.where(here, came, cotangent), jnp.where(here, index, me))
            cot_all = keep(phase(cot_all))

        attn_gather = Gather(line, attn)
        for k in slots:
            attn_gather.step(phase)
            attn_all = keep(set_heads(attn_all, phase(attn_gather.slot(phase, k - 1)), line.slot(k - 1)))
            if k == 1:
                middle_sum = keep(tokens_all.astype(f32) + bias_pair[0] + dot(phase(attn), w_out))
                count_here = phase(counts.astype(f32))
                factor = keep((count_here / sum_over(count_here, "dp", n_dp))[0])
            if k == 2 and n_mp == 4:
                place_near()
                near_rows = lax.dynamic_slice_in_dim(cot_all, (1 - half) * (group // 2), group // 2, axis=0)
                near_active = keep(dot(near_rows, w_down, 1, 1))
            if k == last:
                for j in range(1, last):
                    middle_sum = keep(middle_sum + dot(phase(attn_gather.slot(phase, j)), w_rows(j)))
            turn()
        reduce_down, reduce2, reduce1 = (Reduce(line, share) for _ in range(3))
        for k in slots[1:]:
            cot_gather.step(phase)
            if k == 2:
                heads_last = attn_gather.slot(phase, last)
                middle_all, normed2_all = mix(
                    middle_sum, heads_last, w_out_all, line.slot(last), gains[1], shifts[1]
                )
                hidden, active = keep(*feed_up(normed2_all, w_up, b_up.astype(f32)))
                keep(middle_all, normed2_all)
            if k == 3:
                attn_all = keep(set_heads(attn_all, phase(heads_last), line.slot(last)))
                reduce_down.terms = keep(dot(phase(active), w_down).astype(bf16))
            if k == max(3, n_mp // 2):
                if n_mp == 4:
                    cot_all = keep(place(cot_all, cot_gather.slot(phase, 2), line.slot(2)))
                    d_hidden_all = keep(slope_back(phase(near_active), hidden, 1 - half))
                else:
                    place_near()
                    d_hidden_all = keep(hidden_back(cot_all, hidden, w_down, 1 - half))
            turn()

        scatter = lambda full: lax.psum_scatter(phase(full), "dp", scatter_dimension=0, tiled=True)

        reduce_down.step(phase)
        if n_mp == 4:
            edge = (me == 0) | (me == last)
            came = [phase(side[1], side[3]) for side in (cot_gather.left, cot_gather.right)]
            block = jnp.where(line.low, jnp.where(edge, came[1][1], came[1][0]), jnp.where(edge, came[0][1], came[0][0]))
            cot_all = place(cot_all, block, jnp.where(edge, line.slot(3), line.slot(1)))
        else:
            for k in slots:
                cot_all = place(cot_all, cot_gather.slot(phase, k), line.slot(k))
        d_hidden_all = keep(hidden_back(cot_all, hidden, w_down, half, d_hidden_all))
        reduce2.terms = keep(dot(d_hidden_all, w_up, 1, 1).astype(bf16))
        turn()
        for k in slots:
            reduce2.step(phase)
            if k == 1:
                up_full = keep(weight_grads(factor, phase(normed2_all), d_hidden_all))
            if k == 2:
                grad_up = scatter(up_full)
                down_full = keep(weight_grads(factor, phase(cot_all), active))
            if k == 3:
                grad_down = scatter(down_full)
                split_sums = keep(factor * total(phase(d_hidden_all)))
            turn()
        own = me[None].astype(jnp.int32)
        reduce_down.step(phase)
        d_middle, d_branch, own_sums = keep(
            *middle_back(own, phase(reduce2.terms), reduce2.came, middle_all, gains[1], cotangent)
        )
        d_attn_own = keep(dot(d_branch, w_out_all, 1, 1).astype(bf16))
        spread_out = Spread("dp", n_dp, after(d_branch, d_attn_own), rows_of(attn_all, me), False, factor)
        keep(spread_out.start(phase))
        turn()
        d_attn_blocks = line.shuffle(phase, d_attn_own)
        spread_out.cross(phase)
        keep(*spread_out.second(phase))
        keep(grad_up)
        turn()
        reduce_down.step(phase)
        d_attn = line.stack(phase(*d_attn_blocks))
        grad_proj = keep(attend_back(projected, d_attn, seg_col, seg_row, heads))
        reduce1.terms = keep(half_product(grad_proj, flat_qkv, half))
        turn()
        for k in slots:
            reduce1.step(phase)
            if k == 1:
                keep(*spread_out.fly(phase))
                reduce1.terms = keep(half_product(phase(grad_proj), flat_qkv, 1 - half, reduce1.terms))
                gain1 = gain_sums(reduce1.terms, tokens_all)
                full_sums = factor * jnp.concatenate([gain1, own_sums], axis=0).reshape(-1)
                full_sums = keep(full_sums + keep(flip(full_sums, "mp", n_mp, 1)))
                qkv_full = keep(weight_grads(factor, after(normed1_all, gain1), grad_proj))
                keep(grad_down)
            if k == 2:
                grad_qkv = scatter(qkv_full)
                keep(*spread_out.land(phase))
                heads_sum = [total(phase(grad_proj)[:, :head_cols]), total(grad_proj[:, 2 * head_cols :])]
                split_sums = keep(jnp.concatenate([*[factor * s for s in heads_sum], split_sums]))
            if k == 3:
                keep(*spread_out.fly(phase))
                for _ in slots[3:]:
                    reduce_down.step(phase)
                down_sum = sum(
                    value.astype(f32)
                    for value in (rows_of(phase(reduce_down.terms), me), *reduce_down.came)
                )
                layer_out = keep((rows_of(middle_all, me) + down_sum + bias_pair[1]).astype(bf16))
                full_sums = keep(sum_over(phase(full_sums), "mp", n_mp, 2))
            turn()
        out_rows = spread_out.finish(phase)
        out_blocks = line.shuffle_rows(phase, out_rows.astype(bf16), head_cols)
        grad_input = input_back(
            own, factor, phase(reduce1.terms), reduce1.came, tokens, gains[0], d_middle
        )
        grad_qkv, grad_up, grad_down = present(*phase(grad_qkv, grad_up, grad_down))
        sums = after(jnp.concatenate([full_sums, split_sums]), grad_input).reshape(1, 8, -1)
        sums = lax.all_gather(sums, "dp", axis=0, tiled=True)
        sums, grad_qkv, *out_blocks = lax.optimization_barrier((sums, grad_qkv, *out_blocks))
        grad_out = lax.dynamic_slice_in_dim(out_rows, me * head_cols, head_cols, axis=0)
        for block in out_blocks:
            grad_out = grad_out + block.astype(f32)
        sums = jnp.sum(sums, axis=0).reshape(-1)
        full_sums = sums[: 6 * width].reshape(6, width)
        split_sums = sums[6 * width :]
        return (
            layer_out,
            grad_input,
            jnp.stack([full_sums[0], full_sums[2]]),
            jnp.stack([full_sums[1], full_sums[3]]),
            grad_qkv.transpose(1, 0, 2),
            split_sums[: 2 * head_cols].reshape(2, head_cols),
            grad_out,
            full_sums[4:],
            grad_up,
            split_sums[2 * head_cols :],
            grad_down,
        )

    return body


def solution(mesh):
    split = P(("dp", "mp"), None)
    return jax.shard_map(
        make_body(mesh.shape["dp"], mesh.shape["mp"]),
        mesh=mesh,
        in_specs=(
            split, split, P("dp"), P("dp"), P(), P(), P(None, None, "mp"), P(None, "mp"), P("mp", None), P(),
            P(None, "mp"), P("mp"), P("mp", None),
        ),
        out_specs=(
            split, split, P(), P(), P("dp", None, "mp"), P(None, "mp"), P("mp", "dp"), P(), P("dp", "mp"), P("mp"),
            P("mp", "dp"),
        ),
        check_vma=False,
    )
```

```python
import functools
import jax
import jax.numpy as jnp
from jax import lax
from jax.experimental import pallas as pl
from jax.experimental.pallas import tpu as pltpu
from jax.sharding import PartitionSpec as P

HEAD = 128
SEQ = 1024
BLOCK = 256
SCALE = HEAD ** (-0.5)
f32 = jnp.float32
bf16 = jnp.bfloat16
MIB = 2**20
COST = pl.CostEstimate(flops=1 << 20, bytes_accessed=1 << 16, transcendentals=0)


def dot(left, right, left_dim=1, right_dim=0):
    return lax.dot_general(
        left, right, (((left_dim,), (right_dim,)), ((), ())), preferred_element_type=f32
    )


def block_probs(q_block, k_ref, seg_col, seg_row, block, reach):
    start = block * BLOCK
    scores = dot(k_ref[:reach, :], q_block, 1, 1) * SCALE
    key_place = lax.broadcasted_iota(jnp.int32, (reach, BLOCK), 0)
    query_place = start + lax.broadcasted_iota(jnp.int32, (reach, BLOCK), 1)
    allowed = (seg_col[:reach, :] == seg_row[:, start : start + BLOCK]) & (
        key_place <= query_place
    )
    scores = jnp.where(allowed, scores, -1e30)
    expo = jnp.exp(scores - jnp.max(scores, axis=0, keepdims=True))
    return expo * (1.0 / jnp.sum(expo, axis=0, keepdims=True))


def attend_kernel(q_ref, k_ref, v_ref, seg_col, seg_row, out_ref):
    for block in range(SEQ // BLOCK):
        rows = slice(block * BLOCK, (block + 1) * BLOCK)
        reach = (block + 1) * BLOCK
        probs = block_probs(q_ref[rows, :], k_ref, seg_col, seg_row, block, reach)
        out_ref[rows, :] = dot(probs.astype(bf16), v_ref[:reach, :], 0, 0).astype(bf16)


def attend(projected, seg_col, seg_row, heads):
    tokens = projected.shape[0]
    column = lambda part: pl.BlockSpec((SEQ, HEAD), lambda r, h: (r, part * heads + h))
    return pl.pallas_call(
        attend_kernel,
        grid=(tokens // SEQ, heads),
        in_specs=[
            column(0),
            column(1),
            column(2),
            pl.BlockSpec((SEQ, 1), lambda r, h: (r, 0)),
            pl.BlockSpec((1, SEQ), lambda r, h: (0, r)),
        ],
        out_specs=pl.BlockSpec((SEQ, HEAD), lambda r, h: (r, h)),
        out_shape=jax.ShapeDtypeStruct((tokens, heads * HEAD), bf16),
        compiler_params=pltpu.CompilerParams(vmem_limit_bytes=24 * MIB),
        cost_estimate=COST,
        name="attend",
    )(projected, projected, projected, seg_col, seg_row)


def attend_back_kernel(
    heads, q_ref, k_ref, v_ref, grad_ref, seg_col, seg_row, out_ref, dk_ref, dv_ref
):
    head = pl.program_id(1)
    width = heads * HEAD
    column = lambda part: pl.ds(pl.multiple_of(part * width + head * HEAD, HEAD), HEAD)
    dk_ref[...] = jnp.zeros_like(dk_ref)
    dv_ref[...] = jnp.zeros_like(dv_ref)
    for block in range(SEQ // BLOCK):
        rows = slice(block * BLOCK, (block + 1) * BLOCK)
        reach = (block + 1) * BLOCK
        q_block = q_ref[rows, :]
        g_block = grad_ref[rows, :]
        probs = block_probs(q_block, k_ref, seg_col, seg_row, block, reach)
        d_probs = dot(v_ref[:reach, :], g_block, 1, 1)
        delta = jnp.sum(probs * d_probs, axis=0, keepdims=True)
        d_scores = (probs * (d_probs - delta)).astype(bf16)
        dv_ref[:reach, :] += dot(probs.astype(bf16), g_block)
        dk_ref[:reach, :] += dot(d_scores, q_block)
        out_ref[rows, column(0)] = (dot(d_scores, k_ref[:reach, :], 0, 0) * SCALE).astype(bf16)
    out_ref[:, column(1)] = (dk_ref[...] * SCALE).astype(bf16)
    out_ref[:, column(2)] = dv_ref[...].astype(bf16)


def attend_back(projected, grad_attn, seg_col, seg_row, heads):
    tokens = projected.shape[0]
    column = lambda part: pl.BlockSpec((SEQ, HEAD), lambda r, h: (r, part * heads + h))
    return pl.pallas_call(
        functools.partial(attend_back_kernel, heads),
        grid=(tokens // SEQ, heads),
        in_specs=[
            column(0),
            column(1),
            column(2),
            column(0),
            pl.BlockSpec((SEQ, 1), lambda r, h: (r, 0)),
            pl.BlockSpec((1, SEQ), lambda r, h: (0, r)),
        ],
        out_specs=pl.BlockSpec((SEQ, 3 * heads * HEAD), lambda r, h: (r, 0)),
        out_shape=jax.ShapeDtypeStruct((tokens, 3 * heads * HEAD), bf16),
        scratch_shapes=[pltpu.VMEM((SEQ, HEAD), f32), pltpu.VMEM((SEQ, HEAD), f32)],
        compiler_params=pltpu.CompilerParams(vmem_limit_bytes=32 * MIB),
        cost_estimate=COST,
        name="attend_back",
    )(projected, projected, projected, grad_attn, seg_col, seg_row)


def norm_parts(value):
    mean = jnp.mean(value, axis=-1, keepdims=True)
    centered = value - mean
    inverse = lax.rsqrt(jnp.mean(centered * centered, axis=-1, keepdims=True) + 1e-05)
    return centered * inverse, inverse


def norm_backward(grad, gain, scaled, inverse):
    inner = grad * gain
    return inverse * (
        inner
        - jnp.mean(inner, axis=-1, keepdims=True)
        - scaled * jnp.mean(inner * scaled, axis=-1, keepdims=True)
    )


def gelu_parts(value):
    c = 0.7978845608028654
    square = value * value
    tanh = jnp.tanh(c * value * (1.0 + 0.044715 * square))
    half = 0.5 * (1.0 + tanh)
    slope = half + 0.5 * value * (1.0 - tanh * tanh) * c * (1.0 + 3 * 0.044715 * square)
    return value * half, slope


def mix_kernel(index_ref, sum_ref, heads_ref, w_ref, gain_ref, shift_ref, middle_ref, normed_ref):
    middle = sum_ref[...] + dot(heads_ref[...], w_ref[...])
    middle_ref[...] = middle
    normed_ref[...] = (norm_parts(middle)[0] * gain_ref[...] + shift_ref[...]).astype(bf16)


def mix(summed, heads_block, w_out_all, index, gain, shift):
    tokens, width = summed.shape
    cols = heads_block.shape[1]
    step = 256
    row = lambda size: pl.BlockSpec((step, size), lambda i, at: (i, 0))
    one = pl.BlockSpec((1, width), lambda i, at: (0, 0))
    return pl.pallas_call(
        mix_kernel,
        grid_spec=pltpu.PrefetchScalarGridSpec(
            num_scalar_prefetch=1,
            grid=(tokens // step,),
            in_specs=[row(width), row(cols), pl.BlockSpec((cols, width), lambda i, at: (at[0], 0)), one, one],
            out_specs=[row(width), row(width)],
        ),
        out_shape=[
            jax.ShapeDtypeStruct((tokens, width), f32),
            jax.ShapeDtypeStruct((tokens, width), bf16),
        ],
        compiler_params=pltpu.CompilerParams(vmem_limit_bytes=48 * MIB),
        cost_estimate=COST,
        name="mix",
    )(index[None].astype(jnp.int32), summed, heads_block, w_out_all, gain[None], shift[None])


def up_kernel(x_ref, w_ref, b_ref, hidden_ref, active_ref):
    hidden = dot(x_ref[...], w_ref[...]) + b_ref[...]
    hidden_ref[...] = hidden
    active_ref[...] = gelu_parts(hidden)[0].astype(bf16)


def feed_up(normed, w_up, b_up):
    tokens, width = normed.shape
    cols = w_up.shape[1]
    step = 256
    col = lambda rows: pl.BlockSpec((rows, step), lambda i: (0, i))
    return pl.pallas_call(
        up_kernel,
        grid=(cols // step,),
        in_specs=[pl.BlockSpec((tokens, width), lambda i: (0, 0)), col(width), col(1)],
        out_specs=[col(tokens), col(tokens)],
        out_shape=[
            jax.ShapeDtypeStruct((tokens, cols), f32),
            jax.ShapeDtypeStruct((tokens, cols), bf16),
        ],
        compiler_params=pltpu.CompilerParams(vmem_limit_bytes=48 * MIB),
        cost_estimate=COST,
        name="feed_up",
    )(normed, w_up, b_up[None])


def hidden_kernel(index_ref, cot_ref, hidden_ref, w_ref, *refs):
    slope = gelu_parts(hidden_ref[...])[1]
    refs[-1][...] = (dot(cot_ref[...], w_ref[...], 1, 1) * slope).astype(bf16)


def hidden_back(cot_all, hidden, w_down, half, earlier=None):
    tokens, width = cot_all.shape
    rows = tokens // 2
    cols, step = hidden.shape[1], 512
    given = [] if earlier is None else [earlier]
    return pl.pallas_call(
        hidden_kernel,
        grid_spec=pltpu.PrefetchScalarGridSpec(
            num_scalar_prefetch=1,
            grid=(cols // step,),
            in_specs=[
                pl.BlockSpec((rows, width), lambda i, at: (at[0], 0)),
                pl.BlockSpec((rows, step), lambda i, at: (at[0], i)),
                pl.BlockSpec((step, width), lambda i, at: (i, 0)),
                *[pl.BlockSpec(memory_space=pl.ANY) for _ in given],
            ],
            out_specs=pl.BlockSpec((rows, step), lambda i, at: (at[0], i)),
        ),
        out_shape=jax.ShapeDtypeStruct((tokens, cols), bf16),
        input_output_aliases={4: 0} if given else {},
        compiler_params=pltpu.CompilerParams(vmem_limit_bytes=48 * MIB),
        cost_estimate=COST,
        name="hidden_back",
    )(half[None], cot_all, hidden, w_down, *given)


def slope_kernel(index_ref, grad_ref, hidden_ref, out_ref):
    out_ref[...] = (grad_ref[...] * gelu_parts(hidden_ref[...])[1]).astype(bf16)


def slope_back(d_active, hidden, half):
    tokens, cols = hidden.shape
    step = 64
    steps = tokens // 2 // step
    place = pl.BlockSpec((step, cols), lambda i, at: (at[0] * steps + i, 0))
    return pl.pallas_call(
        slope_kernel,
        grid_spec=pltpu.PrefetchScalarGridSpec(
            num_scalar_prefetch=1,
            grid=(steps,),
            in_specs=[pl.BlockSpec((step, cols), lambda i, at: (i, 0)), place],
            out_specs=place,
        ),
        out_shape=jax.ShapeDtypeStruct((tokens, cols), bf16),
        compiler_params=pltpu.CompilerParams(vmem_limit_bytes=12 * MIB),
        cost_estimate=COST,
        name="slope_back",
    )(half[None], d_active, hidden)


def grads_kernel(factor_ref, left_ref, right_ref, *refs):
    out_ref, turned_ref = refs[-2:]

    @pl.when(pl.program_id(0) == 0)
    def _():
        turned_ref[...] = left_ref[...].T

    out_ref[...] = (factor_ref[0] * dot(turned_ref[...], right_ref[...])).astype(bf16)


def weight_grads(factor, left, right, parts=1, part=0, earlier=None):
    tokens, width = left.shape
    cols, step = right.shape[1], 256
    steps = cols // step
    given = [] if earlier is None else [earlier]
    return pl.pallas_call(
        grads_kernel,
        grid=(steps,),
        in_specs=[
            pl.BlockSpec(memory_space=pltpu.SMEM),
            pl.BlockSpec((tokens, width), lambda i: (0, 0)),
            pl.BlockSpec((tokens, step), lambda i: (0, i)),
            *[pl.BlockSpec(memory_space=pl.ANY) for _ in given],
        ],
        out_specs=pl.BlockSpec((width, step), lambda i: (0, part * steps + i)),
        out_shape=jax.ShapeDtypeStruct((width, parts * cols), bf16),
        input_output_aliases={3: 0} if given else {},
        scratch_shapes=[pltpu.VMEM((width, tokens), bf16)],
        compiler_params=pltpu.CompilerParams(vmem_limit_bytes=48 * MIB),
        cost_estimate=COST,
        name="weight_grads",
    )(factor[None], left, right, *given)


def half_kernel(index_ref, x_ref, w_ref, *refs):
    refs[-1][...] = dot(x_ref[...], w_ref[...], 1, 1).astype(bf16)


def half_product(x, weight, half, earlier=None):
    tokens, depth = x.shape
    rows = tokens // 2
    cols, step = weight.shape[0], 512
    given = [] if earlier is None else [earlier]
    return pl.pallas_call(
        half_kernel,
        grid_spec=pltpu.PrefetchScalarGridSpec(
            num_scalar_prefetch=1,
            grid=(cols // step,),
            in_specs=[
                pl.BlockSpec((rows, depth), lambda i, at: (at[0], 0)),
                pl.BlockSpec((step, depth), lambda i, at: (i, 0)),
                *[pl.BlockSpec(memory_space=pl.ANY) for _ in given],
            ],
            out_specs=pl.BlockSpec((rows, step), lambda i, at: (at[0], i)),
        ),
        out_shape=jax.ShapeDtypeStruct((tokens, cols), bf16),
        input_output_aliases={3: 0} if given else {},
        compiler_params=pltpu.CompilerParams(vmem_limit_bytes=24 * MIB),
        cost_estimate=COST,
        name="half_product",
    )(half[None], x, weight, *given)


def relay(terms, rows, index, came):
    sent = [lax.dynamic_slice_in_dim(terms, index[j] * rows, rows, axis=0) for j in range(2)]
    if came:
        sent = [(term.astype(f32) + value.astype(f32)).astype(bf16) for term, value in zip(sent, came)]
    return sent


def summed_back(term_ref, left_ref, right_ref, value_ref, gain_ref):
    grad = term_ref[...].astype(f32) + left_ref[...].astype(f32) + right_ref[...].astype(f32)
    scaled, inverse = norm_parts(value_ref[...].astype(f32))
    return grad, scaled, norm_backward(grad, gain_ref[...], scaled, inverse)


def middle_back_kernel(
    index_ref, term_ref, left_ref, right_ref, value_ref, gain_ref, cot_ref, middle_ref, branch_ref, sums_ref
):
    @pl.when(pl.program_id(0) == 0)
    def _():
        sums_ref[...] = jnp.zeros_like(sums_ref)

    grad, scaled, back = summed_back(term_ref, left_ref, right_ref, value_ref, gain_ref)
    cot = cot_ref[...].astype(f32)
    middle = cot + back
    branch = middle.astype(bf16)
    middle_ref[...], branch_ref[...] = middle, branch
    for row, value in enumerate((grad * scaled, grad, branch.astype(f32), cot)):
        sums_ref[row : row + 1, :] += jnp.sum(value, axis=0, keepdims=True)


def input_back_kernel(
    index_ref, factor_ref, term_ref, left_ref, right_ref, value_ref, gain_ref, middle_ref, out_ref
):
    back = summed_back(term_ref, left_ref, right_ref, value_ref, gain_ref)[2]
    out_ref[...] = factor_ref[0] * (middle_ref[...] + back)


def back_specs(rows, width):
    step = min(rows, 128)
    steps = rows // step
    here = pl.BlockSpec((step, width), lambda i, at: (i, 0))
    own = pl.BlockSpec((step, width), lambda i, at: (at[0] * steps + i, 0))
    return steps, here, own, pl.BlockSpec((1, width), lambda i, at: (0, 0))


def middle_back(index, terms, came, middle_all, gain, cot):
    rows, width = cot.shape
    steps, here, own, one = back_specs(rows, width)
    return pl.pallas_call(
        middle_back_kernel,
        grid_spec=pltpu.PrefetchScalarGridSpec(
            num_scalar_prefetch=1,
            grid=(steps,),
            in_specs=[own, here, here, own, one, here],
            out_specs=[here, here, pl.BlockSpec((4, width), lambda i, at: (0, 0))],
        ),
        out_shape=[
            jax.ShapeDtypeStruct((rows, width), f32),
            jax.ShapeDtypeStruct((rows, width), bf16),
            jax.ShapeDtypeStruct((4, width), f32),
        ],
        compiler_params=pltpu.CompilerParams(vmem_limit_bytes=48 * MIB),
        cost_estimate=COST,
        name="middle_back",
    )(index, terms, *came, middle_all, gain[None], cot)


def input_back(index, factor, terms, came, tokens, gain, d_middle):
    rows, width = tokens.shape
    steps, here, own, one = back_specs(rows, width)
    return pl.pallas_call(
        input_back_kernel,
        grid_spec=pltpu.PrefetchScalarGridSpec(
            num_scalar_prefetch=1,
            grid=(steps,),
            in_specs=[pl.BlockSpec(memory_space=pltpu.SMEM), own, here, here, here, one, here],
            out_specs=here,
        ),
        out_shape=jax.ShapeDtypeStruct((rows, width), f32),
        compiler_params=pltpu.CompilerParams(vmem_limit_bytes=48 * MIB),
        cost_estimate=COST,
        name="input_back",
    )(index, factor[None], terms, *came, tokens, gain[None], d_middle)


def present_kernel(qkv_ref, up_ref, down_ref, qkv_out, up_out, down_out):
    cols = qkv_out.shape[2]
    for j in range(3):
        qkv_out[j] = qkv_ref[:, j * cols : (j + 1) * cols].astype(f32)
    up_out[...] = up_ref[...].astype(f32)
    down_out[...] = down_ref[...].astype(f32).T


def present(qkv, up, down):
    rows, cols = up.shape
    head_cols = qkv.shape[1] // 3
    step = min(rows, 128)
    row = lambda size: pl.BlockSpec((step, size), lambda i: (i, 0))
    return pl.pallas_call(
        present_kernel,
        grid=(rows // step,),
        in_specs=[row(3 * head_cols), row(cols), row(cols)],
        out_specs=[
            pl.BlockSpec((3, step, head_cols), lambda i: (0, i, 0)),
            row(cols),
            pl.BlockSpec((cols, step), lambda i: (0, i)),
        ],
        out_shape=[
            jax.ShapeDtypeStruct((3, rows, head_cols), f32),
            jax.ShapeDtypeStruct((rows, cols), f32),
            jax.ShapeDtypeStruct((cols, rows), f32),
        ],
        compiler_params=pltpu.CompilerParams(vmem_limit_bytes=48 * MIB),
        cost_estimate=COST,
        name="present",
    )(qkv, up, down)


def blank_kernel(out_ref):
    pass


def blank(shape):
    return pl.pallas_call(
        blank_kernel,
        out_specs=pl.BlockSpec(memory_space=pl.ANY),
        out_shape=jax.ShapeDtypeStruct(shape, bf16),
        name="blank",
    )()


def sums_kernel(term_ref, token_ref, out_ref):
    @pl.when(pl.program_id(0) == 0)
    def _():
        out_ref[...] = jnp.zeros_like(out_ref)

    term = term_ref[...].astype(f32)
    scaled = norm_parts(token_ref[...].astype(f32))[0]
    out_ref[0:1, :] += jnp.sum(term * scaled, axis=0, keepdims=True)
    out_ref[1:2, :] += jnp.sum(term, axis=0, keepdims=True)


def gain_sums(terms, tokens_all):
    rows, width = terms.shape
    block = pl.BlockSpec((128, width), lambda i: (i, 0))
    return pl.pallas_call(
        sums_kernel,
        grid=(rows // 128,),
        in_specs=[block, block],
        out_specs=pl.BlockSpec((2, width), lambda i: (0, 0)),
        out_shape=jax.ShapeDtypeStruct((2, width), f32),
        compiler_params=pltpu.CompilerParams(vmem_limit_bytes=12 * MIB),
        cost_estimate=COST,
        name="gain_sums",
    )(terms, tokens_all)


class Phases:
    def __init__(self):
        self.marks, self.kept, self.sends = (), [], []

    def __call__(self, *values):
        gate = (*self.marks, *self.sends)
        if gate:
            values = lax.optimization_barrier((*values, *gate))[: len(values)]
        return values if len(values) > 1 else values[0]

    def early(self, *values):
        if self.marks:
            values = lax.optimization_barrier((*values, *self.marks))[: len(values)]
        return values if len(values) > 1 else values[0]

    def send(self, *values):
        self.sends += values

    def keep(self, *values):
        self.kept += values
        return values if len(values) > 1 else values[0]

    def turn(self):
        self.marks, self.kept, self.sends = tuple(self.kept), [], []


class Line:
    def __init__(self, name, size):
        self.name, self.n = name, size
        self.me = lax.axis_index(name)
        self.low = self.me < size // 2

    def slot(self, k):
        n = self.n
        return jnp.where(self.low, (self.me + k) % n, (self.me + n - k) % n)

    def shuffle(self, phase, array):
        n = self.n
        cols = array.shape[1] // n
        out = []
        for shift in range(n):
            target = (self.me + shift) % n
            block = lax.dynamic_slice_in_dim(phase.early(array), target * cols, cols, axis=1)
            if shift:
                phase.send(block)
                block = lax.ppermute(block, self.name, [(j, (j + shift) % n) for j in range(n)])
            out.append(phase.keep(block))
        return out

    def shuffle_rows(self, phase, array, rows):
        n = self.n
        out = []
        for shift in range(1, n):
            target = (self.me + shift) % n
            block = lax.dynamic_slice_in_dim(phase.early(array), target * rows, rows, axis=0)
            phase.send(block)
            out.append(lax.ppermute(block, self.name, [(j, (j + shift) % n) for j in range(n)]))
        return out

    def stack(self, blocks):
        n = self.n
        rows, cols = blocks[0].shape
        out = blank((n * rows, cols))
        for shift, block in enumerate(blocks):
            source = (self.me + n - shift) % n
            out = lax.dynamic_update_slice_in_dim(out, block, source * rows, axis=0)
        return out


class Gather:
    def __init__(self, line, block):
        self.line, self.left, self.right, self.slots = line, [block], [block], {0: block}

    def step(self, phase):
        line, n, k = self.line, self.line.n, len(self.left)
        left, right = phase.early(self.left[-1], self.right[-1])
        phase.send(left, right)
        self.left.append(lax.ppermute(left, line.name, [(j, j + 1) for j in range(k - 1, n - 1)]))
        self.right.append(lax.ppermute(right, line.name, [(j, j - 1) for j in range(1, n - k + 1)]))
        phase.keep(self.left[k], self.right[k])

    def slot(self, phase, k):
        if k not in self.slots:
            line, n = self.line, self.line.n
            if 2 * k < n:
                left, right = phase(self.left[k], self.right[k])
                value = jnp.where(line.low, right, left)
            else:
                left, right, left_far, right_far = phase(
                    self.left[n - k], self.right[n - k], self.left[k], self.right[k]
                )
                low_side = jnp.where(line.me + k < n, right_far, left)
                high_side = jnp.where(line.me >= k, left_far, right)
                value = jnp.where(line.low, low_side, high_side)
            self.slots[k] = value
        return self.slots[k]


class Reduce:
    def __init__(self, line, rows):
        self.line, self.rows, self.k, self.came, self.terms = line, rows, 1, (), None

    def step(self, phase):
        line, n, k = self.line, self.line.n, self.k
        blocks = [jnp.clip(line.me + n - k, 0, n - 1), jnp.clip(line.me - n + k, 0, n - 1)]
        self.terms = phase.early(self.terms)
        sent = relay(self.terms, self.rows, jnp.stack(blocks).astype(jnp.int32), self.came)
        phase.send(*sent)
        self.came = (
            lax.ppermute(sent[0], line.name, [(j, j + 1) for j in range(k)]),
            lax.ppermute(sent[1], line.name, [(j, j - 1) for j in range(n - k, n)]),
        )
        phase.keep(*self.came)
        self.k += 1


def flip(value, name, size, bit):
    return lax.ppermute(value, name, [(j, j ^ bit) for j in range(size)])


def sum_over(value, name, size, bit=1):
    while bit < size:
        value = value + flip(value, name, size, bit)
        bit *= 2
    return value


class Spread:
    def __init__(self, name, size, moved, still, moved_left, factor):
        self.name, self.size, self.factor, self.moved_left = name, size, factor, moved_left
        self.moved, self.still = moved, still
        self.bits = [1 << b for b in range(1, size.bit_length() - 1)]
        self.orders = [self.bits, self.bits[::-1]]
        self.block_cols = moved.shape[1] // size

    def blocks(self, moved, wanted):
        cols, index = self.block_cols, lax.axis_index(self.name)
        return jnp.concatenate(
            [lax.dynamic_slice_in_dim(moved, (index ^ r) * cols, cols, axis=1) for r in wanted], axis=1
        )

    def product(self, moved, still):
        left, right = (moved, still) if self.moved_left else (still, moved)
        return self.factor * dot(left, right, 0, 0)

    def listed(self, order, fixed):
        out = [sum(bit for bit, on in fixed.items() if on)]
        for bit in order[::-1]:
            if bit not in fixed:
                out = [*out, *[r + bit for r in out]]
        return out

    def cut(self, array, low, high):
        return array[low:high] if self.moved_left else array[:, low:high]

    def start(self, phase):
        moved = phase(self.moved)
        self.sent = self.product(self.blocks(moved, self.listed(self.bits, {1: True})), self.still).astype(bf16)
        return self.sent

    def cross(self, phase):
        sent = phase.early(self.sent)
        phase.send(sent)
        self.brought = flip(sent, self.name, self.size, 1)
        return self.brought

    def second(self, phase):
        moved, brought = phase(self.moved, self.brought)
        cols, along = self.block_cols, 0 if self.moved_left else 1
        half = self.still.shape[1] // 2
        first_list = self.listed(self.bits, {1: True})
        self.sent, self.kept = [], []
        for which, order in enumerate(self.orders):
            still = self.still[:, which * half : (which + 1) * half]
            part = lax.slice_in_dim(brought, which * half, (which + 1) * half, axis=1 - along)
            for on in (True, False):
                wanted = self.listed(order, {1: False, order[0]: on})
                places = [first_list.index(r + 1) for r in wanted]
                added = jnp.concatenate(
                    [self.cut(part, p * cols, (p + 1) * cols) for p in places], axis=along
                )
                value = (self.product(self.blocks(moved, wanted), still) + added.astype(f32)).astype(bf16)
                (self.sent if on else self.kept).append(value)
        self.done, self.air, self.result = 0, False, None
        return (*self.sent, *self.kept)

    def fly(self, phase):
        sent = phase.early(*self.sent)
        phase.send(*sent)
        self.flying = tuple(
            flip(value, self.name, self.size, order[self.done]) for value, order in zip(sent, self.orders)
        )
        self.done, self.air = self.done + 1, True
        return self.flying

    def land(self, phase):
        along, self.air = 0 if self.moved_left else 1, False
        flying = phase(*self.flying)
        totals = [k.astype(f32) + f.astype(f32) for k, f in zip(self.kept, flying)]
        if self.done == len(self.bits):
            self.result = jnp.concatenate(totals, axis=1 - along)
            return (self.result,)
        size = totals[0].shape[along]
        self.sent = [self.cut(t, size // 2, size).astype(bf16) for t in totals]
        self.kept = [self.cut(t, 0, size // 2).astype(bf16) for t in totals]
        return (*self.sent, *self.kept)

    def finish(self, phase):
        while self.result is None:
            (self.land if self.air else self.fly)(phase)
        return self.result


def after(value, *earlier):
    return lax.optimization_barrier((value, *earlier))[0]


def make_body(n_dp, n_mp):
    def body(
        tokens, cotangent, segment, counts, ln_gain, ln_bias, w_qkv, b_qv, w_out, out_bias, w_up, b_up, w_down
    ):
        line, phase = Line("mp", n_mp), Phases()
        keep, turn = phase.keep, phase.turn
        gains, shifts, bias_pair = ln_gain.astype(f32), ln_bias.astype(f32), out_bias.astype(f32)
        share, width = tokens.shape
        head_cols = w_qkv.shape[2]
        heads = head_cols // HEAD
        group = segment.shape[0]
        seg_col, seg_row = segment[:, None], segment[None, :]
        me = line.me
        place = lambda whole, block, index: lax.dynamic_update_slice_in_dim(
            whole, block, index * share, axis=0
        )
        rows_of = lambda whole, index: lax.dynamic_slice_in_dim(whole, index * share, share, axis=0)
        total = lambda value: jnp.sum(value.astype(f32), axis=0)
        slots, last = range(1, n_mp), n_mp - 1

        flat_qkv = jnp.concatenate([w_qkv[:, j] for j in range(3)], axis=1)
        bias_rows = (
            jnp.stack([b_qv[0], jnp.zeros_like(b_qv[0]), b_qv[1]]).astype(f32).reshape(3 * head_cols)
        )
        state = [blank((group, width)), blank((group, width)), blank((group, 3 * head_cols))]

        def project(k):
            block = phase(gather.slot(phase, k))
            normed = (norm_parts(block.astype(f32))[0] * gains[0] + shifts[0]).astype(bf16)
            proj = (dot(normed, flat_qkv) + bias_rows).astype(bf16)
            for j, value in enumerate((block, normed, proj)):
                state[j] = keep(place(state[j], value, line.slot(k)))

        slice_rows = w_out.shape[0] // n_dp
        w_slice = lax.dynamic_slice_in_dim(
            w_out, lax.axis_index("dp") * slice_rows, slice_rows, axis=0
        )

        gather = Gather(line, tokens)
        for k in slots:
            gather.step(phase)
            if k == 2:
                w_slices = lax.all_gather(phase(w_slice), "mp", axis=0)
            project(k - 1)
            turn()
        cot_gather = Gather(line, cotangent)
        cot_gather.step(phase)
        w_out_all = lax.all_gather(phase(w_slices), "dp", axis=1).reshape(n_mp * w_out.shape[0], width)
        project(last)
        tokens_all, normed1_all, projected = state
        attn = keep(attend(projected, seg_col, seg_row, heads))
        turn()

        set_heads = lambda whole, block, index: lax.dynamic_update_slice_in_dim(
            whole, block, index * head_cols, axis=1
        )
        w_rows = lambda k: lax.dynamic_slice_in_dim(w_out_all, line.slot(k) * head_cols, head_cols, axis=0)
        half = line.low.astype(jnp.int32)
        attn_all = blank((group, n_mp * head_cols))
        cot_all = place(blank((group, width)), phase(cotangent), me)

        def place_near():
            nonlocal cot_all
            for j in range(1, n_mp // 2):
                for came, index in ((cot_gather.left[j], me - j), (cot_gather.right[j], me + j)):
                    here = (index >= 0) & (index < n_mp) & ((index < n_mp // 2) == line.low)
                    came = phase(came)
                    cot_all = place(cot_all, jnp.where(here, came, cotangent), jnp.where(here, index, me))
            cot_all = keep(phase(cot_all))

        attn_gather = Gather(line, attn)
        for k in slots:
            attn_gather.step(phase)
            attn_all = keep(set_heads(attn_all, phase(attn_gather.slot(phase, k - 1)), line.slot(k - 1)))
            if k == 1:
                middle_sum = keep(tokens_all.astype(f32) + bias_pair[0] + dot(phase(attn), w_out))
                count_here = phase(counts.astype(f32))
                factor = keep((count_here / sum_over(count_here, "dp", n_dp))[0])
            if k == 2 and n_mp == 4:
                place_near()
                near_rows = lax.dynamic_slice_in_dim(cot_all, (1 - half) * (group // 2), group // 2, axis=0)
                near_active = keep(dot(near_rows, w_down, 1, 1))
            if k == last:
                for j in range(1, last):
                    middle_sum = keep(middle_sum + dot(phase(attn_gather.slot(phase, j)), w_rows(j)))
            turn()
        reduce_down, reduce2, reduce1 = (Reduce(line, share) for _ in range(3))
        for k in slots[1:]:
            cot_gather.step(phase)
            if k == 2:
                heads_last = attn_gather.slot(phase, last)
                middle_all, normed2_all = mix(
                    middle_sum, heads_last, w_out_all, line.slot(last), gains[1], shifts[1]
                )
                hidden, active = keep(*feed_up(normed2_all, w_up, b_up.astype(f32)))
                keep(middle_all, normed2_all)
            if k == 3:
                attn_all = keep(set_heads(attn_all, phase(heads_last), line.slot(last)))
                reduce_down.terms = keep(dot(phase(active), w_down).astype(bf16))
            if k == max(3, n_mp // 2):
                if n_mp == 4:
                    cot_all = keep(place(cot_all, cot_gather.slot(phase, 2), line.slot(2)))
                    d_hidden_all = keep(slope_back(phase(near_active), hidden, 1 - half))
                else:
                    place_near()
                    d_hidden_all = keep(hidden_back(cot_all, hidden, w_down, 1 - half))
            turn()

        scatter = lambda full: lax.psum_scatter(phase(full), "dp", scatter_dimension=0, tiled=True)

        reduce_down.step(phase)
        if n_mp == 4:
            edge = (me == 0) | (me == last)
            came = [phase(side[1], side[3]) for side in (cot_gather.left, cot_gather.right)]
            block = jnp.where(line.low, jnp.where(edge, came[1][1], came[1][0]), jnp.where(edge, came[0][1], came[0][0]))
            cot_all = place(cot_all, block, jnp.where(edge, line.slot(3), line.slot(1)))
        else:
            for k in slots:
                cot_all = place(cot_all, cot_gather.slot(phase, k), line.slot(k))
        d_hidden_all = keep(hidden_back(cot_all, hidden, w_down, half, d_hidden_all))
        reduce2.terms = keep(dot(d_hidden_all, w_up, 1, 1).astype(bf16))
        turn()
        for k in slots:
            reduce2.step(phase)
            if k == 1:
                up_full = keep(weight_grads(factor, phase(normed2_all), d_hidden_all))
            if k == 2:
                grad_up = scatter(up_full)
                down_full = keep(weight_grads(factor, phase(cot_all), active))
            if k == 3:
                grad_down = scatter(down_full)
                split_sums = keep(factor * total(phase(d_hidden_all)))
            turn()
        own = me[None].astype(jnp.int32)
        reduce_down.step(phase)
        d_middle, d_branch, own_sums = keep(
            *middle_back(own, phase(reduce2.terms), reduce2.came, middle_all, gains[1], cotangent)
        )
        d_attn_own = keep(dot(d_branch, w_out_all, 1, 1).astype(bf16))
        spread_out = Spread("dp", n_dp, after(d_branch, d_attn_own), rows_of(attn_all, me), False, factor)
        keep(spread_out.start(phase))
        turn()
        d_attn_blocks = line.shuffle(phase, d_attn_own)
        spread_out.cross(phase)
        keep(*spread_out.second(phase))
        keep(grad_up)
        turn()
        reduce_down.step(phase)
        d_attn = line.stack(phase(*d_attn_blocks))
        grad_proj = keep(attend_back(projected, d_attn, seg_col, seg_row, heads))
        reduce1.terms = keep(half_product(grad_proj, flat_qkv, half))
        turn()
        for k in slots:
            reduce1.step(phase)
            if k == 1:
                keep(*spread_out.fly(phase))
                reduce1.terms = keep(half_product(phase(grad_proj), flat_qkv, 1 - half, reduce1.terms))
                gain1 = gain_sums(reduce1.terms, tokens_all)
                full_sums = factor * jnp.concatenate([gain1, own_sums], axis=0).reshape(-1)
                full_sums = keep(full_sums + keep(flip(full_sums, "mp", n_mp, 1)))
                qkv_full = keep(weight_grads(factor, after(normed1_all, gain1), grad_proj))
                keep(grad_down)
            if k == 2:
                grad_qkv = scatter(qkv_full)
                keep(*spread_out.land(phase))
                heads_sum = [total(phase(grad_proj)[:, :head_cols]), total(grad_proj[:, 2 * head_cols :])]
                split_sums = keep(jnp.concatenate([*[factor * s for s in heads_sum], split_sums]))
            if k == 3:
                keep(*spread_out.fly(phase))
                for _ in slots[3:]:
                    reduce_down.step(phase)
                down_sum = sum(
                    value.astype(f32)
                    for value in (rows_of(phase(reduce_down.terms), me), *reduce_down.came)
                )
                layer_out = keep((rows_of(middle_all, me) + down_sum + bias_pair[1]).astype(bf16))
                full_sums = keep(sum_over(phase(full_sums), "mp", n_mp, 2))
                grad_up, grad_down = keep(phase(grad_up).astype(f32), phase(grad_down).astype(f32).T)
            turn()
        out_rows = spread_out.finish(phase)
        out_blocks = line.shuffle_rows(phase, out_rows.astype(bf16), head_cols)
        grad_input = input_back(
            own, factor, phase(reduce1.terms), reduce1.came, tokens, gains[0], d_middle
        )
        grad_qkv = phase(grad_qkv).astype(f32)
        grad_qkv = jnp.stack([grad_qkv[:, j * head_cols : (j + 1) * head_cols] for j in range(3)])
        sums = after(jnp.concatenate([full_sums, split_sums]), grad_input).reshape(1, 8, -1)
        sums = lax.all_gather(sums, "dp", axis=0, tiled=True)
        sums, grad_qkv, *out_blocks = lax.optimization_barrier((sums, grad_qkv, *out_blocks))
        grad_out = lax.dynamic_slice_in_dim(out_rows, me * head_cols, head_cols, axis=0)
        for block in out_blocks:
            grad_out = grad_out + block.astype(f32)
        sums = jnp.sum(sums, axis=0).reshape(-1)
        full_sums = sums[: 6 * width].reshape(6, width)
        split_sums = sums[6 * width :]
        return (
            layer_out,
            grad_input,
            jnp.stack([full_sums[0], full_sums[2]]),
            jnp.stack([full_sums[1], full_sums[3]]),
            grad_qkv.transpose(1, 0, 2),
            split_sums[: 2 * head_cols].reshape(2, head_cols),
            grad_out,
            full_sums[4:],
            grad_up,
            split_sums[2 * head_cols :],
            grad_down,
        )

    return body


def solution(mesh):
    split = P(("dp", "mp"), None)
    return jax.shard_map(
        make_body(mesh.shape["dp"], mesh.shape["mp"]),
        mesh=mesh,
        in_specs=(
            split, split, P("dp"), P("dp"), P(), P(), P(None, None, "mp"), P(None, "mp"), P("mp", None), P(),
            P(None, "mp"), P("mp"), P("mp", None),
        ),
        out_specs=(
            split, split, P(), P(), P("dp", None, "mp"), P(None, "mp"), P("mp", "dp"), P(), P("dp", "mp"), P("mp"),
            P("mp", "dp"),
        ),
        check_vma=False,
    )
```
